512 devices in a mesh: leaf: 64 (over y, x, core), sep: 8 (over z).
Axes of the slice: x: 4, y: 8, z: 8, core: 2. Of those that a mesh axis runs over, the one named last changes fastest.
Arguments:
- rhs_root: float32 [16, 4096], P(None, ('leaf', 'sep')), may hold values from -6 to 6
- rhs_level1: float32 [16, 4096], P(None, ('leaf', 'sep')), may hold values from -6 to 6
- rhs_level2: float32 [16, 8192], P(None, ('leaf', 'sep')), may hold values from -6 to 6
- rhs_level3: float32 [16, 8192], P(None, ('leaf', 'sep')), may hold values from -6 to 6
- inv_root: float32 [4096, 4096], P(('leaf', 'sep')), may hold values from -1 to 2, as said below
- inv_level1: float32 [4096, 2048], P(('leaf', 'sep')), may hold values from -1 to 2, as said below
- inv_level2: float32 [8192, 2048], P(('leaf', 'sep')), may hold values from -1 to 2, as said below
- inv_level3: float32 [8192, 1024], P(('leaf', 'sep')), may hold values from -1 to 2, as said below
- cross_level1: float32 [4096, 4096], P(('leaf', 'sep')), may hold values from -0.046875 to 0.046875
- cross_level2: float32 [8192, 6144], P(('leaf', 'sep')), may hold values from -0.046875 to 0.046875
- cross_level3: float32 [8192, 8192], P(('leaf', 'sep')), may hold values from -0.0625 to 0.0625
- subtree_values: float32 [16, 16384], P(None, ('leaf', 'sep')), may hold values from -6 to 6
- coupling: float32 [16384, 2048], P(('leaf', 'sep')), may hold values from -0.1875 to 0.1875
- coupled_rows: int32 [16, 2048], replicated, may hold values from 0 to 9215, as said below
Outputs:
- x_root: float32 [16, 4096], P(None, ('leaf', 'sep'))
- x_level1: float32 [16, 4096], P(None, ('leaf', 'sep'))
- x_level2: float32 [16, 8192], P(None, ('leaf', 'sep'))
- x_level3: float32 [16, 8192], P(None, ('leaf', 'sep'))
- subtree_rhs: float32 [16, 16384], P(None, ('leaf', 'sep'))
The draws below stay inside these ranges and needn't reach their ends.
Inputs may be any that keep to these rules, and one draw needn't show every extreme that they name: `coupled_rows`: each row holds 2048 distinct indices into its subtree's path rows in increasing order; the first is 0 and the last 9215. `inv_root`: lower triangular inside each separator's block of rows, with a positive diagonal. `inv_level1`: lower triangular inside each separator's block of rows, with a positive diagonal. `inv_level2`: lower triangular inside each separator's block of rows, with a positive diagonal. `inv_level3`: lower triangular inside each separator's block of rows, with a positive diagonal.
All inputs are finite; a program needn't handle non-finite values.
Results may differ from the reference program's by a relative error of at most 0.00016.
Values sent between devices are 32-bit elements; how exact they have to be, the bound alone decides.
No kernel may reach another device: no remote copies, remote signals or barrier semaphores. Data moves between devices by JAX's collectives and lax.ppermute only.
A program may use at most 128 MiB of HBM per device.

```python
import math
import jax
import jax.numpy as jnp
from jax import lax

ROOT_ROWS = 4096
LEVEL1_ROWS = 2048
LEVEL2_ROWS = 2048
LEVEL3_ROWS = 1024
SUBTREE_COLS = 1024
COUPLED = 2048
SUBTREES = 16
SAMPLES = 16
PATH_ROWS = 9216


def lower_inverse(key, blocks, block_rows, lowest, highest):
    total = blocks * block_rows
    key_noise = jax.random.fold_in(key, 0)
    key_diag = jax.random.fold_in(key, 2)
    noise = jax.random.normal(key_noise, (total, block_rows), jnp.float32)
    diagonal = jax.random.uniform(key_diag, (total, 1), jnp.float32, lowest, highest)
    row_inside = (jnp.arange(total, dtype=jnp.int32) % block_rows)[:, None]
    column = jnp.arange(block_rows, dtype=jnp.int32)[None, :]
    lower = jnp.where(column < row_inside, noise * (1.5 / math.sqrt(block_rows)), 0.0)
    return lower + jnp.where(column == row_inside, diagonal, 0.0)


def draw_inv_root(key, part):
    key = jax.random.fold_in(key, 11)
    return lower_inverse(key, 1, ROOT_ROWS, 0.6, 1.4)


def draw_inv_level1(key, part):
    key = jax.random.fold_in(key, 12)
    return lower_inverse(key, 2, LEVEL1_ROWS, 0.6, 1.4)


def draw_inv_level2(key, part):
    key = jax.random.fold_in(key, 13)
    return lower_inverse(key, 4, LEVEL2_ROWS, 0.6, 1.4)


def draw_inv_level3(key, part):
    key = jax.random.fold_in(key, 14)
    return lower_inverse(key, 8, LEVEL3_ROWS, 0.6, 1.4)


def draw_coupled_rows(key, part):
    key = jax.random.fold_in(key, 21)
    subkeys = jax.random.split(key, SUBTREES)

    def one_subtree(subkey):
        middle_rows = jax.random.permutation(subkey, PATH_ROWS - 2)[:COUPLED - 2].astype(jnp.int32) + 1
        chosen = jnp.concatenate([jnp.zeros((1,), jnp.int32), middle_rows, jnp.full((1,), PATH_ROWS - 1, jnp.int32)])
        return jnp.sort(chosen)
    return jax.vmap(one_subtree)(subkeys)


def block_scale(key, dims, pieces, smallest, high):
    def one(position, blocks):
        heights = jax.random.uniform(jax.random.fold_in(jax.random.fold_in(key, 6), position), (blocks,), jnp.float32, smallest / len(pieces), high / len(pieces))
        return jnp.repeat(jnp.exp(heights), dims[position] // blocks).reshape((-1,) + (1,) * (len(dims) - position - 1))

    factor_of = one(*pieces[0])
    for cut in pieces[1:]:
        factor_of = factor_of * one(*cut)
    return factor_of


def gaussian(key, dims, scale, reach, cuts=(), kind=jnp.bfloat16):
    level = block_scale(key, dims, cuts, -0.22, 0.18) if cuts else 1.0
    entries = jax.random.normal(key, dims, jnp.float32) * scale * level
    return jnp.minimum(jnp.maximum(entries, -reach), reach).astype(kind)


def setup_inputs(seed: int = 0) -> dict:
    arg_keys = jax.random.split(jax.random.key(seed), 15)
    return {
        "rhs_root": gaussian(arg_keys[0], (SAMPLES, ROOT_ROWS), 1.0, 6.0, ((1, 512),), jnp.float32),
        "rhs_level1": gaussian(arg_keys[1], (SAMPLES, 2 * LEVEL1_ROWS), 1.0, 6.0, ((1, 512),), jnp.float32),
        "rhs_level2": gaussian(arg_keys[2], (SAMPLES, 4 * LEVEL2_ROWS), 1.0, 6.0, ((1, 512),), jnp.float32),
        "rhs_level3": gaussian(arg_keys[3], (SAMPLES, 8 * LEVEL3_ROWS), 1.0, 6.0, ((1, 512),), jnp.float32),
        "inv_root": draw_inv_root(jax.random.fold_in(arg_keys[14], 71), 0),
        "inv_level1": draw_inv_level1(jax.random.fold_in(arg_keys[14], 71), 0),
        "inv_level2": draw_inv_level2(jax.random.fold_in(arg_keys[14], 71), 0),
        "inv_level3": draw_inv_level3(jax.random.fold_in(arg_keys[14], 71), 0),
        "cross_level1": gaussian(arg_keys[8], (2 * LEVEL1_ROWS, ROOT_ROWS), (8 * LEVEL1_ROWS) ** -0.5, 0.046875, ((0, 512),), jnp.float32),
        "cross_level2": gaussian(arg_keys[9], (4 * LEVEL2_ROWS, ROOT_ROWS + LEVEL1_ROWS), (8 * LEVEL2_ROWS) ** -0.5, 0.046875, ((0, 512),), jnp.float32),
        "cross_level3": gaussian(arg_keys[10], (8 * LEVEL3_ROWS, ROOT_ROWS + LEVEL1_ROWS + LEVEL2_ROWS), (8 * LEVEL3_ROWS) ** -0.5, 0.0625, ((0, 512),), jnp.float32),
        "subtree_values": gaussian(arg_keys[11], (SAMPLES, SUBTREES * SUBTREE_COLS), 1.0, 6.0, ((1, 512),), jnp.float32),
        "coupling": gaussian(arg_keys[12], (SUBTREES * SUBTREE_COLS, COUPLED), SUBTREE_COLS ** -0.5, 0.1875, ((0, 512),), jnp.float32),
        "coupled_rows": draw_coupled_rows(jax.random.fold_in(arg_keys[14], 71), 0),
    }


precise = lax.Precision.HIGHEST


def level_widths():
    return [ROOT_ROWS, LEVEL1_ROWS, LEVEL2_ROWS, LEVEL3_ROWS]


def global_rows(coupled_rows):
    widths = level_widths()
    starts = [0, widths[0], widths[0] + widths[1], widths[0] + widths[1] + widths[2]]
    level_starts = [0, widths[0], widths[0] + 2 * widths[1], widths[0] + 2 * widths[1] + 4 * widths[2]]
    tree_depth = SUBTREES.bit_length() - 1
    subtree_ids = jnp.arange(SUBTREES, dtype=jnp.int32)[:, None]
    height = ((coupled_rows >= starts[1]).astype(jnp.int32) + (coupled_rows >= starts[2]).astype(jnp.int32)
              + (coupled_rows >= starts[3]).astype(jnp.int32))
    located = jnp.zeros_like(coupled_rows)
    for level_no in range(4):
        owner = subtree_ids // (2 ** (tree_depth - level_no))
        placed = level_starts[level_no] + owner * widths[level_no] + coupled_rows - starts[level_no]
        located = jnp.where(height == level_no, placed, located)
    return located.astype(jnp.int32), level_starts


def reference(rhs_root, rhs_level1, rhs_level2, rhs_level3, inv_root, inv_level1, inv_level2, inv_level3,
              cross_level1, cross_level2, cross_level3, subtree_values, coupling, coupled_rows):
    widths = level_widths()
    starts = [0, widths[0], widths[0] + widths[1], widths[0] + widths[1] + widths[2]]
    rhs_parts = [rhs_root, rhs_level1, rhs_level2, rhs_level3]
    inverses = [inv_root, inv_level1, inv_level2, inv_level3]
    crosses = [None, cross_level1, cross_level2, cross_level3]
    samples = SAMPLES
    values3 = subtree_values.reshape(samples, SUBTREES, SUBTREE_COLS)
    coupling3 = coupling.reshape(SUBTREES, SUBTREE_COLS, COUPLED)
    update = jnp.einsum("nlm,lmk->lnk", values3, coupling3, precision=precise)
    located, level_starts = global_rows(coupled_rows)
    total_rows = level_starts[3] + 8 * widths[3]
    flat = jnp.zeros((samples, total_rows), jnp.float32)
    flat = flat.at[:, located.reshape(-1)].add(jnp.transpose(update, (1, 0, 2)).reshape(samples, -1))
    pending = [flat[:, level_starts[h]:level_starts[h] + (2 ** h) * widths[h]] for h in range(4)]
    solved = [None, None, None, None]
    for height in (3, 2, 1, 0):
        blocks = 2 ** height
        block_width = widths[height]
        target = (rhs_parts[height] - pending[height]).reshape(samples, blocks, block_width)
        square = inverses[height].reshape(blocks, block_width, block_width)
        result = jnp.einsum("nis,irs->nir", target, square, precision=precise)
        solved[height] = result
        if height > 0:
            spread = jnp.einsum("nir,ira->nia", result, crosses[height].reshape(blocks, block_width, -1),
                                precision=precise)
            for upper_level in range(height):
                piece = spread[:, :, starts[upper_level]:starts[upper_level] + widths[upper_level]]
                piece = piece.reshape(samples, 2 ** upper_level, 2 ** (height - upper_level), widths[upper_level])
                pending[upper_level] = pending[upper_level] + jnp.sum(piece, axis=2).reshape(samples, -1)
    answers = []
    for height in range(4):
        blocks = 2 ** height
        block_width = widths[height]
        residual = solved[height]
        if height > 0:
            ancestors = jnp.concatenate(
                [jnp.repeat(answers[upper_level].reshape(samples, 2 ** upper_level, widths[upper_level]),
                            2 ** (height - upper_level), axis=1) for upper_level in range(height)], axis=2)
            residual = residual - jnp.einsum("nia,ira->nir", ancestors,
                                             crosses[height].reshape(blocks, block_width, -1), precision=precise)
        square = inverses[height].reshape(blocks, block_width, block_width)
        answer = jnp.einsum("nir,irs->nis", residual, square, precision=precise)
        answers.append(answer.reshape(samples, -1))
    known_flat = jnp.concatenate(answers, axis=1)
    selected = known_flat[:, located]
    handed = values3 - jnp.einsum("nlk,lmk->nlm", selected, coupling3, precision=precise)
    return (answers[0], answers[1], answers[2], answers[3], handed.reshape(samples, -1))
```

```python
import jax
import jax.numpy as jnp
from jax import lax
from jax.sharding import Mesh, PartitionSpec as P

ROOT_ROWS = 4096
LEVEL1_ROWS = 2048
LEVEL2_ROWS = 2048
LEVEL3_ROWS = 1024
WIDTHS = (ROOT_ROWS, LEVEL1_ROWS, LEVEL2_ROWS, LEVEL3_ROWS)
Y, X, C = 8, 4, 2
XC = X * C
PAIR = 2

precise = lax.Precision.HIGHEST


def group_size(axes):
    size = 1
    for name in axes:
        size *= lax.axis_size(name)
    return size


def exchange(operand, axes):
    shape = operand.shape
    count = shape[0]
    elements = operand.size // count
    rows = elements // 128 if elements % 128 == 0 else 1
    flat = operand.reshape(count * rows, elements // rows)
    return lax.all_to_all(flat, axes, 0, 0, tiled=True).reshape(shape)


def sum_to_all(partial, axes):
    copies = jnp.broadcast_to(partial[None], (group_size(axes),) + partial.shape)
    return jnp.sum(exchange(copies, axes), axis=0)


def matmul_rows(vector, matrix):
    return jnp.einsum("sk,rk->sr", vector, matrix, precision=precise, preferred_element_type=jnp.float32)


def matmul_columns(vector, matrix):
    return jnp.einsum("sr,rk->sk", vector, matrix, precision=precise, preferred_element_type=jnp.float32)


def body(
    rhs_root,
    rhs_level1,
    rhs_level2,
    rhs_level3,
    inv_root,
    inv_level1,
    inv_level2,
    inv_level3,
    cross_level1,
    cross_level2,
    cross_level3,
    subtree_values,
    coupling,
    coupled_rows,
):
    widths = WIDTHS
    starts = (0, widths[0], widths[0] + widths[1], widths[0] + widths[1] + widths[2])
    path_rows = starts[3] + widths[3]
    ancestors = starts[3]
    depth = lax.axis_size("z")
    y = (lax.axis_index("y2") * 2 + lax.axis_index("y1")) * 2 + lax.axis_index("y0")
    x = lax.axis_index("x")
    c = lax.axis_index("c")
    z = lax.axis_index("z")
    all_y = ("y2", "y1", "y0")

    pack3 = jnp.concatenate([inv_level3, cross_level3], axis=1)
    pack2 = jnp.concatenate([inv_level2, cross_level2], axis=1)
    pack1 = jnp.concatenate([inv_level1, cross_level1, inv_root], axis=1)
    all3 = lax.all_gather(pack3, ("x", "c"), axis=0, tiled=True)
    all2 = lax.all_gather(pack2, ("x", "c"), axis=0, tiled=True)
    all1 = lax.all_gather(pack1, ("x", "c"), axis=0, tiled=True)
    all_coupling = lax.all_gather(coupling, ("x", "c"), axis=0, tiled=True)
    inv3, cross3 = all3[:, : widths[3]], all3[:, widths[3] :]
    inv2, cross2 = all2[:, : widths[2]], all2[:, widths[2] :]
    inv1 = all1[:, : widths[1]]
    cross1 = all1[:, widths[1] : widths[1] + widths[0]]
    inv0 = all1[:, widths[1] + widths[0] :]

    rhs_parts = [rhs_root, rhs_level1, rhs_level2, rhs_level3]
    locals_ = [part.shape[1] for part in rhs_parts]
    small = jnp.concatenate(rhs_parts + [subtree_values], axis=1)
    both_small = lax.all_gather(small, "c", axis=0, tiled=False)
    both_small = both_small.reshape(C, X, C, PAIR, small.shape[1])
    both_small = lax.dynamic_index_in_dim(both_small, c, 2, keepdims=False).reshape(C, X * PAIR, small.shape[1])
    both_coupling = lax.all_gather(coupling, "c", axis=0, tiled=True)
    values = both_small[:, :, sum(locals_) :]
    values = jnp.transpose(values, (1, 0, 2)).reshape(X * PAIR, -1)
    subtree = y * 2 + x // 2
    indices = lax.dynamic_index_in_dim(coupled_rows, subtree, 0, keepdims=False)
    update = matmul_columns(values, both_coupling)
    pending = jnp.zeros((X * PAIR, path_rows), jnp.float32).at[:, indices].add(
        -update, unique_indices=True, indices_are_sorted=True
    )
    offset = 0
    for height in range(4):
        width = locals_[height]
        planes = Y // 2**height
        for other in range(C):
            place = ((y % planes) * XC + x * C + other) * depth + z
            column = starts[height] + place * width
            own = lax.dynamic_slice_in_dim(pending, column, width, 1)
            own = own + both_small[other, :, offset : offset + width]
            pending = lax.dynamic_update_slice_in_dim(pending, own, column, 1)
        offset += width

    block = ancestors // depth
    upper = pending[:, :ancestors].reshape(X, PAIR, depth, block)
    upper = jnp.transpose(upper, (0, 2, 1, 3)).reshape(X, depth, -1)
    lower = jnp.broadcast_to(
        pending[:, ancestors:].reshape(X, 1, PAIR * widths[3]), (X, depth, PAIR * widths[3])
    )
    send = jnp.concatenate([lower, upper], axis=2).reshape(X * depth, -1)
    received = jnp.sum(exchange(send, ("x", "z")), axis=0)
    target3 = received[: PAIR * widths[3]].reshape(PAIR, widths[3])
    upper = received[PAIR * widths[3] :].reshape(PAIR, block)

    solved3 = matmul_rows(target3, inv3)
    rest = -matmul_columns(solved3, cross3)
    own = lax.dynamic_slice_in_dim(rest, z * block, block, 1) + upper
    rest = lax.dynamic_update_slice_in_dim(rest, own, z * block, 1)
    target2 = sum_to_all(rest[:, starts[2] : ancestors], ("y0", "z"))
    solved2 = matmul_rows(target2, inv2)
    rest = rest[:, : starts[2]] - matmul_columns(solved2, cross2)
    target1 = sum_to_all(rest[:, starts[1] :], ("y1", "y0", "z"))
    solved1 = matmul_rows(target1, inv1)
    rest = rest[:, : starts[1]] - matmul_columns(solved1, cross1)

    def sum_root(partial):
        block = widths[0] // depth
        cut = jnp.transpose(partial.reshape(PAIR, depth, block), (1, 0, 2))
        cut = jnp.broadcast_to(cut[None], (Y, depth, PAIR, block)).reshape(Y * depth, PAIR, block)
        mine = jnp.sum(exchange(cut, all_y + ("z",)), axis=0)
        whole = exchange(jnp.broadcast_to(mine[None], (depth, PAIR, block)), ("z",))
        return jnp.transpose(whole, (1, 0, 2)).reshape(PAIR, widths[0])

    target0 = sum_root(rest)
    solved0 = matmul_rows(target0, inv0)
    x0 = sum_root(matmul_columns(solved0, inv0))
    residual = solved1 - matmul_rows(x0, cross1)
    x1 = sum_to_all(matmul_columns(residual, inv1), ("y1", "y0", "z"))
    known = jnp.concatenate([x0, x1], axis=1)
    residual = solved2 - matmul_rows(known, cross2)
    x2 = sum_to_all(matmul_columns(residual, inv2), ("y0", "z"))
    known = jnp.concatenate([known, x2], axis=1)
    residual = solved3 - matmul_rows(known, cross3)
    x3 = sum_to_all(matmul_columns(residual, inv3), ("z",))
    known = jnp.concatenate([known, x3], axis=1)

    rows = coupling.shape[0]
    both_indices = lax.dynamic_slice_in_dim(coupled_rows, y * 2, 2, 0)
    halves = all_coupling.reshape(2, XC // 2 * rows, -1)
    handed = []
    for half in range(2):
        chosen = known[:, both_indices[half]]
        handed.append(matmul_rows(chosen, halves[half]).reshape(PAIR, XC // 2, rows))
    handed = jnp.concatenate(handed, axis=1)

    pieces = []
    for height, answer in enumerate((x0, x1, x2, x3)):
        planes = Y // 2**height
        cube = answer.reshape(PAIR, planes, XC, depth, locals_[height])
        cube = lax.dynamic_index_in_dim(cube, z, 3, keepdims=False)
        pieces.append(lax.dynamic_index_in_dim(cube, y % planes, 1, keepdims=False))
    pieces.append(handed)
    out = jnp.transpose(jnp.concatenate(pieces, axis=2), (1, 0, 2))
    out = exchange(out, ("x", "c")).reshape(XC * PAIR, -1)
    cuts = [0]
    for width in locals_:
        cuts.append(cuts[-1] + width)
    answers = [out[:, cuts[k] : cuts[k + 1]] for k in range(4)]
    return (answers[0], answers[1], answers[2], answers[3], subtree_values - out[:, cuts[4] :])


def solution(mesh):
    shape = (2, 2, 2, X, C, mesh.shape["sep"])
    fine = Mesh(mesh.devices.reshape(shape), ("y2", "y1", "y0", "x", "c", "z"))
    every = ("y2", "y1", "y0", "x", "c", "z")
    columns, rows = P(None, every), P(every, None)
    in_specs = (columns,) * 4 + (rows,) * 7 + (columns, rows, P())
    return jax.shard_map(body, mesh=fine, in_specs=in_specs, out_specs=(columns,) * 5, check_vma=False)
```

```python
import functools

import jax
import jax.numpy as jnp
from jax import lax
from jax.experimental import pallas as pl
from jax.experimental.pallas import tpu as pltpu
from jax.sharding import Mesh, PartitionSpec as P

ROOT_ROWS = 4096
LEVEL1_ROWS = 2048
LEVEL2_ROWS = 2048
LEVEL3_ROWS = 1024
WIDTHS = (ROOT_ROWS, LEVEL1_ROWS, LEVEL2_ROWS, LEVEL3_ROWS)
Y, X, C = 8, 4, 2
XC = X * C
PAIR = 2
LANES = 128
LIMIT = 48 * 2**20
ALL_Y = ("y2", "y1", "y0")
INTERPRET = False


def call(kernel, out_shape, **options):
    limit = options.pop("limit", LIMIT)
    return pl.pallas_call(
        kernel,
        out_shape=out_shape,
        compiler_params=pltpu.CompilerParams(vmem_limit_bytes=limit),
        interpret=INTERPRET,
        **options,
    )


def f32(*shape):
    return jax.ShapeDtypeStruct(shape, jnp.float32)


def exchange(operand, axes):
    flat = operand.reshape(-1, LANES)
    return lax.all_to_all(flat, axes, 0, 0, tiled=True).reshape(operand.shape)


def split3(value):
    high = value.astype(jnp.bfloat16)
    rest = value - high.astype(jnp.float32)
    middle = rest.astype(jnp.bfloat16)
    low = (rest - middle.astype(jnp.float32)).astype(jnp.bfloat16)
    return high, middle, low


def one_hot(index_row, block):
    shape = (LANES, index_row.shape[1])
    rows = lax.broadcasted_iota(jnp.int32, shape, 0) + block * LANES
    return jnp.where(rows == index_row, 1.0, 0.0).astype(jnp.bfloat16)


NT = (((1,), (1,)), ((), ()))
NN = (((1,), (0,)), ((), ()))


def row_dot(matrix, column, vector, first, blocks):
    rows = matrix.shape[0]
    sums = [jnp.zeros((rows, LANES), jnp.float32) for _ in range(PAIR)]
    for block in range(blocks):
        tile = matrix[:, column + block * LANES : column + (block + 1) * LANES]
        for s in range(PAIR):
            at = (first + block) * PAIR + s
            sums[s] = sums[s] + tile * vector[at : at + 1, :]
    return [jnp.sum(value, axis=1, keepdims=True) for value in sums]


def column_dot(matrix, column, blocks, factors, total, fresh):
    rows = matrix.shape[0]
    wide = [jnp.broadcast_to(value, (rows, LANES)) for value in factors]
    for block in range(blocks):
        tile = matrix[:, column + block * LANES : column + (block + 1) * LANES]
        for s in range(PAIR):
            part = jnp.sum((tile * wide[s]).reshape(rows // 8, 8, LANES), axis=0)
            at = block * PAIR + s
            total[at] = jnp.where(fresh, part, total[at] + part)


def forward_kernel(steps, blocks, upper, skip_from, keep, copies, scalars, received, matrix, rest_in, solved, send, rest, vector, total):
    step = pl.program_id(0)

    @pl.when(step == 0)
    def _():
        vector[...] = jnp.sum(received[...], axis=0)

    values = row_dot(matrix, 0, vector, 0, blocks)
    rows = matrix.shape[0]
    for s in range(PAIR):
        solved[s] = jnp.broadcast_to(values[s], (rows, LANES))
    column_dot(matrix, blocks * LANES, upper, values, total, step == 0)

    @pl.when(step == steps - 1)
    def _():
        whole = -jnp.sum(total[...], axis=1)
        if skip_from:
            rest[...] = whole
            size = 2 * upper // skip_from
            at = pl.multiple_of(scalars[0] * size, 8)
            rest[pl.ds(at, size), :] = rest[pl.ds(at, size), :] + vector[2 * blocks :, :]
            whole = rest[...]
        else:
            whole = whole + rest_in[0 : 2 * upper, :]
            rest[...] = whole
        for copy in range(copies):
            send[copy] = whole[2 * keep :, :]


def forward(received, matrix, rest_in, scalars, blocks, keep, copies, first):
    rows, width = matrix.shape
    upper = width // LANES - blocks
    steps = 4
    chunk = rows // steps
    kernel = functools.partial(forward_kernel, steps, blocks, upper, first, keep, copies)
    whole = lambda array: pl.BlockSpec(array.shape, lambda i: (0,) * array.ndim)
    send_rows = 2 * (upper - keep)
    return call(
        kernel,
        (f32(PAIR, rows, LANES), f32(copies, send_rows, LANES), f32(2 * upper, LANES)),
        grid=(steps,),
        in_specs=[
            pl.BlockSpec(memory_space=pltpu.SMEM),
            whole(received),
            pl.BlockSpec((chunk, width), lambda i: (i, 0)),
            whole(rest_in),
        ],
        out_specs=(
            pl.BlockSpec((PAIR, chunk, LANES), lambda i: (0, i, 0)),
            pl.BlockSpec((copies, send_rows, LANES), lambda i: (0, 0, 0)),
            pl.BlockSpec((2 * upper, LANES), lambda i: (0, 0)),
        ),
        scratch_shapes=[pltpu.VMEM(received.shape[1:], jnp.float32), pltpu.VMEM((2 * upper, 8, LANES), jnp.float32)],
    )(scalars, received, matrix, rest_in)


def backward_kernel(steps, blocks, upper, known_blocks, copies, received, matrix, solved, *refs):
    known, (send, newest, total) = refs[: len(known_blocks)], refs[len(known_blocks) :]
    step = pl.program_id(0)

    @pl.when(step == 0)
    def _():
        newest[...] = jnp.sum(received[...], axis=0)

    values = [solved[s][:, 0:1] for s in range(PAIR)]
    column = blocks * LANES
    for ref, count in list(zip(known, known_blocks)) + [(newest, upper - sum(known_blocks))]:
        part = row_dot(matrix, column, ref, 0, count)
        values = [values[s] - part[s] for s in range(PAIR)]
        column += count * LANES
    column_dot(matrix, 0, blocks, values, total, step == 0)

    @pl.when(step == steps - 1)
    def _():
        whole = jnp.sum(total[...], axis=1)
        for copy in range(copies):
            send[copy] = whole


def backward(received, matrix, solved, known, blocks, copies):
    rows, width = matrix.shape
    upper = width // LANES - blocks
    steps = 4
    chunk = rows // steps
    counts = [array.shape[0] // PAIR for array in known]
    kernel = functools.partial(backward_kernel, steps, blocks, upper, counts, copies)
    whole = lambda array: pl.BlockSpec(array.shape, lambda i: (0,) * array.ndim)
    return call(
        kernel,
        (f32(copies, 2 * blocks, LANES), f32(*received.shape[1:])),
        grid=(steps,),
        in_specs=[
            whole(received),
            pl.BlockSpec((chunk, width), lambda i: (i, 0)),
            pl.BlockSpec((PAIR, chunk, LANES), lambda i: (0, i, 0)),
        ]
        + [whole(array) for array in known],
        out_specs=(
            pl.BlockSpec((copies, 2 * blocks, LANES), lambda i: (0, 0, 0)),
            pl.BlockSpec(received.shape[1:], lambda i: (0, 0)),
        ),
        scratch_shapes=[pltpu.VMEM((2 * blocks, 8, LANES), jnp.float32)],
    )(received, matrix, solved, *known)


def root_kernel(steps, blocks, copies, vector, matrix, send, total):
    step = pl.program_id(0)
    values = row_dot(matrix, 0, vector, 0, blocks)
    column_dot(matrix, 0, blocks, values, total, step == 0)

    @pl.when(step == steps - 1)
    def _():
        whole = jnp.sum(total[...], axis=1)
        for copy in range(copies):
            send[copy] = whole


def root(vector, matrix, copies):
    rows, width = matrix.shape
    blocks = width // LANES
    steps = 2
    chunk = rows // steps
    return call(
        functools.partial(root_kernel, steps, blocks, copies),
        f32(copies, 2 * blocks, LANES),
        grid=(steps,),
        in_specs=[pl.BlockSpec(vector.shape, lambda i: (0, 0)), pl.BlockSpec((chunk, width), lambda i: (i, 0))],
        out_specs=pl.BlockSpec((copies, 2 * blocks, LANES), lambda i: (0, 0, 0)),
        scratch_shapes=[pltpu.VMEM((2 * blocks, 8, LANES), jnp.float32)],
    )(vector, matrix)


def sum_kernel(copies, received, send):
    whole = jnp.sum(received[...], axis=0)
    for copy in range(copies):
        send[copy] = whole


def sum_and_copy(received, copies):
    return call(functools.partial(sum_kernel, copies), f32(copies, *received.shape[1:]))(received)


def first_kernel(columns, depth, scalars, small, coupling, index, send, terms, path):
    z, core, x = scalars[0], scalars[1], scalars[2]
    upper = sum(WIDTHS[:3]) // LANES
    count = upper + WIDTHS[3] // LANES
    rows = coupling.shape[1]
    half = pl.multiple_of(core * 8, 8)
    parts = [small[other, pl.ds(half, 8), :] for other in range(C)]
    update = None
    for other in range(C):
        product = lax.dot_general(
            parts[other][:, :rows], coupling[other], NN, precision=lax.Precision.HIGHEST, preferred_element_type=jnp.float32
        )
        update = product if update is None else update + product
    pieces = split3(update)
    terms[:, columns:] = jnp.zeros((32, terms.shape[1] - columns), jnp.bfloat16)
    terms[:, :columns] = jnp.concatenate([*pieces, jnp.zeros_like(pieces[0])], axis=0)

    def expand(block, carry):
        at = pl.multiple_of(scalars[8 + block] * LANES, LANES)
        selector = one_hot(index[0:1, pl.ds(at, 2 * LANES)], block)
        out = lax.dot_general(terms[:, pl.ds(at, 2 * LANES)], selector, NT, preferred_element_type=jnp.float32)
        path[block] = -(out[0:8] + out[8:16] + out[16:24])
        return carry

    lax.fori_loop(0, count, expand, 0, unroll=4)

    lane = lax.broadcasted_iota(jnp.int32, (8, LANES), 1)
    start = 0
    source = rows
    for height in range(4):
        width = 8 if height < 2 else 16
        for other in range(C):
            offset = z * width
            block = start
            if height < 3:
                block = block + scalars[3 + height] * (XC * depth * width // LANES)
            if width == 8:
                offset = offset + other * 64
                block = block + x
            else:
                block = block + x * 2 + other
            moved = pltpu.roll(parts[other], lax.rem(offset - source + LANES, LANES), 1)
            kept = jnp.where((lane >= offset) & (lane < offset + width), moved, 0.0)
            path[block] = path[block] + kept
        start += WIDTHS[height] // LANES
        source += width

    lower = WIDTHS[3] // LANES
    mine = upper // depth
    for block in range(upper):
        value = path[block]
        for dest in range(X):
            at = 2 * lower + 2 * (block % mine)
            send[dest * depth + block // mine, at : at + 2, :] = value[2 * dest : 2 * dest + 2, :]
    for dest in range(X):
        value = jnp.concatenate([path[upper + block][2 * dest : 2 * dest + 2, :] for block in range(lower)], axis=0)
        for other in range(depth):
            send[dest * depth + other, 0 : 2 * lower, :] = value


def first(small, coupling, index, scalars, depth):
    columns = coupling.shape[2]
    upper = sum(WIDTHS[:3]) // LANES
    lower = WIDTHS[3] // LANES
    vmem = pl.BlockSpec(memory_space=pltpu.VMEM)
    return call(
        functools.partial(first_kernel, columns, depth),
        f32(X * depth, 2 * (lower + upper // depth), LANES),
        in_specs=[pl.BlockSpec(memory_space=pltpu.SMEM), vmem, vmem, vmem],
        scratch_shapes=[
            pltpu.VMEM((32, columns + 2 * LANES), jnp.bfloat16),
            pltpu.VMEM((upper + lower, 8, LANES), jnp.float32),
        ],
    )(scalars, small, coupling, index)


def last_kernel(columns, counts, scalars, received, x0, x1, x2, coupling, index, send, x3, terms, chosen):
    x3[...] = jnp.sum(received[...], axis=0)
    blocks = sum(counts)
    at = 0
    for ref, count in zip((x0, x1, x2, x3), counts):
        pieces = split3(ref[...].reshape(count, PAIR, LANES))
        stacked = jnp.concatenate([*pieces, jnp.zeros_like(pieces[0])], axis=1)
        terms[at : at + count] = stacked.astype(jnp.float32)
        at += count
    chosen[...] = jnp.zeros_like(chosen)
    for half in range(2):

        def pick(block, carry):
            at = pl.multiple_of(scalars[8 + half * blocks + block] * LANES, LANES)
            selector = one_hot(index[half : half + 1, pl.ds(at, 2 * LANES)], block)
            out = lax.dot_general(
                terms[block].astype(jnp.bfloat16), selector, NN, preferred_element_type=jnp.float32
            )
            chosen[half, :, pl.ds(at, 2 * LANES)] = chosen[half, :, pl.ds(at, 2 * LANES)] + out
            return carry

        lax.fori_loop(0, blocks, pick, 0, unroll=4)
    rows = coupling.shape[0] // 2
    handed = []
    for half in range(2):
        value = chosen[half, 0:2, :columns] + chosen[half, 2:4, :columns] + chosen[half, 4:6, :columns]
        handed.append(
            lax.dot_general(
                value,
                coupling[half * rows : (half + 1) * rows, :],
                NT,
                precision=lax.Precision.HIGHEST,
                preferred_element_type=jnp.float32,
            )
        )
    send[...] = jnp.zeros_like(send)
    for dest in range(XC):
        core, x = dest // X, dest % X
        for level, ref in enumerate((x0, x1, x2, x3)):
            block = x if level < 2 else x * 2 + core
            if level < 3:
                block = block + scalars[level] * (counts[level] // (Y // 2**level))
            send[dest, 2 * level : 2 * level + 2, :] = ref[pl.ds(block * 2, 2), :]
        send[dest, 8:10, :] = handed[x // 2]


def last(received, known, coupling, index, scalars):
    columns = coupling.shape[1]
    counts = [width // LANES for width in WIDTHS]
    vmem = pl.BlockSpec(memory_space=pltpu.VMEM)
    return call(
        functools.partial(last_kernel, columns, counts),
        f32(XC, 16, LANES),
        in_specs=[pl.BlockSpec(memory_space=pltpu.SMEM)] + [vmem] * 6,
        scratch_shapes=[
            pltpu.VMEM(received.shape[1:], jnp.float32),
            pltpu.VMEM((sum(counts), 8, LANES), jnp.float32),
            pltpu.VMEM((2, 8, columns + 2 * LANES), jnp.float32),
        ],
    )(scalars, received, *known, coupling, index)


def finish_kernel(scalars, received, values, out0, out1, out2, out3, handed):
    z, core = scalars[0], scalars[1]
    offsets = (core * 64 + z * 8, core * 64 + z * 8, z * 16, z * 16, scalars[2] * values.shape[1])
    for level, ref in enumerate((out0, out1, out2, out3, handed)):
        value = jnp.concatenate([received[source, 2 * level : 2 * level + 2, :] for source in range(XC)], axis=0)
        moved = pltpu.roll(value, lax.rem(LANES - offsets[level], LANES), 1)[:, : ref.shape[1]]
        ref[...] = values[...] - moved if level == 4 else moved


def finish(received, values, scalars, widths):
    vmem = pl.BlockSpec(memory_space=pltpu.VMEM)
    shapes = tuple(f32(XC * PAIR, width) for width in widths) + (f32(*values.shape),)
    return call(
        finish_kernel, shapes, in_specs=[pl.BlockSpec(memory_space=pltpu.SMEM), vmem, vmem]
    )(scalars, received, values)


def body(
    rhs_root,
    rhs_level1,
    rhs_level2,
    rhs_level3,
    inv_root,
    inv_level1,
    inv_level2,
    inv_level3,
    cross_level1,
    cross_level2,
    cross_level3,
    subtree_values,
    coupling,
    coupled_rows,
):
    depth = lax.axis_size("z")
    y = (lax.axis_index("y2") * 2 + lax.axis_index("y1")) * 2 + lax.axis_index("y0")
    x, c, z = lax.axis_index("x"), lax.axis_index("c"), lax.axis_index("z")
    counts = [width // LANES for width in WIDTHS]
    blocks = sum(counts)

    def gathered(parts):
        whole = parts[0] if len(parts) == 1 else jnp.concatenate(parts, axis=1)
        return lax.all_gather(whole, ("x", "c"), axis=0, tiled=True)

    matrix3 = gathered([inv_level3, cross_level3])
    matrix2 = gathered([inv_level2, cross_level2])
    matrix1 = gathered([inv_level1, cross_level1])
    matrix0 = gathered([inv_root])
    all_coupling = gathered([coupling])

    rhs_parts = [rhs_root, rhs_level1, rhs_level2, rhs_level3]
    small = jnp.concatenate([subtree_values] + rhs_parts, axis=1)
    small = jnp.pad(small, ((0, 0), (0, LANES - small.shape[1])))
    both_small = lax.all_gather(small, "c", axis=0, tiled=False)
    both_coupling = lax.all_gather(coupling, "c", axis=0, tiled=False)

    both_indices = lax.dynamic_slice_in_dim(coupled_rows, y * 2, 2, 0)
    edges = jnp.arange(blocks, dtype=jnp.int32) * LANES
    windows = jnp.sum((both_indices[:, None, :] < edges[None, :, None]).astype(jnp.int32), axis=2) // LANES
    both_indices = jnp.pad(both_indices, ((0, 0), (0, 2 * LANES)), constant_values=-1)
    own_windows = lax.dynamic_index_in_dim(windows, x // 2, 0, keepdims=False)
    own_indices = lax.dynamic_slice_in_dim(both_indices, x // 2, 1, 0)

    def scalars(head, *tails):
        head = jnp.stack([jnp.asarray(value, jnp.int32) for value in head] + [jnp.int32(0)] * (8 - len(head)))
        return jnp.concatenate([head, *tails])

    places = scalars([z, c, x, y, y % 4, y % 2], own_windows)
    send = first(both_small, both_coupling, own_indices, places, depth)
    received = exchange(send, ("x", "z"))
    solved3, send, rest = forward(
        received, matrix3, jnp.zeros((8, LANES), jnp.float32), places, counts[3], counts[0] + counts[1], 2 * depth, depth
    )
    received = exchange(send, ("y0", "z"))
    solved2, send, rest = forward(received, matrix2, rest, places, counts[2], counts[0], 4 * depth, 0)
    received = exchange(send, ("y1", "y0", "z"))
    solved1, send, rest = forward(received, matrix1, rest, places, counts[1], 0, Y, 0)

    def sum_root(copies):
        received = exchange(copies.reshape(Y * depth, -1, LANES), ALL_Y + ("z",))
        return exchange(sum_and_copy(received, depth), ("z",))

    target = sum_root(send).reshape(-1, LANES)
    received = sum_root(root(target, matrix0, Y)).reshape(1, -1, LANES)
    send, x0 = backward(received, matrix1, solved1, [], counts[1], 4 * depth)
    received = exchange(send, ("y1", "y0", "z"))
    send, x1 = backward(received, matrix2, solved2, [x0], counts[2], 2 * depth)
    received = exchange(send, ("y0", "z"))
    send, x2 = backward(received, matrix3, solved3, [x0, x1], counts[3], depth)
    received = exchange(send, ("z",))
    heads = scalars([y, y % 4, y % 2], windows.reshape(-1))
    send = last(received, [x0, x1, x2], all_coupling, both_indices, heads)
    received = exchange(send, ("c", "x"))
    ends = scalars([z, c, (x % 2) * 2 + c])
    return finish(received, subtree_values, ends, [part.shape[1] for part in rhs_parts])


def solution(mesh):
    shape = (2, 2, 2, X, C, mesh.shape["sep"])
    fine = Mesh(mesh.devices.reshape(shape), ("y2", "y1", "y0", "x", "c", "z"))
    every = ("y2", "y1", "y0", "x", "c", "z")
    columns, rows = P(None, every), P(every, None)
    in_specs = (columns,) * 4 + (rows,) * 7 + (columns, rows, P())
    return jax.shard_map(body, mesh=fine, in_specs=in_specs, out_specs=(columns,) * 5, check_vma=False)
```

```python
import functools

import jax
import jax.numpy as jnp
from jax import lax
from jax.experimental import pallas as pl
from jax.experimental.pallas import tpu as pltpu
from jax.sharding import Mesh, PartitionSpec as P

ROOT_ROWS = 4096
LEVEL1_ROWS = 2048
LEVEL2_ROWS = 2048
LEVEL3_ROWS = 1024
WIDTHS = (ROOT_ROWS, LEVEL1_ROWS, LEVEL2_ROWS, LEVEL3_ROWS)
Y, X, C = 8, 4, 2
XC = X * C
PAIR = 2
LANES = 128
CHUNK = 32
HBM = pl.BlockSpec(memory_space=pltpu.HBM)
LIMIT = 16 * 2**20
WHOLE = 50 * 2**20
ALL_Y = ("y2", "y1", "y0")
INTERPRET = False
VMEM = pl.BlockSpec(memory_space=pltpu.VMEM)
SMEM = pl.BlockSpec(memory_space=pltpu.SMEM)


def call(kernel, out_shape, **options):
    limit = options.pop("limit", LIMIT)
    return pl.pallas_call(
        kernel,
        out_shape=out_shape,
        compiler_params=pltpu.CompilerParams(vmem_limit_bytes=limit),
        interpret=INTERPRET,
        **options,
    )


def cost(elements):
    return pl.CostEstimate(flops=8 * elements, bytes_accessed=4 * elements, transcendentals=0)


def f32(*shape):
    return jax.ShapeDtypeStruct(shape, jnp.float32)


def exchange(operand, axes):
    flat = operand.reshape(-1, LANES)
    return lax.all_to_all(flat, axes, 0, 0, tiled=True).reshape(operand.shape)


def split3(value):
    high = value.astype(jnp.bfloat16)
    rest = value - high.astype(jnp.float32)
    middle = rest.astype(jnp.bfloat16)
    low = (rest - middle.astype(jnp.float32)).astype(jnp.bfloat16)
    return high, middle, low


def one_hot(index_row, block):
    shape = (LANES, index_row.shape[1])
    rows = lax.broadcasted_iota(jnp.int32, shape, 0) + block * LANES
    return jnp.where(rows == index_row, 1.0, 0.0).astype(jnp.bfloat16)


NT = (((1,), (1,)), ((), ()))
NN = (((1,), (0,)), ((), ()))


def row_dot(matrix, rows, column, vector, first, blocks):
    sums = [jnp.zeros((CHUNK, LANES), jnp.float32) for _ in range(PAIR)]
    for block in range(blocks):
        tile = matrix[rows, column + block * LANES : column + (block + 1) * LANES]
        for s in range(PAIR):
            at = (first + block) * PAIR + s
            sums[s] = sums[s] + tile * vector[at : at + 1, :]
    return [jnp.sum(value, axis=1, keepdims=True) for value in sums]


def column_dot(matrix, rows, column, blocks, factors, total):
    wide = [jnp.broadcast_to(value, (CHUNK, LANES)) for value in factors]
    for block in range(blocks):
        tile = matrix[rows, column + block * LANES : column + (block + 1) * LANES]
        for s in range(PAIR):
            part = jnp.sum((tile * wide[s]).reshape(CHUNK // 8, 8, LANES), axis=0)
            at = block * PAIR + s
            total[at] = total[at] + part


def chunk_copies(matrices, buffer, ready):
    copies = []
    for number, matrix in enumerate(matrices):
        count = matrix.shape[0] // CHUNK
        for chunk in range(count):
            place = number * count + chunk
            columns = pl.ds(0, buffer.shape[1])
            source = matrix.at[pl.ds(chunk * CHUNK, CHUNK), columns]
            copies.append(pltpu.make_async_copy(source, buffer.at[pl.ds(place * CHUNK, CHUNK), columns], ready.at[place]))
    for copy in copies:
        copy.start()
    return copies


def each_chunk(copies, step):
    for place, copy in enumerate(copies):
        copy.wait()
        step(pl.ds(place * CHUNK, CHUNK))


def chunk_buffers(matrices, width):
    rows = 2 * matrices[0].shape[0]
    return [pltpu.VMEM((rows, width), jnp.float32), pltpu.SemaphoreType.DMA((rows // CHUNK,))]


def forward_kernel(blocks, upper, depth, keep, scalars, received, own, other, rest_in, solved, send, rest, vector, total, buffer, ready):
    copies = chunk_copies((own, other), buffer, ready)
    vector[...] = jnp.sum(received[...], axis=0)
    total[...] = jnp.zeros_like(total)

    def step(rows):
        values = row_dot(buffer, rows, 0, vector, 0, blocks)
        for s in range(PAIR):
            solved[s, rows, :] = jnp.broadcast_to(values[s], (CHUNK, LANES))
        column_dot(buffer, rows, blocks * LANES, upper, values, total)

    each_chunk(copies, step)
    whole = -jnp.sum(total[...], axis=1)
    if depth:
        rest[...] = whole
        size = 2 * upper // depth
        at = pl.multiple_of(scalars[0] * size, 8)
        rest[pl.ds(at, size), :] = rest[pl.ds(at, size), :] + vector[2 * blocks :, :]
        whole = rest[...]
    else:
        whole = whole + rest_in[0 : 2 * upper, :]
        rest[...] = whole
    for copy in range(send.shape[0]):
        send[copy] = whole[2 * keep :, :]


def forward(received, matrices, rest_in, scalars, blocks, upper, keep, copies, depth):
    rows = matrices[0].shape[0]
    width = upper * LANES + blocks * LANES
    return call(
        functools.partial(forward_kernel, blocks, upper, depth, keep),
        (f32(PAIR, 2 * rows, LANES), f32(copies, 2 * (upper - keep), LANES), f32(2 * upper, LANES)),
        in_specs=[SMEM, VMEM, HBM, HBM, VMEM],
        out_specs=(VMEM,) * 3,
        scratch_shapes=[pltpu.VMEM(received.shape[1:], jnp.float32), pltpu.VMEM((2 * upper, 8, LANES), jnp.float32)]
        + chunk_buffers(matrices, width),
        cost_estimate=cost(2 * rows * width),
        limit=WHOLE,
    )(scalars, received, *matrices, rest_in)


def backward_kernel(blocks, known_blocks, received, own, other, solved, *refs):
    known, (send, newest, total, buffer, ready) = refs[: len(known_blocks) - 1], refs[len(known_blocks) - 1 :]
    copies = chunk_copies((own, other), buffer, ready)
    newest[...] = jnp.sum(received[...], axis=0)
    total[...] = jnp.zeros_like(total)

    def step(rows):
        values = [solved[s, rows, 0:1] for s in range(PAIR)]
        column = blocks * LANES
        for ref, count in zip((*known, newest), known_blocks):
            part = row_dot(buffer, rows, column, ref, 0, count)
            values = [values[s] - part[s] for s in range(PAIR)]
            column += count * LANES
        column_dot(buffer, rows, 0, blocks, values, total)

    each_chunk(copies, step)
    whole = jnp.sum(total[...], axis=1)
    for copy in range(send.shape[0]):
        send[copy] = whole


def backward(received, matrices, solved, known, blocks, copies):
    rows = matrices[0].shape[0]
    counts = [array.shape[0] // PAIR for array in known] + [received.shape[1] // PAIR]
    width = (blocks + sum(counts)) * LANES
    return call(
        functools.partial(backward_kernel, blocks, counts),
        (f32(copies, 2 * blocks, LANES), f32(*received.shape[1:])),
        in_specs=[VMEM, HBM, HBM, VMEM] + [VMEM] * len(known),
        out_specs=(VMEM,) * 2,
        scratch_shapes=[pltpu.VMEM((2 * blocks, 8, LANES), jnp.float32)] + chunk_buffers(matrices, width),
        cost_estimate=cost(2 * rows * width),
        limit=WHOLE,
    )(received, *matrices, solved, *known)


def root_kernel(column, blocks, vector, own, other, send, total, buffer, ready):
    copies = chunk_copies((own.at[:, column:], other.at[:, column:]), buffer, ready)
    total[...] = jnp.zeros_like(total)

    def step(rows):
        values = row_dot(buffer, rows, 0, vector, 0, blocks)
        column_dot(buffer, rows, 0, blocks, values, total)

    each_chunk(copies, step)
    whole = jnp.sum(total[...], axis=1)
    for copy in range(send.shape[0]):
        send[copy] = whole


def root(vector, matrices, column, copies):
    rows = matrices[0].shape[0]
    blocks = vector.shape[0] // PAIR
    return call(
        functools.partial(root_kernel, column, blocks),
        f32(copies, 2 * blocks, LANES),
        in_specs=[VMEM, HBM, HBM],
        out_specs=VMEM,
        scratch_shapes=[pltpu.VMEM((2 * blocks, 8, LANES), jnp.float32)] + chunk_buffers(matrices, blocks * LANES),
        cost_estimate=cost(2 * rows * blocks * LANES),
        limit=WHOLE,
    )(vector, *matrices)


def sum_kernel(copies, received, send):
    whole = jnp.sum(received[...], axis=0)
    for copy in range(copies):
        send[copy] = whole


def sum_and_copy(received, copies):
    return call(functools.partial(sum_kernel, copies), f32(copies, *received.shape[1:]))(received)


def first_kernel(depth, scalars, small, coupling, index, send, terms, path):
    z, core, x = scalars[0], scalars[1], scalars[2]
    upper = sum(WIDTHS[:3]) // LANES
    count = upper + WIDTHS[3] // LANES
    rows, columns = coupling.shape[1:]
    half = pl.multiple_of(core * 8, 8)
    parts = [small[other, pl.ds(half, 8), :] for other in range(C)]
    update = None
    for other in range(C):
        product = lax.dot_general(
            parts[other][:, :rows], coupling[other], NN, precision=lax.Precision.HIGHEST, preferred_element_type=jnp.float32
        )
        update = product if update is None else update + product
    pieces = split3(update)
    terms[:, columns:] = jnp.zeros((32, terms.shape[1] - columns), jnp.bfloat16)
    terms[:, :columns] = jnp.concatenate([*pieces, jnp.zeros_like(pieces[0])], axis=0)

    def expand(block, carry):
        at = pl.multiple_of(scalars[8 + block] * LANES, LANES)
        selector = one_hot(index[0:1, pl.ds(at, 2 * LANES)], block)
        out = lax.dot_general(terms[:, pl.ds(at, 2 * LANES)], selector, NT, preferred_element_type=jnp.float32)
        path[block] = -(out[0:8] + out[8:16] + out[16:24])
        return carry

    lax.fori_loop(0, count, expand, 0, unroll=4)

    lane = lax.broadcasted_iota(jnp.int32, (8, LANES), 1)
    start = 0
    source = rows
    for height in range(4):
        width = 8 if height < 2 else 16
        for other in range(C):
            offset = z * width
            block = start
            if height < 3:
                block = block + scalars[3 + height] * (XC * depth * width // LANES)
            if width == 8:
                offset = offset + other * 64
                block = block + x
            else:
                block = block + x * 2 + other
            moved = pltpu.roll(parts[other], lax.rem(offset - source + LANES, LANES), 1)
            kept = jnp.where((lane >= offset) & (lane < offset + width), moved, 0.0)
            path[block] = path[block] + kept
        start += WIDTHS[height] // LANES
        source += width

    lower = WIDTHS[3] // LANES
    mine = upper // depth
    for block in range(upper):
        value = path[block]
        for dest in range(X):
            at = 2 * lower + 2 * (block % mine)
            send[dest * depth + block // mine, at : at + 2, :] = value[2 * dest : 2 * dest + 2, :]
    for dest in range(X):
        value = jnp.concatenate([path[upper + block][2 * dest : 2 * dest + 2, :] for block in range(lower)], axis=0)
        for other in range(depth):
            send[dest * depth + other, 0 : 2 * lower, :] = value


def first(small, coupling, index, scalars, depth):
    columns = coupling.shape[2]
    upper = sum(WIDTHS[:3]) // LANES
    lower = WIDTHS[3] // LANES
    return call(
        functools.partial(first_kernel, depth),
        f32(X * depth, 2 * (lower + upper // depth), LANES),
        in_specs=[SMEM, VMEM, VMEM, VMEM],
        scratch_shapes=[
            pltpu.VMEM((32, columns + 2 * LANES), jnp.bfloat16),
            pltpu.VMEM((upper + lower, 8, LANES), jnp.float32),
        ],
    )(scalars, small, coupling, index)


def pick(scalars, index, terms, first_block, blocks, chosen):
    total = sum(WIDTHS) // LANES

    def one(block, carry):
        for half in range(2):
            at = pl.multiple_of(scalars[8 + half * total + first_block + block] * LANES, LANES)
            selector = one_hot(index[half : half + 1, pl.ds(at, 2 * LANES)], first_block + block)
            out = lax.dot_general(
                terms[block].astype(jnp.bfloat16), selector, NN, preferred_element_type=jnp.float32
            )
            chosen[half, :, pl.ds(at, 2 * LANES)] = chosen[half, :, pl.ds(at, 2 * LANES)] + out
        return carry

    lax.fori_loop(0, blocks, one, 0, unroll=4)


def store_terms(ref, terms):
    blocks = ref.shape[0] // PAIR
    pieces = split3(ref[...].reshape(blocks, PAIR, LANES))
    terms[...] = jnp.concatenate([*pieces, jnp.zeros_like(pieces[0])], axis=1).astype(jnp.float32)


def pick_kernel(first_block, scalars, x, index, chosen, terms):
    store_terms(x, terms)
    chosen[...] = jnp.zeros_like(chosen)
    pick(scalars, index, terms, first_block, x.shape[0] // PAIR, chosen)


def picked(x, index, scalars, first_block):
    blocks = x.shape[0] // PAIR
    return call(
        functools.partial(pick_kernel, first_block),
        f32(2, 8, index.shape[1]),
        in_specs=[SMEM, VMEM, VMEM],
        out_specs=VMEM,
        scratch_shapes=[pltpu.VMEM((blocks, 8, LANES), jnp.float32)],
        cost_estimate=cost(blocks * 2 * LANES * LANES),
    )(scalars, x, index)


def last_kernel(columns, counts, scalars, received, x0, x1, x2, coupling, index, chosen0, chosen1, chosen2, send, x3, terms, chosen, buffer, ready):
    copy = pltpu.make_async_copy(coupling, buffer, ready)
    copy.start()
    x3[...] = jnp.sum(received[...], axis=0)
    store_terms(x3, terms)
    chosen[...] = chosen0[...] + chosen1[...] + chosen2[...]
    pick(scalars, index, terms, sum(counts[:3]), counts[3], chosen)
    rows = coupling.shape[0] // 2
    copy.wait()
    handed = []
    for half in range(2):
        value = chosen[half, 0:2, :columns] + chosen[half, 2:4, :columns] + chosen[half, 4:6, :columns]
        handed.append(
            lax.dot_general(
                value,
                buffer[half * rows : (half + 1) * rows, :],
                NT,
                precision=lax.Precision.HIGHEST,
                preferred_element_type=jnp.float32,
            )
        )
    send[...] = jnp.zeros_like(send)
    for dest in range(XC):
        core, x = dest // X, dest % X
        for level, ref in enumerate((x0, x1, x2, x3)):
            block = x if level < 2 else x * 2 + core
            if level < 3:
                block = block + scalars[level] * (counts[level] // (Y // 2**level))
            send[dest, 2 * level : 2 * level + 2, :] = ref[pl.ds(block * 2, 2), :]
        send[dest, 8:10, :] = handed[x // 2]


def last(received, known, chosen, coupling, index, scalars):
    columns = coupling.shape[1]
    counts = [width // LANES for width in WIDTHS]
    return call(
        functools.partial(last_kernel, columns, counts),
        f32(XC, 16, LANES),
        in_specs=[SMEM] + [VMEM] * 4 + [HBM] + [VMEM] * 4,
        out_specs=VMEM,
        scratch_shapes=[
            pltpu.VMEM(received.shape[1:], jnp.float32),
            pltpu.VMEM((counts[3], 8, LANES), jnp.float32),
            pltpu.VMEM((2, 8, columns + 2 * LANES), jnp.float32),
            pltpu.VMEM(coupling.shape, jnp.float32),
            pltpu.SemaphoreType.DMA,
        ],
        limit=WHOLE,
    )(scalars, received, *known, coupling, index, *chosen)


def finish_kernel(scalars, received, values, out0, out1, out2, out3, handed):
    z, core = scalars[0], scalars[1]
    offsets = (core * 64 + z * 8, core * 64 + z * 8, z * 16, z * 16, scalars[2] * values.shape[1])
    for level, ref in enumerate((out0, out1, out2, out3, handed)):
        value = jnp.concatenate([received[source, 2 * level : 2 * level + 2, :] for source in range(XC)], axis=0)
        moved = pltpu.roll(value, lax.rem(LANES - offsets[level], LANES), 1)[:, : ref.shape[1]]
        ref[...] = values[...] - moved if level == 4 else moved


def finish(received, values, scalars, widths):
    shapes = tuple(f32(XC * PAIR, width) for width in widths) + (f32(*values.shape),)
    return call(
        finish_kernel, shapes, in_specs=[SMEM, VMEM, VMEM]
    )(scalars, received, values)


def body(
    rhs_root,
    rhs_level1,
    rhs_level2,
    rhs_level3,
    inv_root,
    inv_level1,
    inv_level2,
    inv_level3,
    cross_level1,
    cross_level2,
    cross_level3,
    subtree_values,
    coupling,
    coupled_rows,
):
    depth = lax.axis_size("z")
    y = (lax.axis_index("y2") * 2 + lax.axis_index("y1")) * 2 + lax.axis_index("y0")
    x, c, z = lax.axis_index("x"), lax.axis_index("c"), lax.axis_index("z")
    counts = [width // LANES for width in WIDTHS]
    blocks = sum(counts)

    rhs_parts = [rhs_root, rhs_level1, rhs_level2, rhs_level3]
    small = jnp.concatenate([subtree_values] + rhs_parts, axis=1)
    small = jnp.pad(small, ((0, 0), (0, LANES - small.shape[1])))
    both_small = lax.all_gather(small, "c", axis=0, tiled=False)
    both_coupling = lax.all_gather(coupling, "c", axis=0, tiled=False)

    def gathered(parts):
        return lax.all_gather(jnp.concatenate(parts, axis=1), "x", axis=0, tiled=True)

    def swap(after, own):
        after, own = lax.optimization_barrier((after, own))
        return after, (own, lax.ppermute(own, "c", [(0, 1), (1, 0)]))

    own3 = gathered([inv_level3, cross_level3])
    own2 = gathered([inv_level2, cross_level2])
    own1 = gathered([inv_level1, cross_level1, inv_root])
    all_coupling = lax.all_gather(coupling, ("x", "c"), axis=0, tiled=True)

    both_indices = lax.dynamic_slice_in_dim(coupled_rows, y * 2, 2, 0)
    edges = jnp.arange(blocks, dtype=jnp.int32) * LANES
    windows = jnp.sum((both_indices[:, None, :] < edges[None, :, None]).astype(jnp.int32), axis=2) // LANES
    both_indices = jnp.pad(both_indices, ((0, 0), (0, 2 * LANES)), constant_values=-1)
    own_windows = lax.dynamic_index_in_dim(windows, x // 2, 0, keepdims=False)
    own_indices = lax.dynamic_slice_in_dim(both_indices, x // 2, 1, 0)

    def scalars(head, *tails):
        head = jnp.stack([jnp.asarray(value, jnp.int32) for value in head] + [jnp.int32(0)] * (8 - len(head)))
        return jnp.concatenate([head, *tails])

    places = scalars([z, c, x, y, y % 4, y % 2], own_windows)
    send = first(both_small, both_coupling, own_indices, places, depth)
    received, matrix3 = swap(exchange(send, ("x", "z")), own3)
    solved3, send, rest = forward(
        received, matrix3, jnp.zeros((8, LANES), jnp.float32), places, counts[3], sum(counts[:3]), counts[0] + counts[1], 2 * depth, depth
    )
    send, matrix2 = swap(send, own2)
    received = exchange(send, ("y0", "z"))
    solved2, send, rest = forward(received, matrix2, rest, places, counts[2], counts[0] + counts[1], counts[0], 4 * depth, 0)
    send, matrix1 = swap(send, own1)
    received = exchange(send, ("y1", "y0", "z"))
    solved1, send, rest = forward(received, matrix1, rest, places, counts[1], counts[0], 0, Y, 0)

    def sum_root(copies):
        received = exchange(copies.reshape(Y * depth, -1, LANES), ALL_Y + ("z",))
        return exchange(sum_and_copy(received, depth), ("z",))

    target = sum_root(send).reshape(-1, LANES)
    received = sum_root(root(target, matrix1, WIDTHS[1] + WIDTHS[0], Y)).reshape(1, -1, LANES)
    heads = scalars([y, y % 4, y % 2], windows.reshape(-1))
    send, x0 = backward(received, matrix1, solved1, [], counts[1], 4 * depth)
    received = exchange(send, ("y1", "y0", "z"))
    received, chosen0 = lax.optimization_barrier((received, picked(x0, both_indices, heads, 0)))
    send, x1 = backward(received, matrix2, solved2, [x0], counts[2], 2 * depth)
    received = exchange(send, ("y0", "z"))
    received, chosen1 = lax.optimization_barrier((received, picked(x1, both_indices, heads, counts[0])))
    send, x2 = backward(received, matrix3, solved3, [x0, x1], counts[3], depth)
    received = exchange(send, ("z",))
    chosen2 = picked(x2, both_indices, heads, counts[0] + counts[1])
    send = last(received, [x0, x1, x2], [chosen0, chosen1, chosen2], all_coupling, both_indices, heads)
    received = exchange(send, ("c", "x"))
    ends = scalars([z, c, (x % 2) * 2 + c])
    return finish(received, subtree_values, ends, [part.shape[1] for part in rhs_parts])


def solution(mesh):
    shape = (2, 2, 2, X, C, mesh.shape["sep"])
    fine = Mesh(mesh.devices.reshape(shape), ("y2", "y1", "y0", "x", "c", "z"))
    every = ("y2", "y1", "y0", "x", "c", "z")
    columns, rows = P(None, every), P(every, None)
    in_specs = (columns,) * 4 + (rows,) * 7 + (columns, rows, P())
    return jax.shard_map(body, mesh=fine, in_specs=in_specs, out_specs=(columns,) * 5, check_vma=False)
```

```python
import functools

import jax
import jax.numpy as jnp
from jax import lax
from jax.experimental import pallas as pl
from jax.experimental.pallas import tpu as pltpu
from jax.sharding import Mesh, PartitionSpec as P

ROOT_ROWS = 4096
LEVEL1_ROWS = 2048
LEVEL2_ROWS = 2048
LEVEL3_ROWS = 1024
WIDTHS = (ROOT_ROWS, LEVEL1_ROWS, LEVEL2_ROWS, LEVEL3_ROWS)
Y, X, C = 8, 4, 2
XC = X * C
PAIR = 2
LANES = 128
CHUNK = 32
HBM = pl.BlockSpec(memory_space=pltpu.HBM)
LIMIT = 16 * 2**20
WHOLE = 58 * 2**20
ALL_Y = ("y2", "y1", "y0")
INTERPRET = False
VMEM = pl.BlockSpec(memory_space=pltpu.VMEM)
SMEM = pl.BlockSpec(memory_space=pltpu.SMEM)


def call(kernel, out_shape, **options):
    limit = options.pop("limit", LIMIT)
    return pl.pallas_call(
        kernel,
        out_shape=out_shape,
        compiler_params=pltpu.CompilerParams(vmem_limit_bytes=limit),
        interpret=INTERPRET,
        **options,
    )


def cost(elements):
    return pl.CostEstimate(flops=8 * elements, bytes_accessed=4 * elements, transcendentals=0)


def f32(*shape):
    return jax.ShapeDtypeStruct(shape, jnp.float32)


def exchange(operand, axes):
    flat = operand.reshape(-1, LANES)
    return lax.all_to_all(flat, axes, 0, 0, tiled=True).reshape(operand.shape)


def split3(value):
    high = value.astype(jnp.bfloat16)
    rest = value - high.astype(jnp.float32)
    middle = rest.astype(jnp.bfloat16)
    low = (rest - middle.astype(jnp.float32)).astype(jnp.bfloat16)
    return high, middle, low


def one_hot(index_row, block):
    shape = (LANES, index_row.shape[1])
    rows = lax.broadcasted_iota(jnp.int32, shape, 0) + block * LANES
    return jnp.where(rows == index_row, 1.0, 0.0).astype(jnp.bfloat16)


NT = (((1,), (1,)), ((), ()))
NN = (((1,), (0,)), ((), ()))


def row_dot(matrix, rows, column, vector, first, blocks):
    sums = [jnp.zeros((CHUNK, LANES), jnp.float32) for _ in range(PAIR)]
    for block in range(blocks):
        tile = matrix[rows, column + block * LANES : column + (block + 1) * LANES]
        for s in range(PAIR):
            at = (first + block) * PAIR + s
            sums[s] = sums[s] + tile * vector[at : at + 1, :]
    return [jnp.sum(value, axis=1, keepdims=True) for value in sums]


def column_dot(matrix, rows, column, blocks, factors, total):
    wide = [jnp.broadcast_to(value, (CHUNK, LANES)) for value in factors]
    for block in range(blocks):
        tile = matrix[rows, column + block * LANES : column + (block + 1) * LANES]
        for s in range(PAIR):
            part = jnp.sum((tile * wide[s]).reshape(CHUNK // 8, 8, LANES), axis=0)
            at = block * PAIR + s
            total[at] = total[at] + part


def chunk_copies(matrices, buffer, ready):
    copies = []
    for number, matrix in enumerate(matrices):
        count = matrix.shape[0] // CHUNK
        for chunk in range(count):
            place = number * count + chunk
            columns = pl.ds(0, buffer.shape[1])
            source = matrix.at[pl.ds(chunk * CHUNK, CHUNK), columns]
            copies.append(pltpu.make_async_copy(source, buffer.at[pl.ds(place * CHUNK, CHUNK), columns], ready.at[place]))
    for copy in copies:
        copy.start()
    return copies


def each_chunk(copies, step):
    for place, copy in enumerate(copies):
        copy.wait()
        step(pl.ds(place * CHUNK, CHUNK))


def chunk_buffers(rows, width):
    return [pltpu.VMEM((rows, width), jnp.float32), pltpu.SemaphoreType.DMA((rows // CHUNK,))]


def forward_kernel(blocks, upper, keep, extra, scalars, received, matrix, rest_in, solved, send, rest, vector, total, buffer, ready):
    copies = chunk_copies((matrix,), buffer, ready)
    if extra:
        for source in range(blocks):
            vector[2 * source : 2 * source + 2, :] = received[source, 0:2, :]
    else:
        vector[...] = jnp.sum(received[...], axis=0)
    total[...] = jnp.zeros_like(total)

    def step(rows):
        values = row_dot(buffer, rows, 0, vector, 0, blocks)
        for s in range(PAIR):
            solved[s, rows, :] = jnp.broadcast_to(values[s], (CHUNK, LANES))
        column_dot(buffer, rows, blocks * LANES, upper, values, total)

    each_chunk(copies, step)
    whole = -jnp.sum(total[...], axis=1)
    if extra:
        rest[...] = whole
        for row in range(extra):
            at = pl.ds(scalars[6] * extra + row, 1)
            rest[at, :] = rest[at, :] + rest_in[2 + row : 3 + row, :]
        whole = rest[...]
    else:
        whole = whole + rest_in[0 : 2 * upper, :]
        rest[...] = whole
    for copy in range(send.shape[0]):
        send[copy] = whole[2 * keep :, :]


def forward(received, matrix, rest_in, scalars, blocks, upper, keep, copies, extra):
    rows = matrix.shape[0]
    width = upper * LANES + blocks * LANES
    return call(
        functools.partial(forward_kernel, blocks, upper, keep, extra),
        (f32(PAIR, rows, LANES), f32(copies, 2 * (upper - keep), LANES), f32(2 * upper, LANES)),
        in_specs=[SMEM, VMEM, HBM, VMEM],
        out_specs=(VMEM,) * 3,
        scratch_shapes=[pltpu.VMEM((2 * blocks, LANES), jnp.float32), pltpu.VMEM((2 * upper, 8, LANES), jnp.float32)]
        + chunk_buffers(rows, width),
        cost_estimate=cost(rows * width),
        limit=WHOLE,
    )(scalars, received, matrix, rest_in)


def lowest_kernel(blocks, upper, received, own, other, path, send, total, buffer, ready):
    rows = own.shape[0]
    copies = []
    for number, matrix in enumerate((own, other)):
        copies.append(pltpu.make_async_copy(matrix, buffer.at[pl.ds(number * rows, rows), :], ready.at[number]))
    for copy in copies:
        copy.start()
    for copy in copies:
        copy.wait()
    samples = range(received.shape[1])
    sums = [jnp.zeros((2 * rows, LANES), jnp.float32) for _ in samples]
    for block in range(blocks):
        tile = buffer[:, block * LANES : (block + 1) * LANES]
        for s in samples:
            sums[s] = sums[s] + tile * received[block, s : s + 1, :]
    wide = [jnp.broadcast_to(jnp.sum(value, axis=1, keepdims=True), (2 * rows, LANES)) for value in sums]
    for s in samples:
        total[s] = wide[s]

    def one(block, carry):
        at = pl.multiple_of((blocks + block) * LANES, LANES)
        tile = buffer[:, pl.ds(at, LANES)]
        parts = [jnp.sum(tile * total[s], axis=0, keepdims=True) for s in samples]
        path_block = path[block] - jnp.concatenate(parts, axis=0)
        send_block(block, path_block)
        return carry

    groups = send.shape[0] // X
    share = (upper - groups) // groups

    def send_block(block, value):
        low = block >= upper - groups
        place = jnp.where(low, block - (upper - groups), block // share)
        row = jnp.where(low, 0, 2 + 2 * lax.rem(block, share))
        depth = groups // 2
        for x in range(X):
            dest = (place // depth) * (X * depth) + x * depth + lax.rem(place, depth)
            send[dest, pl.ds(row, 2), :] = value[2 * x : 2 * x + 2, :]

    lax.fori_loop(0, upper, one, 0, unroll=4)


def lowest(received, own, other, path, blocks, upper, groups):
    rows, width = own.shape
    return call(
        functools.partial(lowest_kernel, blocks, upper),
        f32(X * groups, 8, LANES),
        in_specs=[VMEM, HBM, HBM, VMEM],
        out_specs=VMEM,
        scratch_shapes=[
            pltpu.VMEM((received.shape[1], 2 * rows, LANES), jnp.float32),
            pltpu.VMEM((2 * rows, width), jnp.float32),
            pltpu.SemaphoreType.DMA((2,)),
        ],
        cost_estimate=cost(2 * rows * width),
    )(received, own, other, path)


def backward_kernel(blocks, known_blocks, scalars, received, matrix, solved, *refs):
    known, (send, newest, total, vector, buffer, ready) = refs[: len(known_blocks) - 1], refs[len(known_blocks) - 1 :]
    copies = chunk_copies((matrix,), buffer, ready)
    newest[...] = jnp.sum(received[...], axis=0)
    total[...] = jnp.zeros_like(total)
    again = solved.shape[2] == LANES and solved.shape[0] == blocks
    if again:
        for block in range(blocks):
            vector[2 * block : 2 * block + 2, :] = solved[block, pl.ds(scalars[2] * 2, 2), :]

    def step(rows):
        if again:
            values = row_dot(buffer, rows, 0, vector, 0, blocks)
        else:
            values = [solved[s, rows, 0:1] for s in range(PAIR)]
        column = blocks * LANES
        for ref, count in zip((*known, newest), known_blocks):
            part = row_dot(buffer, rows, column, ref, 0, count)
            values = [values[s] - part[s] for s in range(PAIR)]
            column += count * LANES
        column_dot(buffer, rows, 0, blocks, values, total)

    each_chunk(copies, step)
    whole = jnp.sum(total[...], axis=1)
    for copy in range(send.shape[0]):
        send[copy] = whole


def backward(received, matrix, solved, known, scalars, blocks, copies):
    rows = matrix.shape[0]
    counts = [array.shape[0] // PAIR for array in known] + [received.shape[1] // PAIR]
    width = (blocks + sum(counts)) * LANES
    return call(
        functools.partial(backward_kernel, blocks, counts),
        (f32(copies, 2 * blocks, LANES), f32(*received.shape[1:])),
        in_specs=[SMEM, VMEM, HBM, VMEM] + [VMEM] * len(known),
        out_specs=(VMEM,) * 2,
        scratch_shapes=[pltpu.VMEM((2 * blocks, 8, LANES), jnp.float32), pltpu.VMEM((2 * blocks, LANES), jnp.float32)]
        + chunk_buffers(rows, width),
        cost_estimate=cost(rows * width),
        limit=WHOLE,
    )(scalars, received, matrix, solved, *known)


def root_kernel(column, blocks, vector, matrix, send, total, buffer, ready):
    copies = chunk_copies((matrix.at[:, column:],), buffer, ready)
    total[...] = jnp.zeros_like(total)

    def step(rows):
        values = row_dot(buffer, rows, 0, vector, 0, blocks)
        column_dot(buffer, rows, 0, blocks, values, total)

    each_chunk(copies, step)
    whole = jnp.sum(total[...], axis=1)
    for copy in range(send.shape[0]):
        send[copy] = whole


def root(vector, matrix, column, copies):
    rows = matrix.shape[0]
    blocks = vector.shape[0] // PAIR
    return call(
        functools.partial(root_kernel, column, blocks),
        f32(copies, 2 * blocks, LANES),
        in_specs=[VMEM, HBM],
        out_specs=VMEM,
        scratch_shapes=[pltpu.VMEM((2 * blocks, 8, LANES), jnp.float32)] + chunk_buffers(rows, blocks * LANES),
        cost_estimate=cost(rows * blocks * LANES),
        limit=WHOLE,
    )(vector, matrix)


def sum_kernel(copies, received, send):
    whole = jnp.sum(received[...], axis=0)
    for copy in range(copies):
        send[copy] = whole


def sum_and_copy(received, copies):
    return call(functools.partial(sum_kernel, copies), f32(copies, *received.shape[1:]))(received)


def first_kernel(depth, scalars, small, coupling, index, send, path, terms):
    z, core, x = scalars[0], scalars[1], scalars[2]
    upper = sum(WIDTHS[:3]) // LANES
    count = upper + WIDTHS[3] // LANES
    rows, columns = coupling.shape[1:]
    half = pl.multiple_of(core * 8, 8)
    parts = [small[other, pl.ds(half, 8), :] for other in range(C)]
    update = None
    for other in range(C):
        product = lax.dot_general(
            parts[other][:, :rows], coupling[other], NN, precision=lax.Precision.HIGHEST, preferred_element_type=jnp.float32
        )
        update = product if update is None else update + product
    pieces = split3(update)
    terms[:, columns:] = jnp.zeros((32, terms.shape[1] - columns), jnp.bfloat16)
    terms[:, :columns] = jnp.concatenate([*pieces, jnp.zeros_like(pieces[0])], axis=0)

    def expand(block, carry):
        at = pl.multiple_of(scalars[8 + block] * LANES, LANES)
        selector = one_hot(index[0:1, pl.ds(at, 2 * LANES)], block)
        out = lax.dot_general(terms[:, pl.ds(at, 2 * LANES)], selector, NT, preferred_element_type=jnp.float32)
        path[block] = -(out[0:8] + out[8:16] + out[16:24])
        return carry

    lax.fori_loop(0, count, expand, 0, unroll=4)

    lane = lax.broadcasted_iota(jnp.int32, (8, LANES), 1)
    start = 0
    source = rows
    for height in range(4):
        width = 8 if height < 2 else 16
        for other in range(C):
            offset = z * width
            block = start
            if height < 3:
                block = block + scalars[3 + height] * (XC * depth * width // LANES)
            if width == 8:
                offset = offset + other * 64
                block = block + x
            else:
                block = block + x * 2 + other
            moved = pltpu.roll(parts[other], lax.rem(offset - source + LANES, LANES), 1)
            kept = jnp.where((lane >= offset) & (lane < offset + width), moved, 0.0)
            path[block] = path[block] + kept
        start += WIDTHS[height] // LANES
        source += width

    for dest in range(X):
        for other in range(depth):
            send[dest * depth + other] = path[upper + other]


def first(small, coupling, index, scalars, depth):
    columns = coupling.shape[2]
    upper = sum(WIDTHS[:3]) // LANES
    lower = WIDTHS[3] // LANES
    return call(
        functools.partial(first_kernel, depth),
        (f32(X * depth, 8, LANES), f32(upper + lower, 8, LANES)),
        in_specs=[SMEM, VMEM, VMEM, VMEM],
        out_specs=(VMEM, VMEM),
        scratch_shapes=[pltpu.VMEM((32, columns + 2 * LANES), jnp.bfloat16)],
    )(scalars, small, coupling, index)


def pick(scalars, index, terms, first_block, blocks, chosen):
    total = sum(WIDTHS) // LANES

    def one(block, carry):
        for half in range(2):
            at = pl.multiple_of(scalars[8 + half * total + first_block + block] * LANES, LANES)
            selector = one_hot(index[half : half + 1, pl.ds(at, 2 * LANES)], first_block + block)
            out = lax.dot_general(
                terms[block].astype(jnp.bfloat16), selector, NN, preferred_element_type=jnp.float32
            )
            chosen[half, :, pl.ds(at, 2 * LANES)] = chosen[half, :, pl.ds(at, 2 * LANES)] + out
        return carry

    lax.fori_loop(0, blocks, one, 0, unroll=4)


def store_terms(ref, terms):
    blocks = ref.shape[0] // PAIR
    pieces = split3(ref[...].reshape(blocks, PAIR, LANES))
    terms[...] = jnp.concatenate([*pieces, jnp.zeros_like(pieces[0])], axis=1).astype(jnp.float32)


def pick_kernel(first_block, scalars, x, index, chosen, terms):
    store_terms(x, terms)
    chosen[...] = jnp.zeros_like(chosen)
    pick(scalars, index, terms, first_block, x.shape[0] // PAIR, chosen)


def picked(x, index, scalars, first_block):
    blocks = x.shape[0] // PAIR
    return call(
        functools.partial(pick_kernel, first_block),
        f32(2, 8, index.shape[1]),
        in_specs=[SMEM, VMEM, VMEM],
        out_specs=VMEM,
        scratch_shapes=[pltpu.VMEM((blocks, 8, LANES), jnp.float32)],
        cost_estimate=cost(blocks * 2 * LANES * LANES),
    )(scalars, x, index)


def last_kernel(columns, counts, scalars, received, x0, x1, x2, coupling, index, chosen0, chosen1, chosen2, send, x3, terms, chosen, buffer, ready):
    copy = pltpu.make_async_copy(coupling, buffer, ready)
    copy.start()
    x3[...] = jnp.sum(received[...], axis=0)
    store_terms(x3, terms)
    chosen[...] = chosen0[...] + chosen1[...] + chosen2[...]
    pick(scalars, index, terms, sum(counts[:3]), counts[3], chosen)
    rows = coupling.shape[0] // 2
    copy.wait()
    handed = []
    for half in range(2):
        value = chosen[half, 0:2, :columns] + chosen[half, 2:4, :columns] + chosen[half, 4:6, :columns]
        handed.append(
            lax.dot_general(
                value,
                buffer[half * rows : (half + 1) * rows, :],
                NT,
                precision=lax.Precision.HIGHEST,
                preferred_element_type=jnp.float32,
            )
        )
    send[...] = jnp.zeros_like(send)
    for dest in range(XC):
        core, x = dest // X, dest % X
        for level, ref in enumerate((x0, x1, x2, x3)):
            block = x if level < 2 else x * 2 + core
            if level < 3:
                block = block + scalars[level] * (counts[level] // (Y // 2**level))
            send[dest, 2 * level : 2 * level + 2, :] = ref[pl.ds(block * 2, 2), :]
        send[dest, 8:10, :] = handed[x // 2]


def last(received, known, chosen, coupling, index, scalars):
    columns = coupling.shape[1]
    counts = [width // LANES for width in WIDTHS]
    return call(
        functools.partial(last_kernel, columns, counts),
        f32(XC, 16, LANES),
        in_specs=[SMEM] + [VMEM] * 4 + [HBM] + [VMEM] * 4,
        out_specs=VMEM,
        scratch_shapes=[
            pltpu.VMEM(received.shape[1:], jnp.float32),
            pltpu.VMEM((counts[3], 8, LANES), jnp.float32),
            pltpu.VMEM((2, 8, columns + 2 * LANES), jnp.float32),
            pltpu.VMEM(coupling.shape, jnp.float32),
            pltpu.SemaphoreType.DMA,
        ],
        limit=WHOLE,
    )(scalars, received, *known, coupling, index, *chosen)


def finish_kernel(scalars, received, values, out0, out1, out2, out3, handed):
    z, core = scalars[0], scalars[1]
    offsets = (core * 64 + z * 8, core * 64 + z * 8, z * 16, z * 16, scalars[2] * values.shape[1])
    for level, ref in enumerate((out0, out1, out2, out3, handed)):
        value = jnp.concatenate([received[source, 2 * level : 2 * level + 2, :] for source in range(XC)], axis=0)
        moved = pltpu.roll(value, lax.rem(LANES - offsets[level], LANES), 1)
        if level < 2:
            ref[...] = jnp.transpose(moved)[: ref.shape[0], :]
        elif level < 4:
            ref[...] = moved[:, : ref.shape[1]]
        else:
            ref[...] = values[...] - moved[:, : ref.shape[1]]


def finish(received, values, scalars, widths):
    samples = XC * PAIR
    shapes = [f32(width, samples) for width in widths[:2]] + [f32(samples, width) for width in widths[2:]]
    outs = call(finish_kernel, (*shapes, f32(*values.shape)), in_specs=[SMEM, VMEM, VMEM])(scalars, received, values)
    return outs[0].T, outs[1].T, *outs[2:]


def body(
    rhs_root,
    rhs_level1,
    rhs_level2,
    rhs_level3,
    inv_root,
    inv_level1,
    inv_level2,
    inv_level3,
    cross_level1,
    cross_level2,
    cross_level3,
    subtree_values,
    coupling,
    coupled_rows,
):
    depth = lax.axis_size("z")
    y = (lax.axis_index("y2") * 2 + lax.axis_index("y1")) * 2 + lax.axis_index("y0")
    x, c, z = lax.axis_index("x"), lax.axis_index("c"), lax.axis_index("z")
    counts = [width // LANES for width in WIDTHS]
    blocks = sum(counts)

    rhs_parts = [rhs_root, rhs_level1, rhs_level2, rhs_level3]
    small = jnp.concatenate([subtree_values] + rhs_parts, axis=1)
    small = jnp.pad(small, ((0, 0), (0, LANES - small.shape[1])))
    both_small = lax.all_gather(small, "c", axis=0, tiled=False)
    both_coupling = lax.all_gather(coupling, "c", axis=0, tiled=False)

    def gathered(whole):
        return lax.all_gather(whole, ("x", "c"), axis=0, tiled=True)

    matrix2 = gathered(jnp.concatenate([inv_level2, cross_level2], axis=1))
    matrix1 = gathered(jnp.concatenate([inv_level1, cross_level1, inv_root], axis=1))

    both_indices = lax.dynamic_slice_in_dim(coupled_rows, y * 2, 2, 0)
    edges = jnp.arange(blocks, dtype=jnp.int32) * LANES
    windows = jnp.sum((both_indices[:, None, :] < edges[None, :, None]).astype(jnp.int32), axis=2) // LANES
    both_indices = jnp.pad(both_indices, ((0, 0), (0, 2 * LANES)), constant_values=-1)
    own_windows = lax.dynamic_index_in_dim(windows, x // 2, 0, keepdims=False)
    own_indices = lax.dynamic_slice_in_dim(both_indices, x // 2, 1, 0)

    def scalars(head, *tails):
        head = jnp.stack([jnp.asarray(value, jnp.int32) for value in head] + [jnp.int32(0)] * (8 - len(head)))
        return jnp.concatenate([head, *tails])

    places = scalars([z, c, x, y, y % 4, y % 2, (y % 2) * depth + z], own_windows)
    send, path = first(both_small, both_coupling, own_indices, places, depth)
    send, inv_level3, cross_level3, coupling = lax.optimization_barrier((send, inv_level3, cross_level3, coupling))
    own3 = jnp.concatenate([inv_level3, cross_level3], axis=1)
    received, other3 = lax.optimization_barrier(
        (exchange(send, ("x", "z")), lax.ppermute(own3, "c", [(0, 1), (1, 0)]))
    )
    target3 = exchange(sum_and_copy(received, depth), ("z",))
    send = lowest(target3, own3, other3, path, counts[3], sum(counts[:3]), 2 * depth)
    send, own3, coupling = lax.optimization_barrier((send, own3, coupling))
    matrix3 = gathered(own3)
    all_coupling = gathered(coupling)
    received = sum_and_copy(exchange(send, ("y0", "x", "z")), 2 * depth)
    solved2, send, rest = forward(
        exchange(received, ("y0", "z")), matrix2, received[0], places, counts[2], counts[0] + counts[1], counts[0], 4 * depth, 6
    )
    received = exchange(send, ("y1", "y0", "z"))
    solved1, send, rest = forward(received, matrix1, rest, places, counts[1], counts[0], 0, Y, 0)

    def sum_root(copies):
        received = exchange(copies.reshape(Y * depth, -1, LANES), ALL_Y + ("z",))
        return exchange(sum_and_copy(received, depth), ("z",))

    target = sum_root(send).reshape(-1, LANES)
    received = sum_root(root(target, matrix1, WIDTHS[1] + WIDTHS[0], Y)).reshape(1, -1, LANES)
    heads = scalars([y, y % 4, y % 2], windows.reshape(-1))
    send, x0 = backward(received, matrix1, solved1, [], places, counts[1], 4 * depth)
    received = exchange(send, ("y1", "y0", "z"))
    received, chosen0 = lax.optimization_barrier((received, picked(x0, both_indices, heads, 0)))
    send, x1 = backward(received, matrix2, solved2, [x0], places, counts[2], 2 * depth)
    received = exchange(send, ("y0", "z"))
    received, chosen1 = lax.optimization_barrier((received, picked(x1, both_indices, heads, counts[0])))
    send, x2 = backward(received, matrix3, target3, [x0, x1], places, counts[3], depth)
    received = exchange(send, ("z",))
    chosen2 = picked(x2, both_indices, heads, counts[0] + counts[1])
    send = last(received, [x0, x1, x2], [chosen0, chosen1, chosen2], all_coupling, both_indices, heads)
    received = exchange(send, ("c", "x"))
    ends = scalars([z, c, (x % 2) * 2 + c])
    return finish(received, subtree_values, ends, [part.shape[1] for part in rhs_parts])


def solution(mesh):
    shape = (2, 2, 2, X, C, mesh.shape["sep"])
    fine = Mesh(mesh.devices.reshape(shape), ("y2", "y1", "y0", "x", "c", "z"))
    every = ("y2", "y1", "y0", "x", "c", "z")
    columns, rows = P(None, every), P(every, None)
    in_specs = (columns,) * 4 + (rows,) * 7 + (columns, rows, P())
    return jax.shard_map(body, mesh=fine, in_specs=in_specs, out_specs=(columns,) * 5, check_vma=False)
```

```python
import functools

import jax
import jax.numpy as jnp
from jax import lax
from jax.experimental import pallas as pl
from jax.experimental.pallas import tpu as pltpu
from jax.sharding import Mesh, PartitionSpec as P

ROOT_ROWS = 4096
LEVEL1_ROWS = 2048
LEVEL2_ROWS = 2048
LEVEL3_ROWS = 1024
WIDTHS = (ROOT_ROWS, LEVEL1_ROWS, LEVEL2_ROWS, LEVEL3_ROWS)
Y, X, C = 8, 4, 2
XC = X * C
PAIR = 2
LANES = 128
CHUNK = 32
HBM = pl.BlockSpec(memory_space=pltpu.HBM)
LIMIT = 16 * 2**20
WHOLE = 50 * 2**20
ALL_Y = ("y2", "y1", "y0")
INTERPRET = False
VMEM = pl.BlockSpec(memory_space=pltpu.VMEM)
SMEM = pl.BlockSpec(memory_space=pltpu.SMEM)


def call(kernel, out_shape, **options):
    limit = options.pop("limit", LIMIT)
    return pl.pallas_call(
        kernel,
        out_shape=out_shape,
        compiler_params=pltpu.CompilerParams(vmem_limit_bytes=limit),
        interpret=INTERPRET,
        **options,
    )


def cost(elements):
    return pl.CostEstimate(flops=8 * elements, bytes_accessed=4 * elements, transcendentals=0)


def f32(*shape):
    return jax.ShapeDtypeStruct(shape, jnp.float32)


def exchange(operand, axes):
    flat = operand.reshape(-1, LANES)
    return lax.all_to_all(flat, axes, 0, 0, tiled=True).reshape(operand.shape)


def split3(value):
    high = value.astype(jnp.bfloat16)
    rest = value - high.astype(jnp.float32)
    middle = rest.astype(jnp.bfloat16)
    low = (rest - middle.astype(jnp.float32)).astype(jnp.bfloat16)
    return high, middle, low


def one_hot(index_row, block):
    shape = (LANES, index_row.shape[1])
    rows = lax.broadcasted_iota(jnp.int32, shape, 0) + block * LANES
    return jnp.where(rows == index_row, 1.0, 0.0).astype(jnp.bfloat16)


NT = (((1,), (1,)), ((), ()))
NN = (((1,), (0,)), ((), ()))


def row_dot(matrix, rows, column, vector, first, blocks):
    sums = [jnp.zeros((CHUNK, LANES), jnp.float32) for _ in range(PAIR)]
    for block in range(blocks):
        tile = matrix[rows, column + block * LANES : column + (block + 1) * LANES]
        for s in range(PAIR):
            at = (first + block) * PAIR + s
            sums[s] = sums[s] + tile * vector[at : at + 1, :]
    return [jnp.sum(value, axis=1, keepdims=True) for value in sums]


def column_dot(matrix, rows, column, blocks, factors, total):
    wide = [jnp.broadcast_to(value, (CHUNK, LANES)) for value in factors]
    for block in range(blocks):
        tile = matrix[rows, column + block * LANES : column + (block + 1) * LANES]
        for s in range(PAIR):
            part = jnp.sum((tile * wide[s]).reshape(CHUNK // 8, 8, LANES), axis=0)
            at = block * PAIR + s
            total[at] = total[at] + part


def chunk_copies(matrix, buffer, ready):
    copies = []
    for place in range(matrix.shape[0] // 8):
        rows, columns = pl.ds(place * 8, 8), pl.ds(0, buffer.shape[1])
        copies.append(pltpu.make_async_copy(matrix.at[rows, columns], buffer.at[rows, columns], ready.at[place]))
    for copy in copies:
        copy.start()
    return copies


def each_chunk(copies, step):
    share = CHUNK // 8
    for chunk in range(len(copies) // share):
        for copy in copies[chunk * share : (chunk + 1) * share]:
            copy.wait()
        step(pl.ds(chunk * CHUNK, CHUNK))


def chunk_buffers(rows, width):
    return [pltpu.VMEM((rows, width), jnp.float32), pltpu.SemaphoreType.DMA((rows // 8,))]


def forward_kernel(blocks, upper, keep, extra, scalars, received, matrix, rest_in, solved, send, rest, vector, total, buffer, ready):
    copies = chunk_copies(matrix, buffer, ready)
    if extra:
        for source in range(blocks):
            vector[2 * source : 2 * source + 2, :] = received[source, 0:2, :]
    else:
        vector[...] = jnp.sum(received[...], axis=0)
    total[...] = jnp.zeros_like(total)

    def step(rows):
        values = row_dot(buffer, rows, 0, vector, 0, blocks)
        for s in range(PAIR):
            solved[s, rows, :] = jnp.broadcast_to(values[s], (CHUNK, LANES))
        column_dot(buffer, rows, blocks * LANES, upper, values, total)

    each_chunk(copies, step)
    whole = -jnp.sum(total[...], axis=1)
    if extra:
        rest[...] = whole
        for row in range(extra):
            at = pl.ds(scalars[6] * extra + row, 1)
            rest[at, :] = rest[at, :] + rest_in[2 + row : 3 + row, :]
        whole = rest[...]
    else:
        whole = whole + rest_in[0 : 2 * upper, :]
        rest[...] = whole
    for copy in range(send.shape[0]):
        send[copy] = whole[2 * keep :, :]


def forward(received, matrix, rest_in, scalars, blocks, upper, keep, copies, extra):
    rows = matrix.shape[0]
    width = upper * LANES + blocks * LANES
    return call(
        functools.partial(forward_kernel, blocks, upper, keep, extra),
        (f32(PAIR, rows, LANES), f32(copies, 2 * (upper - keep), LANES), f32(2 * upper, LANES)),
        in_specs=[SMEM, VMEM, HBM, VMEM],
        out_specs=(VMEM,) * 3,
        scratch_shapes=[pltpu.VMEM((2 * blocks, LANES), jnp.float32), pltpu.VMEM((2 * upper, 8, LANES), jnp.float32)]
        + chunk_buffers(rows, width),
        cost_estimate=cost(rows * width),
        limit=WHOLE,
    )(scalars, received, matrix, rest_in)


def lowest_kernel(blocks, upper, received, own, other, path, send, total, buffer, ready):
    rows = own.shape[0]
    copies = chunk_copies(own, buffer.at[0:rows, :], ready.at[0]) + chunk_copies(other, buffer.at[rows:, :], ready.at[1])
    for copy in copies:
        copy.wait()
    samples = range(received.shape[1])
    sums = [jnp.zeros((2 * rows, LANES), jnp.float32) for _ in samples]
    for block in range(blocks):
        tile = buffer[:, block * LANES : (block + 1) * LANES]
        for s in samples:
            sums[s] = sums[s] + tile * received[block, s : s + 1, :]
    wide = [jnp.broadcast_to(jnp.sum(value, axis=1, keepdims=True), (2 * rows, LANES)) for value in sums]
    for s in samples:
        total[s] = wide[s]

    def one(block, carry):
        at = pl.multiple_of((blocks + block) * LANES, LANES)
        tile = buffer[:, pl.ds(at, LANES)]
        parts = [jnp.sum(tile * total[s], axis=0, keepdims=True) for s in samples]
        path_block = path[block] - jnp.concatenate(parts, axis=0)
        send_block(block, path_block)
        return carry

    groups = send.shape[0] // X
    share = (upper - groups) // groups

    def send_block(block, value):
        low = block >= upper - groups
        place = jnp.where(low, block - (upper - groups), block // share)
        row = jnp.where(low, 0, 2 + 2 * lax.rem(block, share))
        depth = groups // 2
        for x in range(X):
            dest = (place // depth) * (X * depth) + x * depth + lax.rem(place, depth)
            send[dest, pl.ds(row, 2), :] = value[2 * x : 2 * x + 2, :]

    lax.fori_loop(0, upper, one, 0, unroll=4)


def lowest(received, own, other, path, blocks, upper, groups):
    rows, width = own.shape
    return call(
        functools.partial(lowest_kernel, blocks, upper),
        f32(X * groups, 8, LANES),
        in_specs=[VMEM, HBM, HBM, VMEM],
        out_specs=VMEM,
        scratch_shapes=[
            pltpu.VMEM((received.shape[1], 2 * rows, LANES), jnp.float32),
            pltpu.VMEM((2 * rows, width), jnp.float32),
            pltpu.SemaphoreType.DMA((2, rows // 8)),
        ],
        cost_estimate=cost(2 * rows * width),
    )(received, own, other, path)


def backward_kernel(blocks, known_blocks, scalars, received, matrix, solved, *refs):
    known, (send, newest, total, vector, buffer, ready) = refs[: len(known_blocks) - 1], refs[len(known_blocks) - 1 :]
    copies = chunk_copies(matrix, buffer, ready)
    newest[...] = jnp.sum(received[...], axis=0)
    total[...] = jnp.zeros_like(total)
    again = solved.shape[2] == LANES and solved.shape[0] == blocks
    if again:
        for block in range(blocks):
            vector[2 * block : 2 * block + 2, :] = solved[block, pl.ds(scalars[2] * 2, 2), :]

    def step(rows):
        if again:
            values = row_dot(buffer, rows, 0, vector, 0, blocks)
        else:
            values = [solved[s, rows, 0:1] for s in range(PAIR)]
        column = blocks * LANES
        for ref, count in zip((*known, newest), known_blocks):
            part = row_dot(buffer, rows, column, ref, 0, count)
            values = [values[s] - part[s] for s in range(PAIR)]
            column += count * LANES
        column_dot(buffer, rows, 0, blocks, values, total)

    each_chunk(copies, step)
    whole = jnp.sum(total[...], axis=1)
    for copy in range(send.shape[0]):
        send[copy] = whole


def backward(received, matrix, solved, known, scalars, blocks, copies):
    rows = matrix.shape[0]
    counts = [array.shape[0] // PAIR for array in known] + [received.shape[1] // PAIR]
    width = (blocks + sum(counts)) * LANES
    return call(
        functools.partial(backward_kernel, blocks, counts),
        (f32(copies, 2 * blocks, LANES), f32(*received.shape[1:])),
        in_specs=[SMEM, VMEM, HBM, VMEM] + [VMEM] * len(known),
        out_specs=(VMEM,) * 2,
        scratch_shapes=[pltpu.VMEM((2 * blocks, 8, LANES), jnp.float32), pltpu.VMEM((2 * blocks, LANES), jnp.float32)]
        + chunk_buffers(rows, width),
        cost_estimate=cost(rows * width),
        limit=WHOLE,
    )(scalars, received, matrix, solved, *known)


def root_kernel(column, blocks, vector, matrix, send, total, buffer, ready):
    copies = chunk_copies(matrix.at[:, column:], buffer, ready)
    total[...] = jnp.zeros_like(total)

    def step(rows):
        values = row_dot(buffer, rows, 0, vector, 0, blocks)
        column_dot(buffer, rows, 0, blocks, values, total)

    each_chunk(copies, step)
    whole = jnp.sum(total[...], axis=1)
    for copy in range(send.shape[0]):
        send[copy] = whole


def root(vector, matrix, column, copies):
    rows = matrix.shape[0]
    blocks = vector.shape[0] // PAIR
    return call(
        functools.partial(root_kernel, column, blocks),
        f32(copies, 2 * blocks, LANES),
        in_specs=[VMEM, HBM],
        out_specs=VMEM,
        scratch_shapes=[pltpu.VMEM((2 * blocks, 8, LANES), jnp.float32)] + chunk_buffers(rows, blocks * LANES),
        cost_estimate=cost(rows * blocks * LANES),
        limit=WHOLE,
    )(vector, matrix)


def sum_kernel(copies, received, send):
    whole = jnp.sum(received[...], axis=0)
    for copy in range(copies):
        send[copy] = whole


def sum_and_copy(received, copies):
    return call(functools.partial(sum_kernel, copies), f32(copies, *received.shape[1:]))(received)


def expand(scalars, terms, index, first_block, path):
    def one(block, carry):
        at = pl.multiple_of(scalars[8 + first_block + block] * LANES, LANES)
        selector = one_hot(index[0:1, pl.ds(at, 2 * LANES)], first_block + block)
        out = lax.dot_general(terms[:, pl.ds(at, 2 * LANES)], selector, NT, preferred_element_type=jnp.float32)
        path[block] = -(out[0:8] + out[8:16] + out[16:24])
        return carry

    lax.fori_loop(0, path.shape[0], one, 0, unroll=4)


def add_own(scalars, small, source, depth, heights, path):
    z, core, x = scalars[0], scalars[1], scalars[2]
    half = pl.multiple_of(core * 8, 8)
    lane = lax.broadcasted_iota(jnp.int32, (8, LANES), 1)
    start = 0
    for height in range(4):
        width = 8 if height < 2 else 16
        for other in range(C):
            if height not in heights:
                continue
            offset = z * width
            block = start
            if height < 3:
                block = block + scalars[3 + height] * (XC * depth * width // LANES)
            if width == 8:
                offset = offset + other * 64
                block = block + x
            else:
                block = block + x * 2 + other
            moved = pltpu.roll(small[other, pl.ds(half, 8), :], lax.rem(offset - source + LANES, LANES), 1)
            path[block] = path[block] + jnp.where((lane >= offset) & (lane < offset + width), moved, 0.0)
        start += WIDTHS[height] // LANES if height in heights else 0
        source += width


def first_kernel(depth, scalars, small, coupling, index, send, terms, path):
    rows, columns = coupling.shape[1:]
    half = pl.multiple_of(scalars[1] * 8, 8)
    update = None
    for other in range(C):
        product = lax.dot_general(
            small[other, pl.ds(half, 8), :][:, :rows],
            coupling[other],
            NN,
            precision=lax.Precision.HIGHEST,
            preferred_element_type=jnp.float32,
        )
        update = product if update is None else update + product
    pieces = split3(update)
    terms[:, columns:] = jnp.zeros((32, terms.shape[1] - columns), jnp.bfloat16)
    terms[:, :columns] = jnp.concatenate([*pieces, jnp.zeros_like(pieces[0])], axis=0)
    expand(scalars, terms, index, sum(WIDTHS[:3]) // LANES, path)
    add_own(scalars, small, rows, depth, (3,), path)
    for dest in range(X):
        for other in range(depth):
            send[dest * depth + other] = path[other]


def first(small, coupling, index, scalars, depth):
    columns = coupling.shape[2]
    return call(
        functools.partial(first_kernel, depth),
        (f32(X * depth, 8, LANES), jax.ShapeDtypeStruct((32, columns + 2 * LANES), jnp.bfloat16)),
        in_specs=[SMEM, VMEM, VMEM, VMEM],
        out_specs=(VMEM, VMEM),
        scratch_shapes=[pltpu.VMEM((WIDTHS[3] // LANES, 8, LANES), jnp.float32)],
    )(scalars, small, coupling, index)


def upper_kernel(depth, rows, scalars, small, terms, index, path):
    expand(scalars, terms, index, 0, path)
    add_own(scalars, small, rows, depth, (0, 1, 2), path)


def upper_path(small, terms, index, scalars, depth, rows):
    blocks = sum(WIDTHS[:3]) // LANES
    return call(
        functools.partial(upper_kernel, depth, rows),
        f32(blocks, 8, LANES),
        in_specs=[SMEM, VMEM, VMEM, VMEM],
        out_specs=VMEM,
        cost_estimate=cost(blocks * LANES * LANES),
    )(scalars, small, terms, index)


def pick(scalars, index, terms, first_block, blocks, chosen):
    total = sum(WIDTHS) // LANES

    def one(block, carry):
        for half in range(2):
            at = pl.multiple_of(scalars[8 + half * total + first_block + block] * LANES, LANES)
            selector = one_hot(index[half : half + 1, pl.ds(at, 2 * LANES)], first_block + block)
            out = lax.dot_general(
                terms[block].astype(jnp.bfloat16), selector, NN, preferred_element_type=jnp.float32
            )
            chosen[half, :, pl.ds(at, 2 * LANES)] = chosen[half, :, pl.ds(at, 2 * LANES)] + out
        return carry

    lax.fori_loop(0, blocks, one, 0, unroll=4)


def store_terms(ref, terms):
    blocks = ref.shape[0] // PAIR
    pieces = split3(ref[...].reshape(blocks, PAIR, LANES))
    terms[...] = jnp.concatenate([*pieces, jnp.zeros_like(pieces[0])], axis=1).astype(jnp.float32)


def pick_kernel(first_block, scalars, x, index, chosen, terms):
    store_terms(x, terms)
    chosen[...] = jnp.zeros_like(chosen)
    pick(scalars, index, terms, first_block, x.shape[0] // PAIR, chosen)


def picked(x, index, scalars, first_block):
    blocks = x.shape[0] // PAIR
    return call(
        functools.partial(pick_kernel, first_block),
        f32(2, 8, index.shape[1]),
        in_specs=[SMEM, VMEM, VMEM],
        out_specs=VMEM,
        scratch_shapes=[pltpu.VMEM((blocks, 8, LANES), jnp.float32)],
        cost_estimate=cost(blocks * 2 * LANES * LANES),
    )(scalars, x, index)


def last_kernel(columns, counts, scalars, received, x0, x1, x2, coupling, index, chosen0, chosen1, chosen2, send, x3, terms, chosen, buffer, ready):
    copies = chunk_copies(coupling, buffer, ready)
    x3[...] = jnp.sum(received[...], axis=0)
    store_terms(x3, terms)
    chosen[...] = chosen0[...] + chosen1[...] + chosen2[...]
    pick(scalars, index, terms, sum(counts[:3]), counts[3], chosen)
    rows = coupling.shape[0] // 2
    for copy in copies:
        copy.wait()
    handed = []
    for half in range(2):
        value = chosen[half, 0:2, :columns] + chosen[half, 2:4, :columns] + chosen[half, 4:6, :columns]
        handed.append(
            lax.dot_general(
                value,
                buffer[half * rows : (half + 1) * rows, :],
                NT,
                precision=lax.Precision.HIGHEST,
                preferred_element_type=jnp.float32,
            )
        )
    send[...] = jnp.zeros_like(send)
    for dest in range(XC):
        core, x = dest // X, dest % X
        for level, ref in enumerate((x0, x1, x2, x3)):
            block = x if level < 2 else x * 2 + core
            if level < 3:
                block = block + scalars[level] * (counts[level] // (Y // 2**level))
            send[dest, 2 * level : 2 * level + 2, :] = ref[pl.ds(block * 2, 2), :]
        send[dest, 8:10, :] = handed[x // 2]


def last(received, known, chosen, coupling, index, scalars):
    columns = coupling.shape[1]
    counts = [width // LANES for width in WIDTHS]
    return call(
        functools.partial(last_kernel, columns, counts),
        f32(XC, 16, LANES),
        in_specs=[SMEM] + [VMEM] * 4 + [HBM] + [VMEM] * 4,
        out_specs=VMEM,
        scratch_shapes=[
            pltpu.VMEM(received.shape[1:], jnp.float32),
            pltpu.VMEM((counts[3], 8, LANES), jnp.float32),
            pltpu.VMEM((2, 8, columns + 2 * LANES), jnp.float32),
            *chunk_buffers(*coupling.shape),
        ],
        limit=WHOLE,
    )(scalars, received, *known, coupling, index, *chosen)


def finish_kernel(scalars, received, values, out0, out1, out2, out3, handed):
    z, core = scalars[0], scalars[1]
    offsets = (core * 64 + z * 8, core * 64 + z * 8, z * 16, z * 16, scalars[2] * values.shape[1])
    for level, ref in enumerate((out0, out1, out2, out3, handed)):
        value = jnp.concatenate([received[source, 2 * level : 2 * level + 2, :] for source in range(XC)], axis=0)
        moved = pltpu.roll(value, lax.rem(LANES - offsets[level], LANES), 1)
        if level < 2:
            ref[...] = jnp.transpose(moved)[: ref.shape[0], :]
        elif level < 4:
            ref[...] = moved[:, : ref.shape[1]]
        else:
            ref[...] = values[...] - moved[:, : ref.shape[1]]


def finish(received, values, scalars, widths):
    samples = XC * PAIR
    shapes = [f32(width, samples) for width in widths[:2]] + [f32(samples, width) for width in widths[2:]]
    outs = call(finish_kernel, (*shapes, f32(*values.shape)), in_specs=[SMEM, VMEM, VMEM])(scalars, received, values)
    return outs[0].T, outs[1].T, *outs[2:]


def body(
    rhs_root,
    rhs_level1,
    rhs_level2,
    rhs_level3,
    inv_root,
    inv_level1,
    inv_level2,
    inv_level3,
    cross_level1,
    cross_level2,
    cross_level3,
    subtree_values,
    coupling,
    coupled_rows,
):
    depth = lax.axis_size("z")
    y = (lax.axis_index("y2") * 2 + lax.axis_index("y1")) * 2 + lax.axis_index("y0")
    x, c, z = lax.axis_index("x"), lax.axis_index("c"), lax.axis_index("z")
    counts = [width // LANES for width in WIDTHS]
    blocks = sum(counts)

    rhs_parts = [rhs_root, rhs_level1, rhs_level2, rhs_level3]
    small = jnp.concatenate([subtree_values] + rhs_parts, axis=1)
    small = jnp.pad(small, ((0, 0), (0, LANES - small.shape[1])))
    both_small = lax.all_gather(small, "c", axis=0, tiled=False)
    both_coupling = lax.all_gather(coupling, "c", axis=0, tiled=False)

    def gathered(whole):
        return lax.all_gather(whole, ("x", "c"), axis=0, tiled=True)

    both_indices = lax.dynamic_slice_in_dim(coupled_rows, y * 2, 2, 0)
    edges = jnp.arange(blocks, dtype=jnp.int32) * LANES
    windows = jnp.sum((both_indices[:, None, :] < edges[None, :, None]).astype(jnp.int32), axis=2) // LANES
    both_indices = jnp.pad(both_indices, ((0, 0), (0, 2 * LANES)), constant_values=-1)
    own_windows = lax.dynamic_index_in_dim(windows, x // 2, 0, keepdims=False)
    own_indices = lax.dynamic_slice_in_dim(both_indices, x // 2, 1, 0)

    def scalars(head, *tails):
        head = jnp.stack([jnp.asarray(value, jnp.int32) for value in head] + [jnp.int32(0)] * (8 - len(head)))
        return jnp.concatenate([head, *tails])

    places = scalars([z, c, x, y, y % 4, y % 2, (y % 2) * depth + z], own_windows)
    both_small, inv_level2, cross_level2 = lax.optimization_barrier((both_small, inv_level2, cross_level2))
    matrix2 = gathered(jnp.concatenate([inv_level2, cross_level2], axis=1))
    send, terms = first(both_small, both_coupling, own_indices, places, depth)
    parts = (inv_level3, cross_level3, coupling, terms)
    send, (inv_level3, cross_level3, coupling, terms) = lax.optimization_barrier((send, parts))
    own3 = jnp.concatenate([inv_level3, cross_level3], axis=1)
    path = upper_path(both_small, terms, own_indices, places, depth, coupling.shape[0])
    received, other3, path, inv_root, inv_level1, cross_level1 = lax.optimization_barrier(
        (
            exchange(send, ("x", "z")),
            lax.ppermute(own3, "c", [(0, 1), (1, 0)]),
            path,
            inv_root,
            inv_level1,
            cross_level1,
        )
    )
    matrix1 = gathered(jnp.concatenate([inv_level1, cross_level1, inv_root], axis=1))
    target3 = exchange(sum_and_copy(received, depth), ("z",))
    send = lowest(target3, own3, other3, path, counts[3], sum(counts[:3]), 2 * depth)
    send, own3, coupling = lax.optimization_barrier((send, own3, coupling))
    matrix3 = gathered(own3)
    all_coupling = gathered(coupling)
    received = sum_and_copy(exchange(send, ("y0", "x", "z")), 2 * depth)
    solved2, send, rest = forward(
        exchange(received, ("y0", "z")), matrix2, received[0], places, counts[2], counts[0] + counts[1], counts[0], 4 * depth, 6
    )
    received = exchange(send, ("y1", "y0", "z"))
    solved1, send, rest = forward(received, matrix1, rest, places, counts[1], counts[0], 0, Y, 0)

    def sum_root(copies):
        received = exchange(copies.reshape(Y * depth, -1, LANES), ALL_Y + ("z",))
        return exchange(sum_and_copy(received, depth), ("z",))

    target = sum_root(send).reshape(-1, LANES)
    received = sum_root(root(target, matrix1, WIDTHS[1] + WIDTHS[0], Y)).reshape(1, -1, LANES)
    heads = scalars([y, y % 4, y % 2], windows.reshape(-1))
    send, x0 = backward(received, matrix1, solved1, [], places, counts[1], 4 * depth)
    received = exchange(send, ("y1", "y0", "z"))
    received, chosen0 = lax.optimization_barrier((received, picked(x0, both_indices, heads, 0)))
    send, x1 = backward(received, matrix2, solved2, [x0], places, counts[2], 2 * depth)
    received = exchange(send, ("y0", "z"))
    received, chosen1 = lax.optimization_barrier((received, picked(x1, both_indices, heads, counts[0])))
    send, x2 = backward(received, matrix3, target3, [x0, x1], places, counts[3], depth)
    received = exchange(send, ("z",))
    chosen2 = picked(x2, both_indices, heads, counts[0] + counts[1])
    send = last(received, [x0, x1, x2], [chosen0, chosen1, chosen2], all_coupling, both_indices, heads)
    received = exchange(send, ("c", "x"))
    ends = scalars([z, c, (x % 2) * 2 + c])
    return finish(received, subtree_values, ends, [part.shape[1] for part in rhs_parts])


def solution(mesh):
    shape = (2, 2, 2, X, C, mesh.shape["sep"])
    fine = Mesh(mesh.devices.reshape(shape), ("y2", "y1", "y0", "x", "c", "z"))
    every = ("y2", "y1", "y0", "x", "c", "z")
    columns, rows = P(None, every), P(every, None)
    in_specs = (columns,) * 4 + (rows,) * 7 + (columns, rows, P())
    return jax.shard_map(body, mesh=fine, in_specs=in_specs, out_specs=(columns,) * 5, check_vma=False)
```

```python
import functools

import jax
import jax.numpy as jnp
from jax import lax
from jax.experimental import pallas as pl
from jax.experimental.pallas import tpu as pltpu
from jax.sharding import Mesh, PartitionSpec as P

ROOT_ROWS = 4096
LEVEL1_ROWS = 2048
LEVEL2_ROWS = 2048
LEVEL3_ROWS = 1024
WIDTHS = (ROOT_ROWS, LEVEL1_ROWS, LEVEL2_ROWS, LEVEL3_ROWS)
Y, X, C = 8, 4, 2
XC = X * C
PAIR = 2
LANES = 128
CHUNK = 32
HBM = pl.BlockSpec(memory_space=pltpu.HBM)
LIMIT = 16 * 2**20
STREAM = 50 * 2**20
WHOLE = 57 * 2**20
ALL_Y = ("y2", "y1", "y0")
INTERPRET = False
VMEM = pl.BlockSpec(memory_space=pltpu.VMEM)
SMEM = pl.BlockSpec(memory_space=pltpu.SMEM)


def call(kernel, out_shape, **options):
    limit = options.pop("limit", LIMIT)
    return pl.pallas_call(
        kernel,
        out_shape=out_shape,
        compiler_params=pltpu.CompilerParams(vmem_limit_bytes=limit),
        interpret=INTERPRET,
        **options,
    )


def cost(elements):
    return pl.CostEstimate(flops=8 * elements, bytes_accessed=4 * elements, transcendentals=0)


def f32(*shape):
    return jax.ShapeDtypeStruct(shape, jnp.float32)


def exchange(operand, axes):
    flat = operand.reshape(-1, LANES)
    return lax.all_to_all(flat, axes, 0, 0, tiled=True).reshape(operand.shape)


def split3(value):
    high = value.astype(jnp.bfloat16)
    rest = value - high.astype(jnp.float32)
    middle = rest.astype(jnp.bfloat16)
    low = (rest - middle.astype(jnp.float32)).astype(jnp.bfloat16)
    return high, middle, low


def one_hot(index_row, block):
    shape = (LANES, index_row.shape[1])
    rows = lax.broadcasted_iota(jnp.int32, shape, 0) + block * LANES
    return jnp.where(rows == index_row, 1.0, 0.0).astype(jnp.bfloat16)


NT = (((1,), (1,)), ((), ()))
NN = (((1,), (0,)), ((), ()))


def row_dot(matrix, rows, column, vector, first, blocks):
    sums = [[None, None] for _ in range(PAIR)]
    for block in range(blocks):
        tile = matrix[rows, column + block * LANES : column + (block + 1) * LANES]
        for s in range(PAIR):
            at = (first + block) * PAIR + s
            part, old = tile * vector[at : at + 1, :], sums[s][block % 2]
            sums[s][block % 2] = part if old is None else old + part
    return [jnp.sum(value[0] + value[1], axis=1, keepdims=True) for value in sums]


def column_dot(matrix, rows, column, blocks, factors, total):
    wide = [jnp.broadcast_to(value, (CHUNK, LANES)) for value in factors]
    for block in range(blocks):
        tile = matrix[rows, column + block * LANES : column + (block + 1) * LANES]
        for s in range(PAIR):
            part = jnp.sum((tile * wide[s]).reshape(CHUNK // 8, 8, LANES), axis=0)
            at = block * PAIR + s
            total[at] = total[at] + part


def chunk_copies(matrix, buffer, ready):
    copies = []
    for place in range(matrix.shape[0] // 8):
        rows, columns = pl.ds(place * 8, 8), pl.ds(0, buffer.shape[1])
        copies.append(pltpu.make_async_copy(matrix.at[rows, columns], buffer.at[rows, columns], ready.at[place]))
    return copies


def begin(matrix, stream):
    if not stream:
        return matrix, None
    buffer, ready = stream
    copies = chunk_copies(matrix, buffer, ready)
    start_chunk(copies, 0)
    start_chunk(copies, 1)
    return buffer, copies


def start_chunk(copies, chunk):
    share = CHUNK // 8
    for copy in copies[chunk * share : (chunk + 1) * share]:
        copy.start()


def each_chunk(matrix, copies, step):
    share = CHUNK // 8
    for chunk in range(matrix.shape[0] // CHUNK):
        if copies:
            for copy in copies[chunk * share : (chunk + 1) * share]:
                copy.wait()
            start_chunk(copies, chunk + 2)
        step(pl.ds(chunk * CHUNK, CHUNK))


def stream_buffers(matrix, width, streamed):
    rows = matrix.shape[0]
    return [pltpu.VMEM((rows, width), jnp.float32), pltpu.SemaphoreType.DMA((rows // 8,))] if streamed else []


def fetch_kernel(matrix, out, ready):
    copies = chunk_copies(matrix, out, ready)
    for copy in copies:
        copy.start()
    for copy in copies:
        copy.wait()


def fetched(matrix):
    rows, width = matrix.shape
    return call(
        fetch_kernel,
        f32(rows, width),
        in_specs=[HBM],
        out_specs=VMEM,
        scratch_shapes=[pltpu.SemaphoreType.DMA((rows // 8,))],
        cost_estimate=cost(2 * rows * width),
    )(matrix)


def forward_kernel(blocks, upper, keep, extra, scalars, received, matrix, rest_in, solved, send, rest, vector, total, *stream):
    matrix, copies = begin(matrix, stream)
    if extra:
        for source in range(blocks):
            vector[2 * source : 2 * source + 2, :] = received[source, 0:2, :]
    else:
        vector[...] = jnp.sum(received[...], axis=0)
    total[...] = jnp.zeros_like(total)

    def step(rows):
        values = row_dot(matrix, rows, 0, vector, 0, blocks)
        for s in range(PAIR):
            solved[s, rows, :] = jnp.broadcast_to(values[s], (CHUNK, LANES))
        column_dot(matrix, rows, blocks * LANES, upper, values, total)

    each_chunk(matrix, copies, step)
    whole = -jnp.sum(total[...], axis=1)
    if extra:
        rest[...] = whole
        for row in range(extra):
            at = pl.ds(scalars[6] * extra + row, 1)
            rest[at, :] = rest[at, :] + rest_in[2 + row : 3 + row, :]
        whole = rest[...]
    else:
        whole = whole + rest_in[0 : 2 * upper, :]
        rest[...] = whole
    for copy in range(send.shape[0]):
        send[copy] = whole[2 * keep :, :]


def forward(received, matrix, rest_in, scalars, blocks, upper, keep, copies, extra, streamed):
    rows = matrix.shape[0]
    width = upper * LANES + blocks * LANES
    return call(
        functools.partial(forward_kernel, blocks, upper, keep, extra),
        (f32(PAIR, rows, LANES), f32(copies, 2 * (upper - keep), LANES), f32(2 * upper, LANES)),
        in_specs=[SMEM, VMEM, HBM if streamed else VMEM, VMEM],
        out_specs=(VMEM,) * 3,
        scratch_shapes=[pltpu.VMEM((2 * blocks, LANES), jnp.float32), pltpu.VMEM((2 * upper, 8, LANES), jnp.float32)]
        + stream_buffers(matrix, width, streamed),
        limit=STREAM if streamed else LIMIT,
        cost_estimate=cost(rows * width),
    )(scalars, received, matrix, rest_in)


def lowest_kernel(blocks, upper, received, own, other, path, send, total, buffer, ready):
    rows = own.shape[0]
    copies = chunk_copies(own, buffer.at[0:rows, :], ready.at[0]) + chunk_copies(other, buffer.at[rows:, :], ready.at[1])
    for copy in copies:
        copy.start()
    for copy in copies:
        copy.wait()
    samples = range(received.shape[1])
    sums = [jnp.zeros((2 * rows, LANES), jnp.float32) for _ in samples]
    for block in range(blocks):
        tile = buffer[:, block * LANES : (block + 1) * LANES]
        for s in samples:
            sums[s] = sums[s] + tile * received[block, s : s + 1, :]
    wide = [jnp.broadcast_to(jnp.sum(value, axis=1, keepdims=True), (2 * rows, LANES)) for value in sums]
    for s in samples:
        total[s] = wide[s]

    def one(block, carry):
        at = pl.multiple_of((blocks + block) * LANES, LANES)
        tile = buffer[:, pl.ds(at, LANES)]
        parts = [jnp.sum(tile * total[s], axis=0, keepdims=True) for s in samples]
        path_block = path[block] - jnp.concatenate(parts, axis=0)
        send_block(block, path_block)
        return carry

    groups = send.shape[0] // X
    share = (upper - groups) // groups

    def send_block(block, value):
        low = block >= upper - groups
        place = jnp.where(low, block - (upper - groups), block // share)
        row = jnp.where(low, 0, 2 + 2 * lax.rem(block, share))
        depth = groups // 2
        for x in range(X):
            dest = (place // depth) * (X * depth) + x * depth + lax.rem(place, depth)
            send[dest, pl.ds(row, 2), :] = value[2 * x : 2 * x + 2, :]

    lax.fori_loop(0, upper, one, 0, unroll=4)


def lowest(received, own, other, path, blocks, upper, groups):
    rows, width = own.shape
    return call(
        functools.partial(lowest_kernel, blocks, upper),
        f32(X * groups, 8, LANES),
        in_specs=[VMEM, HBM, HBM, VMEM],
        out_specs=VMEM,
        scratch_shapes=[
            pltpu.VMEM((received.shape[1], 2 * rows, LANES), jnp.float32),
            pltpu.VMEM((2 * rows, width), jnp.float32),
            pltpu.SemaphoreType.DMA((2, rows // 8)),
        ],
        cost_estimate=cost(2 * rows * width),
    )(received, own, other, path)


def backward_kernel(blocks, known_blocks, scalars, received, matrix, solved, *refs):
    known, (send, newest, total, vector, *stream) = refs[: len(known_blocks) - 1], refs[len(known_blocks) - 1 :]
    matrix, copies = begin(matrix, stream)
    newest[...] = jnp.sum(received[...], axis=0)
    total[...] = jnp.zeros_like(total)
    again = solved.shape[2] == LANES and solved.shape[0] == blocks
    if again:
        for block in range(blocks):
            vector[2 * block : 2 * block + 2, :] = solved[block, pl.ds(scalars[2] * 2, 2), :]

    def step(rows):
        if again:
            values = row_dot(matrix, rows, 0, vector, 0, blocks)
        else:
            values = [solved[s, rows, 0:1] for s in range(PAIR)]
        column = blocks * LANES
        for ref, count in zip((*known, newest), known_blocks):
            part = row_dot(matrix, rows, column, ref, 0, count)
            values = [values[s] - part[s] for s in range(PAIR)]
            column += count * LANES
        column_dot(matrix, rows, 0, blocks, values, total)

    each_chunk(matrix, copies, step)
    whole = jnp.sum(total[...], axis=1)
    for copy in range(send.shape[0]):
        send[copy] = whole


def backward(received, matrix, solved, known, scalars, blocks, copies, streamed):
    rows = matrix.shape[0]
    counts = [array.shape[0] // PAIR for array in known] + [received.shape[1] // PAIR]
    width = (blocks + sum(counts)) * LANES
    return call(
        functools.partial(backward_kernel, blocks, counts),
        (f32(copies, 2 * blocks, LANES), f32(*received.shape[1:])),
        in_specs=[SMEM, VMEM, HBM if streamed else VMEM] + [VMEM] * (1 + len(known)),
        out_specs=(VMEM,) * 2,
        scratch_shapes=[pltpu.VMEM((2 * blocks, 8, LANES), jnp.float32), pltpu.VMEM((2 * blocks, LANES), jnp.float32)]
        + stream_buffers(matrix, width, streamed),
        limit=STREAM if streamed else LIMIT,
        cost_estimate=cost(rows * width),
    )(scalars, received, matrix, solved, *known)


def root_kernel(column, blocks, vector, matrix, send, total):
    total[...] = jnp.zeros_like(total)

    def step(rows):
        values = row_dot(matrix, rows, column, vector, 0, blocks)
        column_dot(matrix, rows, column, blocks, values, total)

    for chunk in range(matrix.shape[0] // CHUNK):
        step(pl.ds(chunk * CHUNK, CHUNK))
    whole = jnp.sum(total[...], axis=1)
    for copy in range(send.shape[0]):
        send[copy] = whole


def root(vector, matrix, column, copies):
    rows = matrix.shape[0]
    blocks = vector.shape[0] // PAIR
    return call(
        functools.partial(root_kernel, column, blocks),
        f32(copies, 2 * blocks, LANES),
        in_specs=[VMEM, VMEM],
        out_specs=VMEM,
        scratch_shapes=[pltpu.VMEM((2 * blocks, 8, LANES), jnp.float32)],
        cost_estimate=cost(rows * blocks * LANES),
    )(vector, matrix)


def sum_kernel(copies, received, send):
    whole = jnp.sum(received[...], axis=0)
    for copy in range(copies):
        send[copy] = whole


def sum_and_copy(received, copies):
    return call(functools.partial(sum_kernel, copies), f32(copies, *received.shape[1:]))(received)


def expand(scalars, terms, index, first_block, path):
    def one(block, carry):
        at = pl.multiple_of(scalars[8 + first_block + block] * LANES, LANES)
        selector = one_hot(index[0:1, pl.ds(at, 2 * LANES)], first_block + block)
        out = lax.dot_general(terms[:, pl.ds(at, 2 * LANES)], selector, NT, preferred_element_type=jnp.float32)
        path[block] = -(out[0:8] + out[8:16] + out[16:24])
        return carry

    lax.fori_loop(0, path.shape[0], one, 0, unroll=4)


def add_own(scalars, both, depth, heights, path):
    z, core, x = scalars[0], scalars[1], scalars[2]
    half = pl.multiple_of(core * 8, 8)
    lane = lax.broadcasted_iota(jnp.int32, (8, LANES), 1)
    start = source = 0
    for height in range(4):
        width = 8 if height < 2 else 16
        for other in range(C):
            if height not in heights:
                continue
            offset = z * width
            block = start
            if height < 3:
                block = block + scalars[3 + height] * (XC * depth * width // LANES)
            if width == 8:
                offset = offset + other * 64
                block = block + x
            else:
                block = block + x * 2 + other
            small = both[other, pl.ds(half, 8), both.shape[2] - LANES :]
            moved = pltpu.roll(small, lax.rem(offset - source + LANES, LANES), 1)
            path[block] = path[block] + jnp.where((lane >= offset) & (lane < offset + width), moved, 0.0)
        start += WIDTHS[height] // LANES if height in heights else 0
        source += width


def product_kernel(values, coupling, rhs0, rhs1, rhs2, rhs3, out):
    columns = coupling.shape[1]
    out[:, :columns] = lax.dot_general(
        values[...], coupling[...], NN, precision=lax.Precision.HIGHEST, preferred_element_type=jnp.float32
    )
    parts = [jnp.transpose(rhs0[...]), jnp.transpose(rhs1[...]), rhs2[...], rhs3[...]]
    filled = sum(part.shape[1] for part in parts)
    parts.append(jnp.zeros((out.shape[0], LANES - filled), jnp.float32))
    out[:, columns:] = jnp.concatenate(parts, axis=1)


def own_product(values, coupling, rhs_parts):
    rhs0, rhs1, rhs2, rhs3 = rhs_parts
    shape = f32(values.shape[0], coupling.shape[1] + LANES)
    return call(product_kernel, shape, in_specs=[VMEM] * 6, out_specs=VMEM, limit=WHOLE)(values, coupling, rhs0.T, rhs1.T, rhs2, rhs3)


def first_kernel(depth, groups, scalars, both, index, *refs):
    count = sum(groups)
    parts, (send, terms, *packs), (path, ready) = refs[:count], refs[count:-2], refs[-2:]
    copies = []
    for pack, size in zip(packs, groups):
        column = 0
        for part in parts[:size]:
            width = part.shape[1]
            for row in range(0, part.shape[0], 8):
                target = pack.at[pl.ds(row, 8), pl.ds(column, width)]
                copies.append(pltpu.make_async_copy(part.at[pl.ds(row, 8), :], target, ready.at[len(copies)]))
            column += width
        parts = parts[size:]
    for copy in copies:
        copy.start()
    columns = both.shape[2] - LANES
    half = pl.multiple_of(scalars[1] * 8, 8)
    pieces = split3(both[0, pl.ds(half, 8), :columns] + both[1, pl.ds(half, 8), :columns])
    terms[:, columns:] = jnp.zeros((32, terms.shape[1] - columns), jnp.bfloat16)
    terms[:, :columns] = jnp.concatenate([*pieces, jnp.zeros_like(pieces[0])], axis=0)
    expand(scalars, terms, index, sum(WIDTHS[:3]) // LANES, path)
    add_own(scalars, both, depth, (3,), path)
    for dest in range(X):
        for other in range(depth):
            send[dest * depth + other] = path[other]
    for copy in copies:
        copy.wait()


def first(both, index, scalars, depth, groups):
    columns = both.shape[2] - LANES
    parts = [part for group in groups for part in group]
    packs = [f32(group[0].shape[0], sum(part.shape[1] for part in group)) for group in groups]
    count = sum(part.shape[0] // 8 for part in parts)
    outs = call(
        functools.partial(first_kernel, depth, [len(group) for group in groups]),
        (f32(X * depth, 8, LANES), jax.ShapeDtypeStruct((32, columns + 2 * LANES), jnp.bfloat16), *packs),
        in_specs=[SMEM, VMEM, VMEM] + [HBM] * len(parts),
        out_specs=(VMEM, VMEM) + (HBM,) * len(packs),
        scratch_shapes=[pltpu.VMEM((WIDTHS[3] // LANES, 8, LANES), jnp.float32), pltpu.SemaphoreType.DMA((count,))],
        limit=WHOLE,
    )(scalars, both, index, *parts)
    return outs[0], outs[1], outs[2:]


def upper_kernel(depth, scalars, both, terms, index, path):
    expand(scalars, terms, index, 0, path)
    add_own(scalars, both, depth, (0, 1, 2), path)


def upper_path(both, terms, index, scalars, depth):
    blocks = sum(WIDTHS[:3]) // LANES
    return call(
        functools.partial(upper_kernel, depth),
        f32(blocks, 8, LANES),
        in_specs=[SMEM, VMEM, VMEM, VMEM],
        out_specs=VMEM,
        cost_estimate=cost(blocks * LANES * LANES),
    )(scalars, both, terms, index)


def pick(scalars, index, terms, first_block, blocks, chosen):
    total = sum(WIDTHS) // LANES

    def one(block, carry):
        for half in range(2):
            at = pl.multiple_of(scalars[8 + half * total + first_block + block] * LANES, LANES)
            selector = one_hot(index[half : half + 1, pl.ds(at, 2 * LANES)], first_block + block)
            out = lax.dot_general(
                terms[block].astype(jnp.bfloat16), selector, NN, preferred_element_type=jnp.float32
            )
            chosen[half, :, pl.ds(at, 2 * LANES)] = chosen[half, :, pl.ds(at, 2 * LANES)] + out
        return carry

    lax.fori_loop(0, blocks, one, 0, unroll=4)


def store_terms(ref, terms):
    blocks = ref.shape[0] // PAIR
    pieces = split3(ref[...].reshape(blocks, PAIR, LANES))
    terms[...] = jnp.concatenate([*pieces, jnp.zeros_like(pieces[0])], axis=1).astype(jnp.float32)


def pick_kernel(first_block, scalars, x, index, chosen, terms):
    store_terms(x, terms)
    chosen[...] = jnp.zeros_like(chosen)
    pick(scalars, index, terms, first_block, x.shape[0] // PAIR, chosen)


def picked(x, index, scalars, first_block):
    blocks = x.shape[0] // PAIR
    return call(
        functools.partial(pick_kernel, first_block),
        f32(2, 8, index.shape[1]),
        in_specs=[SMEM, VMEM, VMEM],
        out_specs=VMEM,
        scratch_shapes=[pltpu.VMEM((blocks, 8, LANES), jnp.float32)],
        cost_estimate=cost(blocks * 2 * LANES * LANES),
    )(scalars, x, index)


def last_kernel(columns, counts, scalars, received, x0, x1, x2, coupling, index, chosen0, chosen1, chosen2, send, x3, terms, chosen):
    x3[...] = jnp.sum(received[...], axis=0)
    store_terms(x3, terms)
    chosen[...] = chosen0[...] + chosen1[...] + chosen2[...]
    pick(scalars, index, terms, sum(counts[:3]), counts[3], chosen)
    rows = coupling.shape[0] // 2
    handed = []
    for half in range(2):
        value = chosen[half, 0:2, :columns] + chosen[half, 2:4, :columns] + chosen[half, 4:6, :columns]
        handed.append(
            lax.dot_general(
                value,
                coupling[half * rows : (half + 1) * rows, :],
                NT,
                precision=lax.Precision.HIGHEST,
                preferred_element_type=jnp.float32,
            )
        )
    send[...] = jnp.zeros_like(send)
    for dest in range(XC):
        core, x = dest // X, dest % X
        for level, ref in enumerate((x0, x1, x2, x3)):
            block = x if level < 2 else x * 2 + core
            if level < 3:
                block = block + scalars[level] * (counts[level] // (Y // 2**level))
            send[dest, 2 * level : 2 * level + 2, :] = ref[pl.ds(block * 2, 2), :]
        send[dest, 8:10, :] = handed[x // 2]


def last(received, known, chosen, coupling, index, scalars):
    columns = coupling.shape[1]
    counts = [width // LANES for width in WIDTHS]
    return call(
        functools.partial(last_kernel, columns, counts),
        f32(XC, 16, LANES),
        in_specs=[SMEM] + [VMEM] * 9,
        out_specs=VMEM,
        scratch_shapes=[
            pltpu.VMEM(received.shape[1:], jnp.float32),
            pltpu.VMEM((counts[3], 8, LANES), jnp.float32),
            pltpu.VMEM((2, 8, columns + 2 * LANES), jnp.float32),
        ],
    )(scalars, received, *known, coupling, index, *chosen)


def finish_kernel(scalars, received, values, out0, out1, out2, out3, handed):
    z, core = scalars[0], scalars[1]
    offsets = (core * 64 + z * 8, core * 64 + z * 8, z * 16, z * 16, scalars[2] * values.shape[1])
    for level, ref in enumerate((out0, out1, out2, out3, handed)):
        value = jnp.concatenate([received[source, 2 * level : 2 * level + 2, :] for source in range(XC)], axis=0)
        moved = pltpu.roll(value, lax.rem(LANES - offsets[level], LANES), 1)
        if level < 2:
            ref[...] = jnp.transpose(moved)[: ref.shape[0], :]
        elif level < 4:
            ref[...] = moved[:, : ref.shape[1]]
        else:
            ref[...] = values[...] - moved[:, : ref.shape[1]]


def finish(received, values, scalars, widths):
    samples = XC * PAIR
    shapes = [f32(width, samples) for width in widths[:2]] + [f32(samples, width) for width in widths[2:]]
    outs = call(finish_kernel, (*shapes, f32(*values.shape)), in_specs=[SMEM, VMEM, VMEM])(scalars, received, values)
    return outs[0].T, outs[1].T, *outs[2:]


def body(
    rhs_root,
    rhs_level1,
    rhs_level2,
    rhs_level3,
    inv_root,
    inv_level1,
    inv_level2,
    inv_level3,
    cross_level1,
    cross_level2,
    cross_level3,
    subtree_values,
    coupling,
    coupled_rows,
):
    depth = lax.axis_size("z")
    y = (lax.axis_index("y2") * 2 + lax.axis_index("y1")) * 2 + lax.axis_index("y0")
    x, c, z = lax.axis_index("x"), lax.axis_index("c"), lax.axis_index("z")
    counts = [width // LANES for width in WIDTHS]
    blocks = sum(counts)

    rhs_parts = [rhs_root, rhs_level1, rhs_level2, rhs_level3]
    both = lax.all_gather(own_product(subtree_values, coupling, rhs_parts), "c", axis=0, tiled=False)

    def gathered(whole):
        return lax.all_gather(whole, ("x", "c"), axis=0, tiled=True)

    both_indices = lax.dynamic_slice_in_dim(coupled_rows, y * 2, 2, 0)
    edges = jnp.arange(blocks, dtype=jnp.int32) * LANES
    windows = jnp.sum((both_indices[:, None, :] < edges[None, :, None]).astype(jnp.int32), axis=2) // LANES
    both_indices = jnp.pad(both_indices, ((0, 0), (0, 2 * LANES)), constant_values=-1)
    own_windows = lax.dynamic_index_in_dim(windows, x // 2, 0, keepdims=False)
    own_indices = lax.dynamic_slice_in_dim(both_indices, x // 2, 1, 0)

    def scalars(head, *tails):
        head = jnp.stack([jnp.asarray(value, jnp.int32) for value in head] + [jnp.int32(0)] * (8 - len(head)))
        return jnp.concatenate([head, *tails])

    places = scalars([z, c, x, y, y % 4, y % 2, (y % 2) * depth + z], own_windows)
    groups = ((inv_level3, cross_level3), (inv_level2, cross_level2), (inv_level1, cross_level1, inv_root))
    send, terms, (own3, pack2, pack1) = first(both, own_indices, places, depth, groups)
    matrix2 = gathered(pack2)
    matrix1 = gathered(pack1)
    path = upper_path(both, terms, own_indices, places, depth)
    received, other3, path = lax.optimization_barrier(
        (exchange(send, ("x", "z")), lax.ppermute(own3, "c", [(0, 1), (1, 0)]), path)
    )
    target3 = exchange(sum_and_copy(received, depth), ("z",))
    send = lowest(target3, own3, other3, path, counts[3], sum(counts[:3]), 2 * depth)
    send, own3, coupling = lax.optimization_barrier((send, own3, coupling))
    matrix3 = gathered(own3)
    all_coupling = gathered(coupling)
    received = sum_and_copy(exchange(send, ("y0", "x", "z")), 2 * depth)
    target2 = exchange(received, ("y0", "z"))
    solved2, send, rest = forward(
        target2, matrix2, received[0], places, counts[2], counts[0] + counts[1], counts[0], 4 * depth, 6, True
    )
    received, matrix1 = lax.optimization_barrier((exchange(send, ("y1", "y0", "z")), fetched(matrix1)))
    solved1, send, rest = forward(received, matrix1, rest, places, counts[1], counts[0], 0, Y, 0, False)

    def sum_root(copies):
        received = exchange(copies.reshape(Y * depth, -1, LANES), ALL_Y + ("z",))
        return exchange(sum_and_copy(received, depth), ("z",))

    target = sum_root(send).reshape(-1, LANES)
    received = sum_root(root(target, matrix1, WIDTHS[1] + WIDTHS[0], Y)).reshape(1, -1, LANES)
    heads = scalars([y, y % 4, y % 2], windows.reshape(-1))
    send, x0 = backward(received, matrix1, solved1, [], places, counts[1], 4 * depth, False)
    received = exchange(send, ("y1", "y0", "z"))
    received, chosen0 = lax.optimization_barrier((received, picked(x0, both_indices, heads, 0)))
    send, x1 = backward(received, matrix2, solved2, [x0], places, counts[2], 2 * depth, True)
    received = exchange(send, ("y0", "z"))
    received, chosen1, all_coupling = lax.optimization_barrier(
        (received, picked(x1, both_indices, heads, counts[0]), fetched(all_coupling))
    )
    send, x2 = backward(received, matrix3, target3, [x0, x1], places, counts[3], depth, True)
    received = exchange(send, ("z",))
    chosen2 = picked(x2, both_indices, heads, counts[0] + counts[1])
    send = last(received, [x0, x1, x2], [chosen0, chosen1, chosen2], all_coupling, both_indices, heads)
    received = exchange(send, ("c", "x"))
    ends = scalars([z, c, (x % 2) * 2 + c])
    return finish(received, subtree_values, ends, [part.shape[1] for part in rhs_parts])


def solution(mesh):
    shape = (2, 2, 2, X, C, mesh.shape["sep"])
    fine = Mesh(mesh.devices.reshape(shape), ("y2", "y1", "y0", "x", "c", "z"))
    every = ("y2", "y1", "y0", "x", "c", "z")
    columns, rows = P(None, every), P(every, None)
    in_specs = (columns,) * 4 + (rows,) * 7 + (columns, rows, P())
    return jax.shard_map(body, mesh=fine, in_specs=in_specs, out_specs=(columns,) * 5, check_vma=False)
```

```python
import functools

import jax
import jax.numpy as jnp
from jax import lax
from jax.experimental import pallas as pl
from jax.experimental.pallas import tpu as pltpu
from jax.sharding import Mesh, PartitionSpec as P

ROOT_ROWS = 4096
LEVEL1_ROWS = 2048
LEVEL2_ROWS = 2048
LEVEL3_ROWS = 1024
WIDTHS = (ROOT_ROWS, LEVEL1_ROWS, LEVEL2_ROWS, LEVEL3_ROWS)
Y, X, C = 8, 4, 2
XC = X * C
PAIR = 2
LANES = 128
CHUNK = 32
HBM = pl.BlockSpec(memory_space=pltpu.HBM)
LIMIT = 16 * 2**20
STREAM = 50 * 2**20
WHOLE = 57 * 2**20
ALL_Y = ("y2", "y1", "y0")
INTERPRET = False
VMEM = pl.BlockSpec(memory_space=pltpu.VMEM)
SMEM = pl.BlockSpec(memory_space=pltpu.SMEM)


def call(kernel, out_shape, **options):
    limit = options.pop("limit", LIMIT)
    return pl.pallas_call(
        kernel,
        out_shape=out_shape,
        compiler_params=pltpu.CompilerParams(vmem_limit_bytes=limit),
        interpret=INTERPRET,
        **options,
    )


def cost(elements):
    return pl.CostEstimate(flops=8 * elements, bytes_accessed=4 * elements, transcendentals=0)


def f32(*shape):
    return jax.ShapeDtypeStruct(shape, jnp.float32)


def exchange(operand, axes):
    flat = operand.reshape(-1, LANES)
    return lax.all_to_all(flat, axes, 0, 0, tiled=True).reshape(operand.shape)


def split3(value):
    high = value.astype(jnp.bfloat16)
    rest = value - high.astype(jnp.float32)
    middle = rest.astype(jnp.bfloat16)
    low = (rest - middle.astype(jnp.float32)).astype(jnp.bfloat16)
    return high, middle, low


def one_hot(index_row, block):
    shape = (LANES, index_row.shape[1])
    rows = lax.broadcasted_iota(jnp.int32, shape, 0) + block * LANES
    return jnp.where(rows == index_row, 1.0, 0.0).astype(jnp.bfloat16)


NT = (((1,), (1,)), ((), ()))
NN = (((1,), (0,)), ((), ()))


def row_dot(matrix, rows, column, vector, first, blocks):
    sums = [[None, None] for _ in range(PAIR)]
    for block in range(blocks):
        tile = matrix[rows, column + block * LANES : column + (block + 1) * LANES]
        for s in range(PAIR):
            at = (first + block) * PAIR + s
            part, old = tile * vector[at : at + 1, :], sums[s][block % 2]
            sums[s][block % 2] = part if old is None else old + part
    return [jnp.sum(value[0] + value[1], axis=1, keepdims=True) for value in sums]


def column_dot(matrix, rows, column, blocks, factors, total):
    wide = [jnp.broadcast_to(value, (CHUNK, LANES)) for value in factors]
    for block in range(blocks):
        tile = matrix[rows, column + block * LANES : column + (block + 1) * LANES]
        for s in range(PAIR):
            part = jnp.sum((tile * wide[s]).reshape(CHUNK // 8, 8, LANES), axis=0)
            at = block * PAIR + s
            total[at] = total[at] + part


def chunk_copies(matrix, buffer, ready):
    copies = []
    for place in range(matrix.shape[0] // 8):
        rows, columns = pl.ds(place * 8, 8), pl.ds(0, buffer.shape[1])
        copies.append(pltpu.make_async_copy(matrix.at[rows, columns], buffer.at[rows, columns], ready.at[place]))
    return copies


def begin(matrices, stream):
    if not stream:
        return matrices, None
    buffer, ready = stream
    copies = chunk_copies(matrices[-1].at[pl.ds(matrices[-1].shape[0] - buffer.shape[0], buffer.shape[0]), :], buffer, ready)
    for copy in copies:
        copy.start()
    return (*matrices[:-1], buffer), copies


def each_chunk(matrices, copies, step):
    share = CHUNK // 8
    base = 0
    for matrix in matrices:
        streamed = copies and matrix is matrices[-1]
        for chunk in range(matrix.shape[0] // CHUNK):
            if streamed:
                for copy in copies[chunk * share : (chunk + 1) * share]:
                    copy.wait()
            step(matrix, pl.ds(chunk * CHUNK, CHUNK), pl.ds(base + chunk * CHUNK, CHUNK))
        base += matrix.shape[0]


def stream_buffers(matrices, width):
    if len(matrices) == 1:
        return []
    rows = matrices[1].shape[0] - matrices[0].shape[0]
    return [pltpu.VMEM((rows, width), jnp.float32), pltpu.SemaphoreType.DMA((rows // 8,))]


def fetch_kernel(matrix, out, ready):
    copies = chunk_copies(matrix.at[pl.ds(0, out.shape[0]), :], out, ready)
    for copy in copies:
        copy.start()
    for copy in copies:
        copy.wait()


def fetched(matrix, part=1):
    rows, width = matrix.shape[0] // part, matrix.shape[1]
    return call(
        fetch_kernel,
        f32(rows, width),
        in_specs=[HBM],
        out_specs=VMEM,
        scratch_shapes=[pltpu.SemaphoreType.DMA((rows // 8,))],
        cost_estimate=cost(2 * rows * width),
    )(matrix)


def forward_kernel(blocks, upper, keep, extra, count, scalars, received, rest_in, *refs):
    matrices, (solved, send, rest, vector, total, *stream) = refs[:count], refs[count:]
    matrices, copies = begin(matrices, stream)
    if extra:
        for source in range(blocks):
            vector[2 * source : 2 * source + 2, :] = received[source, 0:2, :]
    else:
        vector[...] = jnp.sum(received[...], axis=0)
    total[...] = jnp.zeros_like(total)

    def step(matrix, rows, place):
        values = row_dot(matrix, rows, 0, vector, 0, blocks)
        for s in range(PAIR):
            solved[s, place, :] = jnp.broadcast_to(values[s], (CHUNK, LANES))
        column_dot(matrix, rows, blocks * LANES, upper, values, total)

    each_chunk(matrices, copies, step)
    whole = -jnp.sum(total[...], axis=1)
    if extra:
        rest[...] = whole
        for row in range(extra):
            at = pl.ds(scalars[6] * extra + row, 1)
            rest[at, :] = rest[at, :] + rest_in[2 + row : 3 + row, :]
        whole = rest[...]
    else:
        whole = whole + rest_in[0 : 2 * upper, :]
        rest[...] = whole
    for copy in range(send.shape[0]):
        send[copy] = whole[2 * keep :, :]


def forward(received, matrices, rest_in, scalars, blocks, upper, keep, copies, extra):
    rows = matrices[-1].shape[0]
    streamed = len(matrices) > 1
    width = upper * LANES + blocks * LANES
    return call(
        functools.partial(forward_kernel, blocks, upper, keep, extra, len(matrices)),
        (f32(PAIR, rows, LANES), f32(copies, 2 * (upper - keep), LANES), f32(2 * upper, LANES)),
        in_specs=[SMEM, VMEM, VMEM] + ([VMEM, HBM] if streamed else [VMEM]),
        out_specs=(VMEM,) * 3,
        scratch_shapes=[pltpu.VMEM((2 * blocks, LANES), jnp.float32), pltpu.VMEM((2 * upper, 8, LANES), jnp.float32)]
        + stream_buffers(matrices, width),
        limit=STREAM if streamed else LIMIT,
        cost_estimate=cost(rows * width),
    )(scalars, received, rest_in, *matrices)


def lowest_kernel(blocks, upper, received, own, other, path, send, total, buffer, ready):
    rows = own.shape[0]
    copies = chunk_copies(own, buffer.at[0:rows, :], ready.at[0]) + chunk_copies(other, buffer.at[rows:, :], ready.at[1])
    for copy in copies:
        copy.start()
    for copy in copies:
        copy.wait()
    samples = range(received.shape[1])
    sums = [jnp.zeros((2 * rows, LANES), jnp.float32) for _ in samples]
    for block in range(blocks):
        tile = buffer[:, block * LANES : (block + 1) * LANES]
        for s in samples:
            sums[s] = sums[s] + tile * received[block, s : s + 1, :]
    wide = [jnp.broadcast_to(jnp.sum(value, axis=1, keepdims=True), (2 * rows, LANES)) for value in sums]
    for s in samples:
        total[s] = wide[s]

    def one(block, carry):
        at = pl.multiple_of((blocks + block) * LANES, LANES)
        tile = buffer[:, pl.ds(at, LANES)]
        parts = [jnp.sum(tile * total[s], axis=0, keepdims=True) for s in samples]
        path_block = path[block] - jnp.concatenate(parts, axis=0)
        send_block(block, path_block)
        return carry

    groups = send.shape[0] // X
    share = (upper - groups) // groups

    def send_block(block, value):
        low = block >= upper - groups
        place = jnp.where(low, block - (upper - groups), block // share)
        row = jnp.where(low, 0, 2 + 2 * lax.rem(block, share))
        depth = groups // 2
        for x in range(X):
            dest = (place // depth) * (X * depth) + x * depth + lax.rem(place, depth)
            send[dest, pl.ds(row, 2), :] = value[2 * x : 2 * x + 2, :]

    lax.fori_loop(0, upper, one, 0, unroll=4)


def lowest(received, own, other, path, blocks, upper, groups):
    rows, width = own.shape
    return call(
        functools.partial(lowest_kernel, blocks, upper),
        f32(X * groups, 8, LANES),
        in_specs=[VMEM, HBM, HBM, VMEM],
        out_specs=VMEM,
        scratch_shapes=[
            pltpu.VMEM((received.shape[1], 2 * rows, LANES), jnp.float32),
            pltpu.VMEM((2 * rows, width), jnp.float32),
            pltpu.SemaphoreType.DMA((2, rows // 8)),
        ],
        cost_estimate=cost(2 * rows * width),
    )(received, own, other, path)


def backward_kernel(blocks, known_blocks, number, scalars, received, solved, *refs):
    matrices, refs = refs[:number], refs[number:]
    known, (send, newest, total, vector, *stream) = refs[: len(known_blocks) - 1], refs[len(known_blocks) - 1 :]
    matrices, copies = begin(matrices, stream)
    newest[...] = jnp.sum(received[...], axis=0)
    total[...] = jnp.zeros_like(total)
    again = solved.shape[2] == LANES and solved.shape[0] == blocks
    if again:
        for block in range(blocks):
            vector[2 * block : 2 * block + 2, :] = solved[block, pl.ds(scalars[2] * 2, 2), :]

    def step(matrix, rows, place):
        if again:
            values = row_dot(matrix, rows, 0, vector, 0, blocks)
        else:
            values = [solved[s, place, 0:1] for s in range(PAIR)]
        column = blocks * LANES
        for ref, count in zip((*known, newest), known_blocks):
            part = row_dot(matrix, rows, column, ref, 0, count)
            values = [values[s] - part[s] for s in range(PAIR)]
            column += count * LANES
        column_dot(matrix, rows, 0, blocks, values, total)

    each_chunk(matrices, copies, step)
    whole = jnp.sum(total[...], axis=1)
    for copy in range(send.shape[0]):
        send[copy] = whole


def backward(received, matrices, solved, known, scalars, blocks, copies):
    rows = matrices[-1].shape[0]
    streamed = len(matrices) > 1
    counts = [array.shape[0] // PAIR for array in known] + [received.shape[1] // PAIR]
    width = (blocks + sum(counts)) * LANES
    return call(
        functools.partial(backward_kernel, blocks, counts, len(matrices)),
        (f32(copies, 2 * blocks, LANES), f32(*received.shape[1:])),
        in_specs=[SMEM, VMEM, VMEM] + ([VMEM, HBM] if streamed else [VMEM]) + [VMEM] * len(known),
        out_specs=(VMEM,) * 2,
        scratch_shapes=[pltpu.VMEM((2 * blocks, 8, LANES), jnp.float32), pltpu.VMEM((2 * blocks, LANES), jnp.float32)]
        + stream_buffers(matrices, width),
        limit=STREAM if streamed else LIMIT,
        cost_estimate=cost(rows * width),
    )(scalars, received, solved, *matrices, *known)


def root_kernel(column, blocks, vector, matrix, send, total):
    total[...] = jnp.zeros_like(total)

    def step(rows):
        values = row_dot(matrix, rows, column, vector, 0, blocks)
        column_dot(matrix, rows, column, blocks, values, total)

    for chunk in range(matrix.shape[0] // CHUNK):
        step(pl.ds(chunk * CHUNK, CHUNK))
    whole = jnp.sum(total[...], axis=1)
    for copy in range(send.shape[0]):
        send[copy] = whole


def root(vector, matrix, column, copies):
    rows = matrix.shape[0]
    blocks = vector.shape[0] // PAIR
    return call(
        functools.partial(root_kernel, column, blocks),
        f32(copies, 2 * blocks, LANES),
        in_specs=[VMEM, VMEM],
        out_specs=VMEM,
        scratch_shapes=[pltpu.VMEM((2 * blocks, 8, LANES), jnp.float32)],
        cost_estimate=cost(rows * blocks * LANES),
    )(vector, matrix)


def sum_kernel(copies, received, send):
    whole = jnp.sum(received[...], axis=0)
    for copy in range(copies):
        send[copy] = whole


def sum_and_copy(received, copies):
    return call(functools.partial(sum_kernel, copies), f32(copies, *received.shape[1:]))(received)


def expand(scalars, terms, index, first_block, path):
    def one(block, carry):
        at = pl.multiple_of(scalars[8 + first_block + block] * LANES, LANES)
        selector = one_hot(index[0:1, pl.ds(at, 2 * LANES)], first_block + block)
        out = lax.dot_general(terms[:, pl.ds(at, 2 * LANES)], selector, NT, preferred_element_type=jnp.float32)
        path[block] = -(out[0:8] + out[8:16] + out[16:24])
        return carry

    lax.fori_loop(0, path.shape[0], one, 0, unroll=4)


def add_own(scalars, both, depth, heights, path):
    z, core, x = scalars[0], scalars[1], scalars[2]
    half = pl.multiple_of(core * 8, 8)
    lane = lax.broadcasted_iota(jnp.int32, (8, LANES), 1)
    start = source = 0
    for height in range(4):
        width = 8 if height < 2 else 16
        for other in range(C):
            if height not in heights:
                continue
            offset = z * width
            block = start
            if height < 3:
                block = block + scalars[3 + height] * (XC * depth * width // LANES)
            if width == 8:
                offset = offset + other * 64
                block = block + x
            else:
                block = block + x * 2 + other
            small = both[other, pl.ds(half, 8), both.shape[2] - LANES :]
            moved = pltpu.roll(small, lax.rem(offset - source + LANES, LANES), 1)
            path[block] = path[block] + jnp.where((lane >= offset) & (lane < offset + width), moved, 0.0)
        start += WIDTHS[height] // LANES if height in heights else 0
        source += width


def product_kernel(values, coupling, rhs0, rhs1, rhs2, rhs3, out):
    columns = coupling.shape[1]
    out[:, :columns] = lax.dot_general(
        values[...], coupling[...], NN, precision=lax.Precision.HIGHEST, preferred_element_type=jnp.float32
    )
    parts = [jnp.transpose(rhs0[...]), jnp.transpose(rhs1[...]), rhs2[...], rhs3[...]]
    filled = sum(part.shape[1] for part in parts)
    parts.append(jnp.zeros((out.shape[0], LANES - filled), jnp.float32))
    out[:, columns:] = jnp.concatenate(parts, axis=1)


def own_product(values, coupling, rhs_parts):
    rhs0, rhs1, rhs2, rhs3 = rhs_parts
    shape = f32(values.shape[0], coupling.shape[1] + LANES)
    return call(product_kernel, shape, in_specs=[VMEM] * 6, out_specs=VMEM, limit=WHOLE)(values, coupling, rhs0.T, rhs1.T, rhs2, rhs3)


def first_kernel(depth, groups, scalars, both, index, *refs):
    count = sum(groups)
    parts, (send, terms, *packs), (path, ready, done, *stages) = refs[:count], refs[count : -3 - len(groups)], refs[-3 - len(groups) :]
    copies = []
    for pack, size in zip(stages, groups):
        column = 0
        for part in parts[:size]:
            width = part.shape[1]
            for row in range(0, part.shape[0], 8):
                target = pack.at[pl.ds(row, 8), pl.ds(column, width)]
                copies.append(pltpu.make_async_copy(part.at[pl.ds(row, 8), :], target, ready.at[len(copies)]))
            column += width
        parts = parts[size:]
    for copy in copies:
        copy.start()
    columns = both.shape[2] - LANES
    half = pl.multiple_of(scalars[1] * 8, 8)
    pieces = split3(both[0, pl.ds(half, 8), :columns] + both[1, pl.ds(half, 8), :columns])
    terms[:, columns:] = jnp.zeros((32, terms.shape[1] - columns), jnp.bfloat16)
    terms[:, :columns] = jnp.concatenate([*pieces, jnp.zeros_like(pieces[0])], axis=0)
    for copy in copies:
        copy.wait()
    copies = []
    for stage, pack in zip(stages, packs):
        for row in range(0, pack.shape[0], 8):
            rows = pl.ds(row, 8)
            copies.append(pltpu.make_async_copy(stage.at[rows, :], pack.at[rows, :], done.at[len(copies)]))
    for copy in copies:
        copy.start()
    expand(scalars, terms, index, sum(WIDTHS[:3]) // LANES, path)
    add_own(scalars, both, depth, (3,), path)
    for dest in range(X):
        for other in range(depth):
            send[dest * depth + other] = path[other]
    for copy in copies:
        copy.wait()


def first(both, index, scalars, depth, groups):
    columns = both.shape[2] - LANES
    parts = [part for group in groups for part in group]
    packs = [f32(group[0].shape[0], sum(part.shape[1] for part in group)) for group in groups]
    count = sum(part.shape[0] // 8 for part in parts)
    outs = call(
        functools.partial(first_kernel, depth, [len(group) for group in groups]),
        (f32(X * depth, 8, LANES), jax.ShapeDtypeStruct((32, columns + 2 * LANES), jnp.bfloat16), *packs),
        in_specs=[SMEM, VMEM, VMEM] + [HBM] * len(parts),
        out_specs=(VMEM, VMEM) + (HBM,) * len(packs),
        scratch_shapes=[
            pltpu.VMEM((WIDTHS[3] // LANES, 8, LANES), jnp.float32),
            pltpu.SemaphoreType.DMA((count,)),
            pltpu.SemaphoreType.DMA((sum(pack.shape[0] // 8 for pack in packs),)),
        ]
        + [pltpu.VMEM(pack.shape, jnp.float32) for pack in packs],
        limit=WHOLE,
    )(scalars, both, index, *parts)
    return outs[0], outs[1], outs[2:]


def upper_kernel(depth, scalars, both, terms, index, path):
    expand(scalars, terms, index, 0, path)
    add_own(scalars, both, depth, (0, 1, 2), path)


def upper_path(both, terms, index, scalars, depth):
    blocks = sum(WIDTHS[:3]) // LANES
    return call(
        functools.partial(upper_kernel, depth),
        f32(blocks, 8, LANES),
        in_specs=[SMEM, VMEM, VMEM, VMEM],
        out_specs=VMEM,
        cost_estimate=cost(blocks * LANES * LANES),
    )(scalars, both, terms, index)


def pick(scalars, index, terms, first_block, blocks, chosen):
    total = sum(WIDTHS) // LANES

    def one(block, carry):
        for half in range(2):
            at = pl.multiple_of(scalars[8 + half * total + first_block + block] * LANES, LANES)
            selector = one_hot(index[half : half + 1, pl.ds(at, 2 * LANES)], first_block + block)
            out = lax.dot_general(
                terms[block].astype(jnp.bfloat16), selector, NN, preferred_element_type=jnp.float32
            )
            chosen[half, :, pl.ds(at, 2 * LANES)] = chosen[half, :, pl.ds(at, 2 * LANES)] + out
        return carry

    lax.fori_loop(0, blocks, one, 0, unroll=4)


def store_terms(ref, terms):
    blocks = ref.shape[0] // PAIR
    pieces = split3(ref[...].reshape(blocks, PAIR, LANES))
    terms[...] = jnp.concatenate([*pieces, jnp.zeros_like(pieces[0])], axis=1).astype(jnp.float32)


def pick_kernel(first_block, scalars, x, index, chosen, terms):
    store_terms(x, terms)
    chosen[...] = jnp.zeros_like(chosen)
    pick(scalars, index, terms, first_block, x.shape[0] // PAIR, chosen)


def picked(x, index, scalars, first_block):
    blocks = x.shape[0] // PAIR
    return call(
        functools.partial(pick_kernel, first_block),
        f32(2, 8, index.shape[1]),
        in_specs=[SMEM, VMEM, VMEM],
        out_specs=VMEM,
        scratch_shapes=[pltpu.VMEM((blocks, 8, LANES), jnp.float32)],
        cost_estimate=cost(blocks * 2 * LANES * LANES),
    )(scalars, x, index)


def last_kernel(columns, counts, scalars, received, x0, x1, x2, coupling, index, chosen0, chosen1, chosen2, send, x3, terms, chosen):
    x3[...] = jnp.sum(received[...], axis=0)
    store_terms(x3, terms)
    chosen[...] = chosen0[...] + chosen1[...] + chosen2[...]
    pick(scalars, index, terms, sum(counts[:3]), counts[3], chosen)
    rows = coupling.shape[0] // 2
    handed = []
    for half in range(2):
        value = chosen[half, 0:2, :columns] + chosen[half, 2:4, :columns] + chosen[half, 4:6, :columns]
        handed.append(
            lax.dot_general(
                value,
                coupling[half * rows : (half + 1) * rows, :],
                NT,
                precision=lax.Precision.HIGHEST,
                preferred_element_type=jnp.float32,
            )
        )
    send[...] = jnp.zeros_like(send)
    for dest in range(XC):
        core, x = dest // X, dest % X
        for level, ref in enumerate((x0, x1, x2, x3)):
            block = x if level < 2 else x * 2 + core
            if level < 3:
                block = block + scalars[level] * (counts[level] // (Y // 2**level))
            send[dest, 2 * level : 2 * level + 2, :] = ref[pl.ds(block * 2, 2), :]
        send[dest, 8:10, :] = handed[x // 2]


def last(received, known, chosen, coupling, index, scalars):
    columns = coupling.shape[1]
    counts = [width // LANES for width in WIDTHS]
    return call(
        functools.partial(last_kernel, columns, counts),
        f32(XC, 16, LANES),
        in_specs=[SMEM] + [VMEM] * 9,
        out_specs=VMEM,
        scratch_shapes=[
            pltpu.VMEM(received.shape[1:], jnp.float32),
            pltpu.VMEM((counts[3], 8, LANES), jnp.float32),
            pltpu.VMEM((2, 8, columns + 2 * LANES), jnp.float32),
        ],
    )(scalars, received, *known, coupling, index, *chosen)


def finish_kernel(scalars, received, values, out0, out1, out2, out3, handed):
    z, core = scalars[0], scalars[1]
    offsets = (core * 64 + z * 8, core * 64 + z * 8, z * 16, z * 16, scalars[2] * values.shape[1])
    for level, ref in enumerate((out0, out1, out2, out3, handed)):
        value = jnp.concatenate([received[source, 2 * level : 2 * level + 2, :] for source in range(XC)], axis=0)
        moved = pltpu.roll(value, lax.rem(LANES - offsets[level], LANES), 1)
        if level < 2:
            ref[...] = jnp.transpose(moved)[: ref.shape[0], :]
        elif level < 4:
            ref[...] = moved[:, : ref.shape[1]]
        else:
            ref[...] = values[...] - moved[:, : ref.shape[1]]


def finish(received, values, scalars, widths):
    samples = XC * PAIR
    shapes = [f32(width, samples) for width in widths[:2]] + [f32(samples, width) for width in widths[2:]]
    outs = call(finish_kernel, (*shapes, f32(*values.shape)), in_specs=[SMEM, VMEM, VMEM])(scalars, received, values)
    return outs[0].T, outs[1].T, *outs[2:]


def body(
    rhs_root,
    rhs_level1,
    rhs_level2,
    rhs_level3,
    inv_root,
    inv_level1,
    inv_level2,
    inv_level3,
    cross_level1,
    cross_level2,
    cross_level3,
    subtree_values,
    coupling,
    coupled_rows,
):
    depth = lax.axis_size("z")
    y = (lax.axis_index("y2") * 2 + lax.axis_index("y1")) * 2 + lax.axis_index("y0")
    x, c, z = lax.axis_index("x"), lax.axis_index("c"), lax.axis_index("z")
    counts = [width // LANES for width in WIDTHS]
    blocks = sum(counts)

    rhs_parts = [rhs_root, rhs_level1, rhs_level2, rhs_level3]
    both = lax.all_gather(own_product(subtree_values, coupling, rhs_parts), "c", axis=0, tiled=False)

    def gathered(whole):
        return lax.all_gather(whole, ("x", "c"), axis=0, tiled=True)

    both_indices = lax.dynamic_slice_in_dim(coupled_rows, y * 2, 2, 0)
    edges = jnp.arange(blocks, dtype=jnp.int32) * LANES
    windows = jnp.sum((both_indices[:, None, :] < edges[None, :, None]).astype(jnp.int32), axis=2) // LANES
    both_indices = jnp.pad(both_indices, ((0, 0), (0, 2 * LANES)), constant_values=-1)
    own_windows = lax.dynamic_index_in_dim(windows, x // 2, 0, keepdims=False)
    own_indices = lax.dynamic_slice_in_dim(both_indices, x // 2, 1, 0)

    def scalars(head, *tails):
        head = jnp.stack([jnp.asarray(value, jnp.int32) for value in head] + [jnp.int32(0)] * (8 - len(head)))
        return jnp.concatenate([head, *tails])

    places = scalars([z, c, x, y, y % 4, y % 2, (y % 2) * depth + z], own_windows)
    groups = ((inv_level3, cross_level3), (inv_level2, cross_level2), (inv_level1, cross_level1, inv_root))
    send, terms, (own3, pack2, pack1) = first(both, own_indices, places, depth, groups)
    matrix2 = gathered(pack2)
    matrix1 = gathered(pack1)
    path = upper_path(both, terms, own_indices, places, depth)
    received, other3, path = lax.optimization_barrier(
        (exchange(send, ("x", "z")), lax.ppermute(own3, "c", [(0, 1), (1, 0)]), path)
    )
    target3 = exchange(sum_and_copy(received, depth), ("z",))
    send = lowest(target3, own3, other3, path, counts[3], sum(counts[:3]), 2 * depth)
    send, own3, coupling = lax.optimization_barrier((send, own3, coupling))
    matrix3 = gathered(own3)
    all_coupling = gathered(coupling)
    received = sum_and_copy(exchange(send, ("y0", "x", "z")), 2 * depth)
    target2, half2 = lax.optimization_barrier((exchange(received, ("y0", "z")), fetched(matrix2, 2)))
    solved2, send, rest = forward(
        target2, (half2, matrix2), received[0], places, counts[2], counts[0] + counts[1], counts[0], 4 * depth, 6
    )
    received, matrix1 = lax.optimization_barrier((exchange(send, ("y1", "y0", "z")), fetched(matrix1)))
    solved1, send, rest = forward(received, (matrix1,), rest, places, counts[1], counts[0], 0, Y, 0)

    def sum_root(copies):
        received = exchange(copies.reshape(Y * depth, -1, LANES), ALL_Y + ("z",))
        return exchange(sum_and_copy(received, depth), ("z",))

    target = sum_root(send).reshape(-1, LANES)
    received = sum_root(root(target, matrix1, WIDTHS[1] + WIDTHS[0], Y)).reshape(1, -1, LANES)
    heads = scalars([y, y % 4, y % 2], windows.reshape(-1))
    send, x0 = backward(received, (matrix1,), solved1, [], places, counts[1], 4 * depth)
    x0, matrix2 = lax.optimization_barrier((x0, matrix2))
    received, chosen0, half2 = lax.optimization_barrier(
        (exchange(send, ("y1", "y0", "z")), picked(x0, both_indices, heads, 0), fetched(matrix2, 2))
    )
    send, x1 = backward(received, (half2, matrix2), solved2, [x0], places, counts[2], 2 * depth)
    received, chosen1, half3 = lax.optimization_barrier(
        (exchange(send, ("y0", "z")), picked(x1, both_indices, heads, counts[0]), fetched(matrix3, 2))
    )
    send, x2 = backward(received, (half3, matrix3), target3, [x0, x1], places, counts[3], depth)
    received, chosen2, all_coupling = lax.optimization_barrier(
        (exchange(send, ("z",)), picked(x2, both_indices, heads, counts[0] + counts[1]), fetched(all_coupling))
    )
    send = last(received, [x0, x1, x2], [chosen0, chosen1, chosen2], all_coupling, both_indices, heads)
    received = exchange(send, ("c", "x"))
    ends = scalars([z, c, (x % 2) * 2 + c])
    return finish(received, subtree_values, ends, [part.shape[1] for part in rhs_parts])


def solution(mesh):
    shape = (2, 2, 2, X, C, mesh.shape["sep"])
    fine = Mesh(mesh.devices.reshape(shape), ("y2", "y1", "y0", "x", "c", "z"))
    every = ("y2", "y1", "y0", "x", "c", "z")
    columns, rows = P(None, every), P(every, None)
    in_specs = (columns,) * 4 + (rows,) * 7 + (columns, rows, P())
    return jax.shard_map(body, mesh=fine, in_specs=in_specs, out_specs=(columns,) * 5, check_vma=False)
```

```python
import functools

import jax
import jax.numpy as jnp
from jax import lax
from jax.experimental import pallas as pl
from jax.experimental.pallas import tpu as pltpu
from jax.sharding import Mesh, PartitionSpec as P

ROOT_ROWS = 4096
LEVEL1_ROWS = 2048
LEVEL2_ROWS = 2048
LEVEL3_ROWS = 1024
WIDTHS = (ROOT_ROWS, LEVEL1_ROWS, LEVEL2_ROWS, LEVEL3_ROWS)
Y, X, C = 8, 4, 2
XC = X * C
PAIR = 2
LANES = 128
CHUNK = 32
HBM = pl.BlockSpec(memory_space=pltpu.HBM)
LIMIT = 16 * 2**20
STREAM = 50 * 2**20
WHOLE = 57 * 2**20
ALL_Y = ("y2", "y1", "y0")
INTERPRET = False
VMEM = pl.BlockSpec(memory_space=pltpu.VMEM)
SMEM = pl.BlockSpec(memory_space=pltpu.SMEM)


def call(kernel, out_shape, **options):
    limit = options.pop("limit", LIMIT)
    return pl.pallas_call(
        kernel,
        out_shape=out_shape,
        compiler_params=pltpu.CompilerParams(vmem_limit_bytes=limit),
        interpret=INTERPRET,
        **options,
    )


def cost(elements):
    return pl.CostEstimate(flops=8 * elements, bytes_accessed=4 * elements, transcendentals=0)


def f32(*shape):
    return jax.ShapeDtypeStruct(shape, jnp.float32)


def exchange(operand, axes):
    flat = operand.reshape(-1, LANES)
    return lax.all_to_all(flat, axes, 0, 0, tiled=True).reshape(operand.shape)


def split3(value):
    high = value.astype(jnp.bfloat16)
    rest = value - high.astype(jnp.float32)
    middle = rest.astype(jnp.bfloat16)
    low = (rest - middle.astype(jnp.float32)).astype(jnp.bfloat16)
    return high, middle, low


def one_hot(index_row, block):
    shape = (LANES, index_row.shape[1])
    rows = lax.broadcasted_iota(jnp.int32, shape, 0) + block * LANES
    return jnp.where(rows == index_row, 1.0, 0.0).astype(jnp.bfloat16)


NT = (((1,), (1,)), ((), ()))
NN = (((1,), (0,)), ((), ()))


def row_dot(matrix, rows, column, vector, first, blocks):
    sums = [[None, None] for _ in range(PAIR)]
    for block in range(blocks):
        tile = matrix[rows, column + block * LANES : column + (block + 1) * LANES]
        for s in range(PAIR):
            at = (first + block) * PAIR + s
            part, old = tile * vector[at : at + 1, :], sums[s][block % 2]
            sums[s][block % 2] = part if old is None else old + part
    return [jnp.sum(value[0] + value[1], axis=1, keepdims=True) for value in sums]


def column_dot(matrix, rows, column, blocks, factors, total):
    wide = [jnp.broadcast_to(value, (CHUNK, LANES)) for value in factors]
    for block in range(blocks):
        tile = matrix[rows, column + block * LANES : column + (block + 1) * LANES]
        for s in range(PAIR):
            part = jnp.sum((tile * wide[s]).reshape(CHUNK // 8, 8, LANES), axis=0)
            at = block * PAIR + s
            total[at] = total[at] + part


def chunk_copies(matrix, buffer, ready):
    copies = []
    for place in range(matrix.shape[0] // 8):
        rows, columns = pl.ds(place * 8, 8), pl.ds(0, buffer.shape[1])
        copies.append(pltpu.make_async_copy(matrix.at[rows, columns], buffer.at[rows, columns], ready.at[place]))
    return copies


def begin(matrices, stream):
    if not stream:
        return matrices, None
    buffer, ready = stream
    copies = chunk_copies(matrices[-1].at[pl.ds(matrices[-1].shape[0] - buffer.shape[0], buffer.shape[0]), :], buffer, ready)
    for copy in copies:
        copy.start()
    return (*matrices[:-1], buffer), copies


def each_chunk(matrices, copies, step):
    share = CHUNK // 8
    base = 0
    for matrix in matrices:
        streamed = copies and matrix is matrices[-1]
        for chunk in range(matrix.shape[0] // CHUNK):
            if streamed:
                for copy in copies[chunk * share : (chunk + 1) * share]:
                    copy.wait()
            step(matrix, pl.ds(chunk * CHUNK, CHUNK), pl.ds(base + chunk * CHUNK, CHUNK))
        base += matrix.shape[0]


def stream_buffers(matrices, width):
    if len(matrices) == 1:
        return []
    rows = matrices[1].shape[0] - matrices[0].shape[0]
    return [pltpu.VMEM((rows, width), jnp.float32), pltpu.SemaphoreType.DMA((rows // 8,))]


def fetch_kernel(matrix, out, ready):
    copies = chunk_copies(matrix.at[pl.ds(0, out.shape[0]), :], out, ready)
    for copy in copies:
        copy.start()
    for copy in copies:
        copy.wait()


def fetched(matrix, part=1.0):
    rows, width = int(matrix.shape[0] * part), matrix.shape[1]
    return call(
        fetch_kernel,
        f32(rows, width),
        in_specs=[HBM],
        out_specs=VMEM,
        scratch_shapes=[pltpu.SemaphoreType.DMA((rows // 8,))],
        cost_estimate=cost(2 * rows * width),
    )(matrix)


def forward_kernel(blocks, upper, keep, extra, count, scalars, received, rest_in, *refs):
    matrices, (solved, send, rest, vector, total, *stream) = refs[:count], refs[count:]
    matrices, copies = begin(matrices, stream)
    if extra:
        for source in range(blocks):
            vector[2 * source : 2 * source + 2, :] = received[source, 0:2, :]
    else:
        vector[...] = jnp.sum(received[...], axis=0)
    total[...] = jnp.zeros_like(total)

    def step(matrix, rows, place):
        values = row_dot(matrix, rows, 0, vector, 0, blocks)
        for s in range(PAIR):
            solved[s, place, :] = jnp.broadcast_to(values[s], (CHUNK, LANES))
        column_dot(matrix, rows, blocks * LANES, upper, values, total)

    each_chunk(matrices, copies, step)
    whole = -jnp.sum(total[...], axis=1)
    if extra:
        rest[...] = whole
        for row in range(extra):
            at = pl.ds(scalars[6] * extra + row, 1)
            rest[at, :] = rest[at, :] + rest_in[2 + row : 3 + row, :]
        whole = rest[...]
    else:
        whole = whole + rest_in[0 : 2 * upper, :]
        rest[...] = whole
    for copy in range(send.shape[0]):
        send[copy] = whole[2 * keep :, :]


def forward(received, matrices, rest_in, scalars, blocks, upper, keep, copies, extra):
    rows = matrices[-1].shape[0]
    streamed = len(matrices) > 1
    width = upper * LANES + blocks * LANES
    return call(
        functools.partial(forward_kernel, blocks, upper, keep, extra, len(matrices)),
        (f32(PAIR, rows, LANES), f32(copies, 2 * (upper - keep), LANES), f32(2 * upper, LANES)),
        in_specs=[SMEM, VMEM, VMEM] + ([VMEM, HBM] if streamed else [VMEM]),
        out_specs=(VMEM,) * 3,
        scratch_shapes=[pltpu.VMEM((2 * blocks, LANES), jnp.float32), pltpu.VMEM((2 * upper, 8, LANES), jnp.float32)]
        + stream_buffers(matrices, width),
        limit=STREAM if streamed else LIMIT,
        cost_estimate=cost(rows * width),
    )(scalars, received, rest_in, *matrices)


def lowest_kernel(blocks, upper, received, own, other, path, send, total, buffer, ready):
    rows = own.shape[0]
    copies = chunk_copies(own, buffer.at[0:rows, :], ready.at[0]) + chunk_copies(other, buffer.at[rows:, :], ready.at[1])
    for copy in copies:
        copy.start()
    for copy in copies:
        copy.wait()
    samples = range(received.shape[1])
    sums = [jnp.zeros((2 * rows, LANES), jnp.float32) for _ in samples]
    for block in range(blocks):
        tile = buffer[:, block * LANES : (block + 1) * LANES]
        for s in samples:
            sums[s] = sums[s] + tile * received[block, s : s + 1, :]
    wide = [jnp.broadcast_to(jnp.sum(value, axis=1, keepdims=True), (2 * rows, LANES)) for value in sums]
    for s in samples:
        total[s] = wide[s]

    def one(block, carry):
        at = pl.multiple_of((blocks + block) * LANES, LANES)
        tile = buffer[:, pl.ds(at, LANES)]
        parts = [jnp.sum(tile * total[s], axis=0, keepdims=True) for s in samples]
        path_block = path[block] - jnp.concatenate(parts, axis=0)
        send_block(block, path_block)
        return carry

    groups = send.shape[0] // X
    share = (upper - groups) // groups

    def send_block(block, value):
        low = block >= upper - groups
        place = jnp.where(low, block - (upper - groups), block // share)
        row = jnp.where(low, 0, 2 + 2 * lax.rem(block, share))
        depth = groups // 2
        for x in range(X):
            dest = (place // depth) * (X * depth) + x * depth + lax.rem(place, depth)
            send[dest, pl.ds(row, 2), :] = value[2 * x : 2 * x + 2, :]

    lax.fori_loop(0, upper, one, 0, unroll=4)


def lowest(received, own, other, path, blocks, upper, groups):
    rows, width = own.shape
    return call(
        functools.partial(lowest_kernel, blocks, upper),
        f32(X * groups, 8, LANES),
        in_specs=[VMEM, HBM, HBM, VMEM],
        out_specs=VMEM,
        scratch_shapes=[
            pltpu.VMEM((received.shape[1], 2 * rows, LANES), jnp.float32),
            pltpu.VMEM((2 * rows, width), jnp.float32),
            pltpu.SemaphoreType.DMA((2, rows // 8)),
        ],
        cost_estimate=cost(2 * rows * width),
    )(received, own, other, path)


def backward_kernel(blocks, known_blocks, number, scalars, received, solved, *refs):
    matrices, refs = refs[:number], refs[number:]
    known, (send, newest, total, vector, *stream) = refs[: len(known_blocks) - 1], refs[len(known_blocks) - 1 :]
    matrices, copies = begin(matrices, stream)
    newest[...] = jnp.sum(received[...], axis=0)
    total[...] = jnp.zeros_like(total)
    again = solved.shape[2] == LANES and solved.shape[0] == blocks
    if again:
        for block in range(blocks):
            vector[2 * block : 2 * block + 2, :] = solved[block, pl.ds(scalars[2] * 2, 2), :]

    def step(matrix, rows, place):
        if again:
            values = row_dot(matrix, rows, 0, vector, 0, blocks)
        else:
            values = [solved[s, place, 0:1] for s in range(PAIR)]
        column = blocks * LANES
        for ref, count in zip((*known, newest), known_blocks):
            part = row_dot(matrix, rows, column, ref, 0, count)
            values = [values[s] - part[s] for s in range(PAIR)]
            column += count * LANES
        column_dot(matrix, rows, 0, blocks, values, total)

    each_chunk(matrices, copies, step)
    whole = jnp.sum(total[...], axis=1)
    for copy in range(send.shape[0]):
        send[copy] = whole


def backward(received, matrices, solved, known, scalars, blocks, copies):
    rows = matrices[-1].shape[0]
    streamed = len(matrices) > 1
    counts = [array.shape[0] // PAIR for array in known] + [received.shape[1] // PAIR]
    width = (blocks + sum(counts)) * LANES
    return call(
        functools.partial(backward_kernel, blocks, counts, len(matrices)),
        (f32(copies, 2 * blocks, LANES), f32(*received.shape[1:])),
        in_specs=[SMEM, VMEM, VMEM] + ([VMEM, HBM] if streamed else [VMEM]) + [VMEM] * len(known),
        out_specs=(VMEM,) * 2,
        scratch_shapes=[pltpu.VMEM((2 * blocks, 8, LANES), jnp.float32), pltpu.VMEM((2 * blocks, LANES), jnp.float32)]
        + stream_buffers(matrices, width),
        limit=STREAM if streamed else LIMIT,
        cost_estimate=cost(rows * width),
    )(scalars, received, solved, *matrices, *known)


def root_kernel(column, blocks, vector, matrix, send, total):
    total[...] = jnp.zeros_like(total)

    def step(rows):
        values = row_dot(matrix, rows, column, vector, 0, blocks)
        column_dot(matrix, rows, column, blocks, values, total)

    for chunk in range(matrix.shape[0] // CHUNK):
        step(pl.ds(chunk * CHUNK, CHUNK))
    whole = jnp.sum(total[...], axis=1)
    for copy in range(send.shape[0]):
        send[copy] = whole


def root(vector, matrix, column, copies):
    rows = matrix.shape[0]
    blocks = vector.shape[0] // PAIR
    return call(
        functools.partial(root_kernel, column, blocks),
        f32(copies, 2 * blocks, LANES),
        in_specs=[VMEM, VMEM],
        out_specs=VMEM,
        scratch_shapes=[pltpu.VMEM((2 * blocks, 8, LANES), jnp.float32)],
        cost_estimate=cost(rows * blocks * LANES),
    )(vector, matrix)


def sum_kernel(copies, received, send):
    whole = jnp.sum(received[...], axis=0)
    for copy in range(copies):
        send[copy] = whole


def sum_and_copy(received, copies):
    return call(functools.partial(sum_kernel, copies), f32(copies, *received.shape[1:]))(received)


def expand(scalars, windows, terms, index, first_block, path):
    def one(block, carry):
        at = pl.multiple_of(windows[scalars[2] // 2, first_block + block] * LANES, LANES)
        selector = one_hot(index[pl.ds(scalars[7] * 2 + scalars[2] // 2, 1), pl.ds(at, 2 * LANES)], first_block + block)
        out = lax.dot_general(terms[:, pl.ds(at, 2 * LANES)], selector, NT, preferred_element_type=jnp.float32)
        path[block] = -(out[0:8] + out[8:16] + out[16:24])
        return carry

    lax.fori_loop(0, path.shape[0], one, 0, unroll=4)


def add_own(scalars, both, depth, heights, path):
    z, core, x = scalars[0], scalars[1], scalars[2]
    half = pl.multiple_of(core * 8, 8)
    lane = lax.broadcasted_iota(jnp.int32, (8, LANES), 1)
    start = source = 0
    for height in range(4):
        width = 8 if height < 2 else 16
        for other in range(C):
            if height not in heights:
                continue
            offset = z * width
            block = start
            if height < 3:
                block = block + scalars[3 + height] * (XC * depth * width // LANES)
            if width == 8:
                offset = offset + other * 64
                block = block + x
            else:
                block = block + x * 2 + other
            small = both[other, pl.ds(half, 8), both.shape[2] - LANES :]
            moved = pltpu.roll(small, lax.rem(offset - source + LANES, LANES), 1)
            path[block] = path[block] + jnp.where((lane >= offset) & (lane < offset + width), moved, 0.0)
        start += WIDTHS[height] // LANES if height in heights else 0
        source += width


def product_kernel(values, coupling, rhs0, rhs1, rhs2, rhs3, out):
    columns = coupling.shape[1]
    out[:, :columns] = lax.dot_general(
        values[...], coupling[...], NN, precision=lax.Precision.HIGHEST, preferred_element_type=jnp.float32
    )
    parts = [jnp.transpose(rhs0[...]), jnp.transpose(rhs1[...]), rhs2[...], rhs3[...]]
    filled = sum(part.shape[1] for part in parts)
    parts.append(jnp.zeros((out.shape[0], LANES - filled), jnp.float32))
    out[:, columns:] = jnp.concatenate(parts, axis=1)


def own_product(values, coupling, rhs_parts):
    rhs0, rhs1, rhs2, rhs3 = rhs_parts
    shape = f32(values.shape[0], coupling.shape[1] + LANES)
    return call(product_kernel, shape, in_specs=[VMEM] * 6, out_specs=VMEM, limit=WHOLE)(values, coupling, rhs0.T, rhs1.T, rhs2, rhs3)


def stage_in(parts, stages, groups, ready):
    copies = []
    for stage, size in zip(stages, groups):
        column = 0
        for part in parts[:size]:
            width = part.shape[1]
            for row in range(0, part.shape[0], 8):
                rows = pl.ds(row, 8)
                copies.append(
                    pltpu.make_async_copy(part.at[rows, :], stage.at[rows, pl.ds(column, width)], ready.at[len(copies)])
                )
            column += width
        parts = parts[size:]
    for copy in copies:
        copy.start()
    return copies


def stage_out(copies, stages, packs, done):
    for copy in copies:
        copy.wait()
    copies = []
    for stage, pack in zip(stages, packs):
        for row in range(0, pack.shape[0], 8):
            rows = pl.ds(row, 8)
            copies.append(pltpu.make_async_copy(stage.at[rows, :], pack.at[rows, :], done.at[len(copies)]))
    for copy in copies:
        copy.start()
    return copies


def pack_shapes(groups):
    parts = [part for group in groups for part in group]
    packs = [f32(group[0].shape[0], sum(part.shape[1] for part in group)) for group in groups]
    scratch = [
        pltpu.SemaphoreType.DMA((sum(part.shape[0] // 8 for part in parts),)),
        pltpu.SemaphoreType.DMA((sum(pack.shape[0] // 8 for pack in packs),)),
    ]
    return parts, packs, scratch + [pltpu.VMEM(pack.shape, jnp.float32) for pack in packs]


def first_kernel(depth, groups, scalars, windows, both, index, *refs):
    count, number = sum(groups), len(groups)
    parts, (send, terms, *packs), (path, ready, done, *stages) = refs[:count], refs[count : -3 - number], refs[-3 - number :]
    copies = stage_in(parts, stages, groups, ready)
    columns = both.shape[2] - LANES
    half = pl.multiple_of(scalars[1] * 8, 8)
    pieces = split3(both[0, pl.ds(half, 8), :columns] + both[1, pl.ds(half, 8), :columns])
    terms[...] = jnp.concatenate([*pieces, jnp.zeros_like(pieces[0])], axis=0)
    expand(scalars, windows, terms, index, sum(WIDTHS[:3]) // LANES, path)
    copies = stage_out(copies, stages, packs, done)
    add_own(scalars, both, depth, (3,), path)
    for dest in range(X):
        for other in range(depth):
            send[dest * depth + other] = path[other]
    for copy in copies:
        copy.wait()


def first(both, index, scalars, windows, depth, groups):
    columns = both.shape[2] - LANES
    parts, packs, scratch = pack_shapes(groups)
    outs = call(
        functools.partial(first_kernel, depth, [len(group) for group in groups]),
        (f32(X * depth, 8, LANES), jax.ShapeDtypeStruct((32, columns), jnp.bfloat16), *packs),
        in_specs=[SMEM, SMEM, VMEM, VMEM] + [HBM] * len(parts),
        out_specs=(VMEM, VMEM) + (HBM,) * len(packs),
        scratch_shapes=[pltpu.VMEM((WIDTHS[3] // LANES, 8, LANES), jnp.float32)] + scratch,
        limit=WHOLE,
    )(scalars, windows, both, index, *parts)
    return outs[0], outs[1], outs[2:]


def upper_kernel(depth, groups, scalars, windows, both, terms, index, *refs):
    count, number = sum(groups), len(groups)
    parts, (path, *packs), (ready, done, *stages) = refs[:count], refs[count : -2 - number], refs[-2 - number :]
    copies = stage_out(stage_in(parts, stages, groups, ready), stages, packs, done)
    expand(scalars, windows, terms, index, 0, path)
    add_own(scalars, both, depth, (0, 1, 2), path)
    for copy in copies:
        copy.wait()


def upper_path(both, terms, index, scalars, windows, depth, groups):
    blocks = sum(WIDTHS[:3]) // LANES
    parts, packs, scratch = pack_shapes(groups)
    outs = call(
        functools.partial(upper_kernel, depth, [len(group) for group in groups]),
        (f32(blocks, 8, LANES), *packs),
        in_specs=[SMEM, SMEM, VMEM, VMEM, VMEM] + [HBM] * len(parts),
        out_specs=(VMEM,) + (HBM,) * len(packs),
        scratch_shapes=scratch,
        cost_estimate=cost(blocks * LANES * LANES),
        limit=STREAM,
    )(scalars, windows, both, terms, index, *parts)
    return outs[0], outs[1:]


def pick(scalars, windows, index, terms, first_block, blocks, chosen):
    def one(block, carry):
        for half in range(2):
            at = pl.multiple_of(windows[half, first_block + block] * LANES, LANES)
            selector = one_hot(index[pl.ds(scalars[7] * 2 + half, 1), pl.ds(at, 2 * LANES)], first_block + block)
            out = lax.dot_general(
                terms[block].astype(jnp.bfloat16), selector, NN, preferred_element_type=jnp.float32
            )
            chosen[half, :, pl.ds(at, 2 * LANES)] = chosen[half, :, pl.ds(at, 2 * LANES)] + out
        return carry

    lax.fori_loop(0, blocks, one, 0, unroll=4)


def store_terms(ref, terms):
    blocks = ref.shape[0] // PAIR
    pieces = split3(ref[...].reshape(blocks, PAIR, LANES))
    terms[...] = jnp.concatenate([*pieces, jnp.zeros_like(pieces[0])], axis=1).astype(jnp.float32)


def pick_kernel(first_block, scalars, windows, x, index, chosen, terms):
    store_terms(x, terms)
    chosen[...] = jnp.zeros_like(chosen)
    pick(scalars, windows, index, terms, first_block, x.shape[0] // PAIR, chosen)


def picked(x, index, scalars, windows, first_block):
    blocks = x.shape[0] // PAIR
    return call(
        functools.partial(pick_kernel, first_block),
        f32(2, 8, index.shape[1]),
        in_specs=[SMEM, SMEM, VMEM, VMEM],
        out_specs=VMEM,
        scratch_shapes=[pltpu.VMEM((blocks, 8, LANES), jnp.float32)],
        cost_estimate=cost(blocks * 2 * LANES * LANES),
    )(scalars, windows, x, index)


def last_kernel(counts, scalars, windows, received, x0, x1, x2, coupling, index, chosen0, chosen1, chosen2, send, x3, terms, chosen):
    x3[...] = jnp.sum(received[...], axis=0)
    store_terms(x3, terms)
    chosen[...] = chosen0[...] + chosen1[...] + chosen2[...]
    pick(scalars, windows, index, terms, sum(counts[:3]), counts[3], chosen)
    rows, columns = coupling.shape[0] // 2, coupling.shape[1]
    lane = lax.broadcasted_iota(jnp.int32, (CHUNK, LANES), 1)
    handed = []
    for half in range(2):
        chosen[half, 0:2, :] = chosen[half, 0:2, :] + chosen[half, 2:4, :] + chosen[half, 4:6, :]
        columns_of = []
        for chunk in range(rows // CHUNK):
            at = half * rows + chunk * CHUNK
            sums = [[None, None] for _ in range(PAIR)]
            for block in range(columns // LANES):
                place = slice(block * LANES, (block + 1) * LANES)
                tile = coupling[at : at + CHUNK, place]
                for s in range(PAIR):
                    part, old = tile * chosen[half, s : s + 1, place], sums[s][block % 2]
                    sums[s][block % 2] = part if old is None else old + part
            totals = [jnp.sum(value[0] + value[1], axis=1, keepdims=True) for value in sums]
            columns_of.append(jnp.where(lane == 0, totals[0], jnp.where(lane == 1, totals[1], 0.0)))
        handed.append(jnp.transpose(jnp.concatenate(columns_of, axis=0))[0:PAIR, :])
    send[...] = jnp.zeros_like(send)
    for dest in range(XC):
        core, x = dest // X, dest % X
        for level, ref in enumerate((x0, x1, x2, x3)):
            block = x if level < 2 else x * 2 + core
            if level < 3:
                block = block + scalars[3 + level] * (counts[level] // (Y // 2**level))
            send[dest, 2 * level : 2 * level + 2, :] = ref[pl.ds(block * 2, 2), :]
        send[dest, 8:10, :] = handed[x // 2]


def last(received, known, chosen, coupling, index, scalars, windows):
    counts = [width // LANES for width in WIDTHS]
    return call(
        functools.partial(last_kernel, counts),
        f32(XC, 16, LANES),
        in_specs=[SMEM, SMEM] + [VMEM] * 9,
        out_specs=VMEM,
        scratch_shapes=[
            pltpu.VMEM(received.shape[1:], jnp.float32),
            pltpu.VMEM((counts[3], 8, LANES), jnp.float32),
            pltpu.VMEM((2, 8, coupling.shape[1]), jnp.float32),
        ],
    )(scalars, windows, received, *known, coupling, index, *chosen)


def finish_kernel(scalars, received, values, out0, out1, out2, out3, handed):
    z, core = scalars[0], scalars[1]
    offsets = (core * 64 + z * 8, core * 64 + z * 8, z * 16, z * 16, (lax.rem(scalars[2], 2) * 2 + core) * values.shape[1])
    for level, ref in enumerate((out0, out1, out2, out3, handed)):
        value = jnp.concatenate([received[source, 2 * level : 2 * level + 2, :] for source in range(XC)], axis=0)
        moved = pltpu.roll(value, lax.rem(LANES - offsets[level], LANES), 1)
        if level < 2:
            ref[...] = jnp.transpose(moved)[: ref.shape[0], :]
        elif level < 4:
            ref[...] = moved[:, : ref.shape[1]]
        else:
            ref[...] = values[...] - moved[:, : ref.shape[1]]


def finish(received, values, scalars, widths):
    samples = XC * PAIR
    shapes = [f32(width, samples) for width in widths[:2]] + [f32(samples, width) for width in widths[2:]]
    outs = call(finish_kernel, (*shapes, f32(*values.shape)), in_specs=[SMEM, VMEM, VMEM])(scalars, received, values)
    return outs[0].T, outs[1].T, *outs[2:]


def body(
    rhs_root,
    rhs_level1,
    rhs_level2,
    rhs_level3,
    inv_root,
    inv_level1,
    inv_level2,
    inv_level3,
    cross_level1,
    cross_level2,
    cross_level3,
    subtree_values,
    coupling,
    coupled_rows,
):
    depth = lax.axis_size("z")
    y = (lax.axis_index("y2") * 2 + lax.axis_index("y1")) * 2 + lax.axis_index("y0")
    x, c, z = lax.axis_index("x"), lax.axis_index("c"), lax.axis_index("z")
    counts = [width // LANES for width in WIDTHS]
    blocks = sum(counts)

    rhs_parts = [rhs_root, rhs_level1, rhs_level2, rhs_level3]
    both = lax.all_gather(own_product(subtree_values, coupling, rhs_parts), "c", axis=0, tiled=False)

    def gathered(whole):
        return lax.all_gather(whole, ("x", "c"), axis=0, tiled=True)

    both, coupled_rows = lax.optimization_barrier((both, coupled_rows))
    edges = jnp.arange(blocks, dtype=jnp.int32) * LANES
    both_indices = lax.dynamic_slice_in_dim(coupled_rows, y * 2, 2, 0)
    windows = jnp.sum((both_indices[:, None, :] < edges[None, :, None]).astype(jnp.int32), axis=2) // LANES
    windows = jnp.minimum(windows, coupled_rows.shape[1] // LANES - 2)

    places = jnp.stack([z, c, x, y, y % 4, y % 2, (y % 2) * depth + z, y])
    send, terms, (pack2,) = first(both, coupled_rows, places, windows, depth, ((inv_level2, cross_level2),))
    matrix2 = gathered(pack2)
    groups = ((inv_level3, cross_level3), (inv_level1, cross_level1, inv_root))
    path, (own3, pack1) = upper_path(both, terms, coupled_rows, places, windows, depth, groups)
    received, path, own3, pack1 = lax.optimization_barrier((exchange(send, ("x", "z")), path, own3, pack1))
    other3 = lax.ppermute(own3, "c", [(0, 1), (1, 0)])
    matrix1 = gathered(pack1)
    target3 = exchange(sum_and_copy(received, depth), ("z",))
    send = lowest(target3, own3, other3, path, counts[3], sum(counts[:3]), 2 * depth)
    send, own3, coupling = lax.optimization_barrier((send, own3, coupling))
    matrix3 = gathered(own3)
    all_coupling = gathered(coupling)
    received = sum_and_copy(exchange(send, ("y0", "x", "z")), 2 * depth)
    target2, half2 = lax.optimization_barrier((exchange(received, ("y0", "z")), fetched(matrix2, 0.5)))
    solved2, send, rest = forward(
        target2, (half2, matrix2), received[0], places, counts[2], counts[0] + counts[1], counts[0], 4 * depth, 6
    )
    received, matrix1 = lax.optimization_barrier((exchange(send, ("y1", "y0", "z")), fetched(matrix1)))
    solved1, send, rest = forward(received, (matrix1,), rest, places, counts[1], counts[0], 0, Y, 0)

    def sum_root(copies):
        received = exchange(copies.reshape(Y * depth, -1, LANES), ALL_Y + ("z",))
        return exchange(sum_and_copy(received, depth), ("z",))

    target = sum_root(send).reshape(-1, LANES)
    received = sum_root(root(target, matrix1, WIDTHS[1] + WIDTHS[0], Y)).reshape(1, -1, LANES)
    send, x0 = backward(received, (matrix1,), solved1, [], places, counts[1], 4 * depth)
    x0, matrix2 = lax.optimization_barrier((x0, matrix2))
    received, chosen0, half2 = lax.optimization_barrier(
        (exchange(send, ("y1", "y0", "z")), picked(x0, coupled_rows, places, windows, 0), fetched(matrix2, 0.5))
    )
    send, x1 = backward(received, (half2, matrix2), solved2, [x0], places, counts[2], 2 * depth)
    received, chosen1, half3 = lax.optimization_barrier(
        (exchange(send, ("y0", "z")), picked(x1, coupled_rows, places, windows, counts[0]), fetched(matrix3, 0.5))
    )
    send, x2 = backward(received, (half3, matrix3), target3, [x0, x1], places, counts[3], depth)
    received, chosen2, all_coupling = lax.optimization_barrier(
        (exchange(send, ("z",)), picked(x2, coupled_rows, places, windows, counts[0] + counts[1]), fetched(all_coupling))
    )
    send = last(received, [x0, x1, x2], [chosen0, chosen1, chosen2], all_coupling, coupled_rows, places, windows)
    received = exchange(send, ("c", "x"))
    return finish(received, subtree_values, places, [part.shape[1] for part in rhs_parts])


def solution(mesh):
    shape = (2, 2, 2, X, C, mesh.shape["sep"])
    fine = Mesh(mesh.devices.reshape(shape), ("y2", "y1", "y0", "x", "c", "z"))
    every = ("y2", "y1", "y0", "x", "c", "z")
    columns, rows = P(None, every), P(every, None)
    in_specs = (columns,) * 4 + (rows,) * 7 + (columns, rows, P())
    return jax.shard_map(body, mesh=fine, in_specs=in_specs, out_specs=(columns,) * 5, check_vma=False)
```

```python
import functools

import jax
import jax.numpy as jnp
from jax import lax
from jax.experimental import pallas as pl
from jax.experimental.pallas import tpu as pltpu
from jax.sharding import Mesh, PartitionSpec as P

ROOT_ROWS = 4096
LEVEL1_ROWS = 2048
LEVEL2_ROWS = 2048
LEVEL3_ROWS = 1024
WIDTHS = (ROOT_ROWS, LEVEL1_ROWS, LEVEL2_ROWS, LEVEL3_ROWS)
Y, X, C = 8, 4, 2
XC = X * C
PAIR = 2
LANES = 128
CHUNK = 32
HBM = pl.BlockSpec(memory_space=pltpu.HBM)
LIMIT = 16 * 2**20
STREAM = 50 * 2**20
WHOLE = 57 * 2**20
ALL_Y = ("y2", "y1", "y0")
INTERPRET = False
VMEM = pl.BlockSpec(memory_space=pltpu.VMEM)
SMEM = pl.BlockSpec(memory_space=pltpu.SMEM)


def call(kernel, out_shape, **options):
    limit = options.pop("limit", LIMIT)
    return pl.pallas_call(
        kernel,
        out_shape=out_shape,
        compiler_params=pltpu.CompilerParams(vmem_limit_bytes=limit),
        interpret=INTERPRET,
        **options,
    )


def cost(elements):
    return pl.CostEstimate(flops=8 * elements, bytes_accessed=4 * elements, transcendentals=0)


def position(name):
    if name == "y":
        return (lax.axis_index("y2") * 2 + lax.axis_index("y1")) * 2 + lax.axis_index("y0")
    if name == "y1":
        return lax.axis_index("y1") * 2 + lax.axis_index("y0")
    return lax.axis_index(name)


def own_subtree():
    return position("y") * 2 + position("x") // 2


def window(counts, subtree, block, columns):
    return pl.multiple_of(jnp.minimum(counts[subtree, block] // LANES, columns // LANES - 2) * LANES, LANES)


def f32(*shape):
    return jax.ShapeDtypeStruct(shape, jnp.float32)


def exchange(operand, axes):
    flat = operand.reshape(-1, LANES)
    return lax.all_to_all(flat, axes, 0, 0, tiled=True).reshape(operand.shape)


def split3(value):
    high = value.astype(jnp.bfloat16)
    rest = value - high.astype(jnp.float32)
    middle = rest.astype(jnp.bfloat16)
    low = (rest - middle.astype(jnp.float32)).astype(jnp.bfloat16)
    return high, middle, low


def one_hot(index_row, block):
    shape = (LANES, index_row.shape[1])
    rows = lax.broadcasted_iota(jnp.int32, shape, 0) + block * LANES
    return jnp.where(rows == index_row, 1.0, 0.0).astype(jnp.bfloat16)


NT = (((1,), (1,)), ((), ()))
NN = (((1,), (0,)), ((), ()))


def row_dot(matrix, rows, column, vector, first, blocks):
    sums = [[None, None] for _ in range(PAIR)]
    for block in range(blocks):
        tile = matrix[rows, column + block * LANES : column + (block + 1) * LANES]
        for s in range(PAIR):
            at = (first + block) * PAIR + s
            part, old = tile * vector[at : at + 1, :], sums[s][block % 2]
            sums[s][block % 2] = part if old is None else old + part
    return [jnp.sum(value[0] + value[1], axis=1, keepdims=True) for value in sums]


def column_dot(matrix, rows, column, blocks, factors, total):
    wide = [jnp.broadcast_to(value, (CHUNK, LANES)) for value in factors]
    for block in range(blocks):
        tile = matrix[rows, column + block * LANES : column + (block + 1) * LANES]
        for s in range(PAIR):
            part = jnp.sum((tile * wide[s]).reshape(CHUNK // 8, 8, LANES), axis=0)
            at = block * PAIR + s
            total[at] = total[at] + part


def chunk_copies(matrix, buffer, ready):
    copies = []
    for place in range(matrix.shape[0] // 8):
        rows, columns = pl.ds(place * 8, 8), pl.ds(0, buffer.shape[1])
        copies.append(pltpu.make_async_copy(matrix.at[rows, columns], buffer.at[rows, columns], ready.at[place]))
    return copies


def begin(matrices, stream):
    if not stream:
        return matrices, None
    buffer, ready = stream
    copies = chunk_copies(matrices[-1].at[pl.ds(matrices[-1].shape[0] - buffer.shape[0], buffer.shape[0]), :], buffer, ready)
    for copy in copies:
        copy.start()
    return (*matrices[:-1], buffer), copies


def each_chunk(matrices, copies, step):
    share = CHUNK // 8
    base = 0
    for matrix in matrices:
        streamed = copies and matrix is matrices[-1]
        for chunk in range(matrix.shape[0] // CHUNK):
            if streamed:
                for copy in copies[chunk * share : (chunk + 1) * share]:
                    copy.wait()
            step(matrix, pl.ds(chunk * CHUNK, CHUNK), pl.ds(base + chunk * CHUNK, CHUNK))
        base += matrix.shape[0]


def stream_buffers(matrices, width):
    if len(matrices) == 1:
        return []
    rows = matrices[1].shape[0] - matrices[0].shape[0]
    return [pltpu.VMEM((rows, width), jnp.float32), pltpu.SemaphoreType.DMA((rows // 8,))]


def fetch_kernel(matrix, out, ready):
    copies = chunk_copies(matrix.at[pl.ds(0, out.shape[0]), :], out, ready)
    for copy in copies:
        copy.start()
    for copy in copies:
        copy.wait()


def fetched(matrix, part=1.0):
    rows, width = int(matrix.shape[0] * part), matrix.shape[1]
    return call(
        fetch_kernel,
        f32(rows, width),
        in_specs=[HBM],
        out_specs=VMEM,
        scratch_shapes=[pltpu.SemaphoreType.DMA((rows // 8,))],
        cost_estimate=cost(2 * rows * width),
    )(matrix)


def forward_kernel(blocks, upper, keep, extra, count, received, rest_in, *refs):
    matrices, (solved, send, rest, vector, total, *stream) = refs[:count], refs[count:]
    matrices, copies = begin(matrices, stream)
    if extra:
        for source in range(blocks):
            vector[2 * source : 2 * source + 2, :] = received[source, 0:2, :]
    else:
        vector[...] = jnp.sum(received[...], axis=0)
    total[...] = jnp.zeros_like(total)

    def step(matrix, rows, place):
        values = row_dot(matrix, rows, 0, vector, 0, blocks)
        for s in range(PAIR):
            solved[s, place, :] = jnp.broadcast_to(values[s], (CHUNK, LANES))
        column_dot(matrix, rows, blocks * LANES, upper, values, total)

    each_chunk(matrices, copies, step)
    whole = -jnp.sum(total[...], axis=1)
    if extra:
        rest[...] = whole
        place = position("y0") * (blocks // 2) + position("z")
        for row in range(extra):
            at = pl.ds(place * extra + row, 1)
            rest[at, :] = rest[at, :] + rest_in[2 + row : 3 + row, :]
        whole = rest[...]
    else:
        whole = whole + rest_in[0 : 2 * upper, :]
        rest[...] = whole
    for copy in range(send.shape[0]):
        send[copy] = whole[2 * keep :, :]


def forward(received, matrices, rest_in, blocks, upper, keep, copies, extra):
    rows = matrices[-1].shape[0]
    streamed = len(matrices) > 1
    width = upper * LANES + blocks * LANES
    return call(
        functools.partial(forward_kernel, blocks, upper, keep, extra, len(matrices)),
        (f32(PAIR, rows, LANES), f32(copies, 2 * (upper - keep), LANES), f32(2 * upper, LANES)),
        in_specs=[VMEM, VMEM] + ([VMEM, HBM] if streamed else [VMEM]),
        out_specs=(VMEM,) * 3,
        scratch_shapes=[pltpu.VMEM((2 * blocks, LANES), jnp.float32), pltpu.VMEM((2 * upper, 8, LANES), jnp.float32)]
        + stream_buffers(matrices, width),
        limit=STREAM if streamed else LIMIT,
        cost_estimate=cost(rows * width),
    )(received, rest_in, *matrices)


def lowest_kernel(blocks, upper, received, own, other, path, send, total, buffer, ready):
    rows = own.shape[0]
    copies = chunk_copies(own, buffer.at[0:rows, :], ready.at[0]) + chunk_copies(other, buffer.at[rows:, :], ready.at[1])
    for copy in copies:
        copy.start()
    for copy in copies:
        copy.wait()
    samples = range(received.shape[1])
    sums = [jnp.zeros((2 * rows, LANES), jnp.float32) for _ in samples]
    for block in range(blocks):
        tile = buffer[:, block * LANES : (block + 1) * LANES]
        for s in samples:
            sums[s] = sums[s] + tile * received[block, s : s + 1, :]
    wide = [jnp.broadcast_to(jnp.sum(value, axis=1, keepdims=True), (2 * rows, LANES)) for value in sums]
    for s in samples:
        total[s] = wide[s]

    def one(block, carry):
        at = pl.multiple_of((blocks + block) * LANES, LANES)
        tile = buffer[:, pl.ds(at, LANES)]
        parts = [jnp.sum(tile * total[s], axis=0, keepdims=True) for s in samples]
        path_block = path[block] - jnp.concatenate(parts, axis=0)
        send_block(block, path_block)
        return carry

    groups = send.shape[0] // X
    share = (upper - groups) // groups

    def send_block(block, value):
        low = block >= upper - groups
        place = jnp.where(low, block - (upper - groups), block // share)
        row = jnp.where(low, 0, 2 + 2 * lax.rem(block, share))
        depth = groups // 2
        for x in range(X):
            dest = (place // depth) * (X * depth) + x * depth + lax.rem(place, depth)
            send[dest, pl.ds(row, 2), :] = value[2 * x : 2 * x + 2, :]

    lax.fori_loop(0, upper, one, 0, unroll=4)


def lowest(received, own, other, path, blocks, upper, groups):
    rows, width = own.shape
    return call(
        functools.partial(lowest_kernel, blocks, upper),
        f32(X * groups, 8, LANES),
        in_specs=[VMEM, HBM, HBM, VMEM],
        out_specs=VMEM,
        scratch_shapes=[
            pltpu.VMEM((received.shape[1], 2 * rows, LANES), jnp.float32),
            pltpu.VMEM((2 * rows, width), jnp.float32),
            pltpu.SemaphoreType.DMA((2, rows // 8)),
        ],
        cost_estimate=cost(2 * rows * width),
    )(received, own, other, path)


def backward_kernel(blocks, known_blocks, number, received, solved, *refs):
    matrices, refs = refs[:number], refs[number:]
    known, (send, newest, total, vector, *stream) = refs[: len(known_blocks) - 1], refs[len(known_blocks) - 1 :]
    matrices, copies = begin(matrices, stream)
    newest[...] = jnp.sum(received[...], axis=0)
    total[...] = jnp.zeros_like(total)
    again = solved.shape[2] == LANES and solved.shape[0] == blocks
    if again:
        for block in range(blocks):
            vector[2 * block : 2 * block + 2, :] = solved[block, pl.ds(position("x") * 2, 2), :]

    def step(matrix, rows, place):
        if again:
            values = row_dot(matrix, rows, 0, vector, 0, blocks)
        else:
            values = [solved[s, place, 0:1] for s in range(PAIR)]
        column = blocks * LANES
        for ref, count in zip((*known, newest), known_blocks):
            part = row_dot(matrix, rows, column, ref, 0, count)
            values = [values[s] - part[s] for s in range(PAIR)]
            column += count * LANES
        column_dot(matrix, rows, 0, blocks, values, total)

    each_chunk(matrices, copies, step)
    whole = jnp.sum(total[...], axis=1)
    for copy in range(send.shape[0]):
        send[copy] = whole


def backward(received, matrices, solved, known, blocks, copies):
    rows = matrices[-1].shape[0]
    streamed = len(matrices) > 1
    counts = [array.shape[0] // PAIR for array in known] + [received.shape[1] // PAIR]
    width = (blocks + sum(counts)) * LANES
    return call(
        functools.partial(backward_kernel, blocks, counts, len(matrices)),
        (f32(copies, 2 * blocks, LANES), f32(*received.shape[1:])),
        in_specs=[VMEM, VMEM] + ([VMEM, HBM] if streamed else [VMEM]) + [VMEM] * len(known),
        out_specs=(VMEM,) * 2,
        scratch_shapes=[pltpu.VMEM((2 * blocks, 8, LANES), jnp.float32), pltpu.VMEM((2 * blocks, LANES), jnp.float32)]
        + stream_buffers(matrices, width),
        limit=STREAM if streamed else LIMIT,
        cost_estimate=cost(rows * width),
    )(received, solved, *matrices, *known)


def root_kernel(column, blocks, vector, matrix, send, total):
    total[...] = jnp.zeros_like(total)

    def step(rows):
        values = row_dot(matrix, rows, column, vector, 0, blocks)
        column_dot(matrix, rows, column, blocks, values, total)

    for chunk in range(matrix.shape[0] // CHUNK):
        step(pl.ds(chunk * CHUNK, CHUNK))
    whole = jnp.sum(total[...], axis=1)
    for copy in range(send.shape[0]):
        send[copy] = whole


def root(vector, matrix, column, copies):
    rows = matrix.shape[0]
    blocks = vector.shape[0] // PAIR
    return call(
        functools.partial(root_kernel, column, blocks),
        f32(copies, 2 * blocks, LANES),
        in_specs=[VMEM, VMEM],
        out_specs=VMEM,
        scratch_shapes=[pltpu.VMEM((2 * blocks, 8, LANES), jnp.float32)],
        cost_estimate=cost(rows * blocks * LANES),
    )(vector, matrix)


def sum_kernel(copies, received, send):
    whole = jnp.sum(received[...], axis=0)
    for copy in range(copies):
        send[copy] = whole


def sum_and_copy(received, copies):
    return call(functools.partial(sum_kernel, copies), f32(copies, *received.shape[1:]))(received)


def expand(counts, terms, index, first_block, path):
    subtree = own_subtree()

    def one(block, carry):
        at = window(counts, subtree, first_block + block, index.shape[1])
        selector = one_hot(index[pl.ds(subtree, 1), pl.ds(at, 2 * LANES)], first_block + block)
        out = lax.dot_general(terms[:, pl.ds(at, 2 * LANES)], selector, NT, preferred_element_type=jnp.float32)
        path[block] = -(out[0:8] + out[8:16] + out[16:24])
        return carry

    lax.fori_loop(0, path.shape[0], one, 0, unroll=4)


def add_own(both, depth, heights, path):
    z, core, x = position("z"), position("c"), position("x")
    half = pl.multiple_of(core * 8, 8)
    lane = lax.broadcasted_iota(jnp.int32, (8, LANES), 1)
    start = source = 0
    for height in range(4):
        width = 8 if height < 2 else 16
        for other in range(C):
            if height not in heights:
                continue
            offset = z * width
            block = start
            if height < 3:
                block = block + position(("y", "y1", "y0")[height]) * (XC * depth * width // LANES)
            if width == 8:
                offset = offset + other * 64
                block = block + x
            else:
                block = block + x * 2 + other
            small = both[other, pl.ds(half, 8), both.shape[2] - LANES :]
            moved = pltpu.roll(small, lax.rem(offset - source + LANES, LANES), 1)
            path[block] = path[block] + jnp.where((lane >= offset) & (lane < offset + width), moved, 0.0)
        start += WIDTHS[height] // LANES if height in heights else 0
        source += width


def product_kernel(values, coupling, rhs0, rhs1, rhs2, rhs3, out):
    columns = coupling.shape[1]
    out[:, :columns] = lax.dot_general(
        values[...], coupling[...], NN, precision=lax.Precision.HIGHEST, preferred_element_type=jnp.float32
    )
    parts = [jnp.transpose(rhs0[...]), jnp.transpose(rhs1[...]), rhs2[...], rhs3[...]]
    filled = sum(part.shape[1] for part in parts)
    parts.append(jnp.zeros((out.shape[0], LANES - filled), jnp.float32))
    out[:, columns:] = jnp.concatenate(parts, axis=1)


def own_product(values, coupling, rhs_parts):
    rhs0, rhs1, rhs2, rhs3 = rhs_parts
    shape = f32(values.shape[0], coupling.shape[1] + LANES)
    return call(product_kernel, shape, in_specs=[VMEM] * 6, out_specs=VMEM, limit=WHOLE)(values, coupling, rhs0.T, rhs1.T, rhs2, rhs3)


def stage_in(parts, stages, groups, ready):
    copies = []
    for stage, size in zip(stages, groups):
        column = 0
        for part in parts[:size]:
            width = part.shape[1]
            for row in range(0, part.shape[0], 8):
                rows = pl.ds(row, 8)
                copies.append(
                    pltpu.make_async_copy(part.at[rows, :], stage.at[rows, pl.ds(column, width)], ready.at[len(copies)])
                )
            column += width
        parts = parts[size:]
    for copy in copies:
        copy.start()
    return copies


def stage_out(copies, stages, packs, done):
    for copy in copies:
        copy.wait()
    copies = []
    for stage, pack in zip(stages, packs):
        for row in range(0, pack.shape[0], 8):
            rows = pl.ds(row, 8)
            copies.append(pltpu.make_async_copy(stage.at[rows, :], pack.at[rows, :], done.at[len(copies)]))
    for copy in copies:
        copy.start()
    return copies


def pack_shapes(groups):
    parts = [part for group in groups for part in group]
    packs = [f32(group[0].shape[0], sum(part.shape[1] for part in group)) for group in groups]
    scratch = [
        pltpu.SemaphoreType.DMA((sum(part.shape[0] // 8 for part in parts),)),
        pltpu.SemaphoreType.DMA((sum(pack.shape[0] // 8 for pack in packs),)),
    ]
    return parts, packs, scratch + [pltpu.VMEM(pack.shape, jnp.float32) for pack in packs]


def first_kernel(depth, groups, counts, both, index, *refs):
    count, number = sum(groups), len(groups)
    parts, (send, terms, *packs), (path, ready, done, *stages) = refs[:count], refs[count : -3 - number], refs[-3 - number :]
    copies = stage_in(parts, stages, groups, ready)
    columns = both.shape[2] - LANES
    half = pl.multiple_of(position("c") * 8, 8)
    pieces = split3(both[0, pl.ds(half, 8), :columns] + both[1, pl.ds(half, 8), :columns])
    terms[...] = jnp.concatenate([*pieces, jnp.zeros_like(pieces[0])], axis=0)
    expand(counts, terms, index, sum(WIDTHS[:3]) // LANES, path)
    copies = stage_out(copies, stages, packs, done)
    add_own(both, depth, (3,), path)
    for dest in range(X):
        for other in range(depth):
            send[dest * depth + other] = path[other]
    for copy in copies:
        copy.wait()


def first(both, index, counts, depth, groups):
    columns = both.shape[2] - LANES
    parts, packs, scratch = pack_shapes(groups)
    outs = call(
        functools.partial(first_kernel, depth, [len(group) for group in groups]),
        (f32(X * depth, 8, LANES), jax.ShapeDtypeStruct((32, columns), jnp.bfloat16), *packs),
        in_specs=[SMEM, VMEM, VMEM] + [HBM] * len(parts),
        out_specs=(VMEM, VMEM) + (HBM,) * len(packs),
        scratch_shapes=[pltpu.VMEM((WIDTHS[3] // LANES, 8, LANES), jnp.float32)] + scratch,
        limit=WHOLE,
    )(counts, both, index, *parts)
    return outs[0], outs[1], outs[2:]


def upper_kernel(depth, counts, both, terms, index, path):
    expand(counts, terms, index, 0, path)
    add_own(both, depth, (0, 1, 2), path)


def upper_path(both, terms, index, counts, depth):
    blocks = sum(WIDTHS[:3]) // LANES
    return call(
        functools.partial(upper_kernel, depth),
        f32(blocks, 8, LANES),
        in_specs=[SMEM, VMEM, VMEM, VMEM],
        out_specs=VMEM,
        cost_estimate=cost(blocks * LANES * LANES),
    )(counts, both, terms, index)


def pick(counts, index, terms, first_block, blocks, chosen):
    def one(block, carry):
        for half in range(2):
            at = window(counts, position("y") * 2 + half, first_block + block, index.shape[1])
            selector = one_hot(index[pl.ds(position("y") * 2 + half, 1), pl.ds(at, 2 * LANES)], first_block + block)
            out = lax.dot_general(
                terms[block].astype(jnp.bfloat16), selector, NN, preferred_element_type=jnp.float32
            )
            chosen[half, :, pl.ds(at, 2 * LANES)] = chosen[half, :, pl.ds(at, 2 * LANES)] + out
        return carry

    lax.fori_loop(0, blocks, one, 0, unroll=4)


def store_terms(ref, terms):
    blocks = ref.shape[0] // PAIR
    pieces = split3(ref[...].reshape(blocks, PAIR, LANES))
    terms[...] = jnp.concatenate([*pieces, jnp.zeros_like(pieces[0])], axis=1).astype(jnp.float32)


def pick_kernel(first_block, counts, x, index, chosen, terms):
    store_terms(x, terms)
    chosen[...] = jnp.zeros_like(chosen)
    pick(counts, index, terms, first_block, x.shape[0] // PAIR, chosen)


def picked(x, index, counts, first_block):
    blocks = x.shape[0] // PAIR
    return call(
        functools.partial(pick_kernel, first_block),
        f32(2, 8, index.shape[1]),
        in_specs=[SMEM, VMEM, VMEM],
        out_specs=VMEM,
        scratch_shapes=[pltpu.VMEM((blocks, 8, LANES), jnp.float32)],
        cost_estimate=cost(blocks * 2 * LANES * LANES),
    )(counts, x, index)


def last_kernel(widths, counts, received, x0, x1, x2, coupling, index, chosen0, chosen1, chosen2, send, x3, terms, chosen):
    x3[...] = jnp.sum(received[...], axis=0)
    store_terms(x3, terms)
    chosen[...] = chosen0[...] + chosen1[...] + chosen2[...]
    pick(counts, index, terms, sum(widths[:3]), widths[3], chosen)
    rows, columns = coupling.shape[0] // 2, coupling.shape[1]
    lane = lax.broadcasted_iota(jnp.int32, (CHUNK, LANES), 1)
    handed = []
    for half in range(2):
        chosen[half, 0:2, :] = chosen[half, 0:2, :] + chosen[half, 2:4, :] + chosen[half, 4:6, :]
        columns_of = []
        for chunk in range(rows // CHUNK):
            at = half * rows + chunk * CHUNK
            sums = [[None, None] for _ in range(PAIR)]
            for block in range(columns // LANES):
                place = slice(block * LANES, (block + 1) * LANES)
                tile = coupling[at : at + CHUNK, place]
                for s in range(PAIR):
                    part, old = tile * chosen[half, s : s + 1, place], sums[s][block % 2]
                    sums[s][block % 2] = part if old is None else old + part
            totals = [jnp.sum(value[0] + value[1], axis=1, keepdims=True) for value in sums]
            columns_of.append(jnp.where(lane == 0, totals[0], jnp.where(lane == 1, totals[1], 0.0)))
        handed.append(jnp.transpose(jnp.concatenate(columns_of, axis=0))[0:PAIR, :])
    send[...] = jnp.zeros_like(send)
    for dest in range(XC):
        core, x = dest // X, dest % X
        for level, ref in enumerate((x0, x1, x2, x3)):
            block = x if level < 2 else x * 2 + core
            if level < 3:
                block = block + position(("y", "y1", "y0")[level]) * (widths[level] // (Y // 2**level))
            send[dest, 2 * level : 2 * level + 2, :] = ref[pl.ds(block * 2, 2), :]
        send[dest, 8:10, :] = handed[x // 2]


def last(received, known, chosen, coupling, index, counts):
    widths = [width // LANES for width in WIDTHS]
    return call(
        functools.partial(last_kernel, widths),
        f32(XC, 16, LANES),
        in_specs=[SMEM] + [VMEM] * 9,
        out_specs=VMEM,
        scratch_shapes=[
            pltpu.VMEM(received.shape[1:], jnp.float32),
            pltpu.VMEM((widths[3], 8, LANES), jnp.float32),
            pltpu.VMEM((2, 8, coupling.shape[1]), jnp.float32),
        ],
    )(counts, received, *known, coupling, index, *chosen)


def finish_kernel(received, values, out0, out1, out2, out3, handed):
    z, core = position("z"), position("c")
    offsets = (core * 64 + z * 8, core * 64 + z * 8, z * 16, z * 16, (lax.rem(position("x"), 2) * 2 + core) * values.shape[1])
    for level, ref in enumerate((out0, out1, out2, out3, handed)):
        value = jnp.concatenate([received[source, 2 * level : 2 * level + 2, :] for source in range(XC)], axis=0)
        moved = pltpu.roll(value, lax.rem(LANES - offsets[level], LANES), 1)
        if level < 2:
            ref[...] = jnp.transpose(moved)[: ref.shape[0], :]
        elif level < 4:
            ref[...] = moved[:, : ref.shape[1]]
        else:
            ref[...] = values[...] - moved[:, : ref.shape[1]]


def finish(received, values, widths):
    samples = XC * PAIR
    shapes = [f32(width, samples) for width in widths[:2]] + [f32(samples, width) for width in widths[2:]]
    outs = call(finish_kernel, (*shapes, f32(*values.shape)), in_specs=[VMEM, VMEM])(received, values)
    return outs[0].T, outs[1].T, *outs[2:]


def body(
    rhs_root,
    rhs_level1,
    rhs_level2,
    rhs_level3,
    inv_root,
    inv_level1,
    inv_level2,
    inv_level3,
    cross_level1,
    cross_level2,
    cross_level3,
    subtree_values,
    coupling,
    coupled_rows,
):
    depth = lax.axis_size("z")
    counts = [width // LANES for width in WIDTHS]
    blocks = sum(counts)

    rhs_parts = [rhs_root, rhs_level1, rhs_level2, rhs_level3]
    both = lax.all_gather(own_product(subtree_values, coupling, rhs_parts), "c", axis=0, tiled=False)

    def gathered(whole):
        return lax.all_gather(whole, ("x", "c"), axis=0, tiled=True)

    both, coupled_rows = lax.optimization_barrier((both, coupled_rows))
    edges = jnp.arange(blocks, dtype=jnp.int32) * LANES
    ahead = jnp.sum((coupled_rows[:, None, :] < edges[None, :, None]).astype(jnp.int32), axis=2)

    groups = ((inv_level3, cross_level3), (inv_level2, cross_level2), (inv_level1, cross_level1, inv_root))
    send, terms, (own3, pack2, pack1) = first(both, coupled_rows, ahead, depth, groups)
    matrix2 = gathered(pack2)
    matrix1 = gathered(pack1)
    path = upper_path(both, terms, coupled_rows, ahead, depth)
    received, other3, path = lax.optimization_barrier(
        (exchange(send, ("x", "z")), lax.ppermute(own3, "c", [(0, 1), (1, 0)]), path)
    )
    target3 = exchange(sum_and_copy(received, depth), ("z",))
    send = lowest(target3, own3, other3, path, counts[3], sum(counts[:3]), 2 * depth)
    send, own3, coupling = lax.optimization_barrier((send, own3, coupling))
    matrix3 = gathered(own3)
    all_coupling = gathered(coupling)
    received = sum_and_copy(exchange(send, ("y0", "x", "z")), 2 * depth)
    target2, half2 = lax.optimization_barrier((exchange(received, ("y0", "z")), fetched(matrix2, 0.5)))
    solved2, send, rest = forward(
        target2, (half2, matrix2), received[0], counts[2], counts[0] + counts[1], counts[0], 4 * depth, 6
    )
    received, matrix1 = lax.optimization_barrier((exchange(send, ("y1", "y0", "z")), fetched(matrix1)))
    solved1, send, rest = forward(received, (matrix1,), rest, counts[1], counts[0], 0, Y, 0)

    def sum_root(copies):
        received = exchange(copies.reshape(Y * depth, -1, LANES), ALL_Y + ("z",))
        return exchange(sum_and_copy(received, depth), ("z",))

    target = sum_root(send).reshape(-1, LANES)
    received = sum_root(root(target, matrix1, WIDTHS[1] + WIDTHS[0], Y)).reshape(1, -1, LANES)
    send, x0 = backward(received, (matrix1,), solved1, [], counts[1], 4 * depth)
    x0, matrix2 = lax.optimization_barrier((x0, matrix2))
    received, chosen0, half2 = lax.optimization_barrier(
        (exchange(send, ("y1", "y0", "z")), picked(x0, coupled_rows, ahead, 0), fetched(matrix2, 0.5))
    )
    send, x1 = backward(received, (half2, matrix2), solved2, [x0], counts[2], 2 * depth)
    received, chosen1, half3 = lax.optimization_barrier(
        (exchange(send, ("y0", "z")), picked(x1, coupled_rows, ahead, counts[0]), fetched(matrix3, 0.5))
    )
    send, x2 = backward(received, (half3, matrix3), target3, [x0, x1], counts[3], depth)
    received, chosen2, all_coupling = lax.optimization_barrier(
        (exchange(send, ("z",)), picked(x2, coupled_rows, ahead, counts[0] + counts[1]), fetched(all_coupling))
    )
    send = last(received, [x0, x1, x2], [chosen0, chosen1, chosen2], all_coupling, coupled_rows, ahead)
    received = exchange(send, ("c", "x"))
    return finish(received, subtree_values, [part.shape[1] for part in rhs_parts])


def solution(mesh):
    shape = (2, 2, 2, X, C, mesh.shape["sep"])
    fine = Mesh(mesh.devices.reshape(shape), ("y2", "y1", "y0", "x", "c", "z"))
    every = ("y2", "y1", "y0", "x", "c", "z")
    columns, rows = P(None, every), P(every, None)
    in_specs = (columns,) * 4 + (rows,) * 7 + (columns, rows, P())
    return jax.shard_map(body, mesh=fine, in_specs=in_specs, out_specs=(columns,) * 5, check_vma=False)
```

```python
import functools

import jax
import jax.numpy as jnp
from jax import lax
from jax.experimental import pallas as pl
from jax.experimental.pallas import tpu as pltpu
from jax.sharding import Mesh, PartitionSpec as P

ROOT_ROWS = 4096
LEVEL1_ROWS = 2048
LEVEL2_ROWS = 2048
LEVEL3_ROWS = 1024
WIDTHS = (ROOT_ROWS, LEVEL1_ROWS, LEVEL2_ROWS, LEVEL3_ROWS)
Y, X, C = 8, 4, 2
XC = X * C
PAIR = 2
LANES = 128
CHUNK = 32
HBM = pl.BlockSpec(memory_space=pltpu.HBM)
LIMIT = 16 * 2**20
STREAM = 50 * 2**20
WHOLE = 57 * 2**20
ALL_Y = ("y2", "y1", "y0")
INTERPRET = False
VMEM = pl.BlockSpec(memory_space=pltpu.VMEM)
SMEM = pl.BlockSpec(memory_space=pltpu.SMEM)


def call(kernel, out_shape, **options):
    limit = options.pop("limit", LIMIT)
    return pl.pallas_call(
        kernel,
        out_shape=out_shape,
        compiler_params=pltpu.CompilerParams(vmem_limit_bytes=limit),
        interpret=INTERPRET,
        **options,
    )


def cost(elements):
    return pl.CostEstimate(flops=8 * elements, bytes_accessed=4 * elements, transcendentals=0)


def position(name):
    if name == "y":
        return (lax.axis_index("y2") * 2 + lax.axis_index("y1")) * 2 + lax.axis_index("y0")
    if name == "y1":
        return lax.axis_index("y1") * 2 + lax.axis_index("y0")
    return lax.axis_index(name)


def own_subtree():
    return position("y") * 2 + position("x") // 2


def window(counts, half, block, columns):
    return pl.multiple_of(jnp.minimum(counts[half, block] // LANES, columns // LANES - 2) * LANES, LANES)


def f32(*shape):
    return jax.ShapeDtypeStruct(shape, jnp.float32)


def exchange(operand, axes):
    flat = operand.reshape(-1, LANES)
    return lax.all_to_all(flat, axes, 0, 0, tiled=True).reshape(operand.shape)


def split3(value):
    high = value.astype(jnp.bfloat16)
    rest = value - high.astype(jnp.float32)
    middle = rest.astype(jnp.bfloat16)
    low = (rest - middle.astype(jnp.float32)).astype(jnp.bfloat16)
    return high, middle, low


def one_hot(index_row, block):
    shape = (LANES, index_row.shape[1])
    rows = lax.broadcasted_iota(jnp.int32, shape, 0) + block * LANES
    return jnp.where(rows == index_row, 1.0, 0.0).astype(jnp.bfloat16)


NT = (((1,), (1,)), ((), ()))
NN = (((1,), (0,)), ((), ()))


def row_dot(matrix, rows, column, vector, first, blocks):
    sums = [[None, None] for _ in range(PAIR)]
    for block in range(blocks):
        tile = matrix[rows, column + block * LANES : column + (block + 1) * LANES]
        for s in range(PAIR):
            at = (first + block) * PAIR + s
            part, old = tile * vector[at : at + 1, :], sums[s][block % 2]
            sums[s][block % 2] = part if old is None else old + part
    return [jnp.sum(value[0] + value[1], axis=1, keepdims=True) for value in sums]


def column_dot(matrix, rows, column, blocks, factors, total):
    wide = [jnp.broadcast_to(value, (CHUNK, LANES)) for value in factors]
    for block in range(blocks):
        tile = matrix[rows, column + block * LANES : column + (block + 1) * LANES]
        for s in range(PAIR):
            part = jnp.sum((tile * wide[s]).reshape(CHUNK // 8, 8, LANES), axis=0)
            at = block * PAIR + s
            total[at] = total[at] + part


def chunk_copies(matrix, buffer, ready):
    copies = []
    for place in range(matrix.shape[0] // 8):
        rows, columns = pl.ds(place * 8, 8), pl.ds(0, buffer.shape[1])
        copies.append(pltpu.make_async_copy(matrix.at[rows, columns], buffer.at[rows, columns], ready.at[place]))
    return copies


def begin(matrices, stream):
    if not stream:
        return matrices, None
    buffer, ready = stream
    copies = chunk_copies(matrices[-1].at[pl.ds(matrices[-1].shape[0] - buffer.shape[0], buffer.shape[0]), :], buffer, ready)
    for copy in copies:
        copy.start()
    return (*matrices[:-1], buffer), copies


def each_chunk(matrices, copies, step):
    share = CHUNK // 8
    base = 0
    for matrix in matrices:
        streamed = copies and matrix is matrices[-1]
        for chunk in range(matrix.shape[0] // CHUNK):
            if streamed:
                for copy in copies[chunk * share : (chunk + 1) * share]:
                    copy.wait()
            step(matrix, pl.ds(chunk * CHUNK, CHUNK), pl.ds(base + chunk * CHUNK, CHUNK))
        base += matrix.shape[0]


def stream_buffers(matrices, width):
    if len(matrices) == 1:
        return []
    rows = matrices[1].shape[0] - matrices[0].shape[0]
    return [pltpu.VMEM((rows, width), jnp.float32), pltpu.SemaphoreType.DMA((rows // 8,))]


def fetch_kernel(matrix, out, ready):
    copies = chunk_copies(matrix.at[pl.ds(0, out.shape[0]), :], out, ready)
    for copy in copies:
        copy.start()
    for copy in copies:
        copy.wait()


def fetched(matrix, part=1.0):
    rows, width = int(matrix.shape[0] * part), matrix.shape[1]
    return call(
        fetch_kernel,
        f32(rows, width),
        in_specs=[HBM],
        out_specs=VMEM,
        scratch_shapes=[pltpu.SemaphoreType.DMA((rows // 8,))],
        cost_estimate=cost(2 * rows * width),
    )(matrix)


def forward_kernel(blocks, upper, keep, extra, count, received, rest_in, *refs):
    matrices, (solved, send, rest, vector, total, *stream) = refs[:count], refs[count:]
    matrices, copies = begin(matrices, stream)
    if extra:
        for source in range(blocks):
            vector[2 * source : 2 * source + 2, :] = received[source, 0:2, :]
    else:
        vector[...] = jnp.sum(received[...], axis=0)
    total[...] = jnp.zeros_like(total)

    def step(matrix, rows, place):
        values = row_dot(matrix, rows, 0, vector, 0, blocks)
        for s in range(PAIR):
            solved[s, place, :] = jnp.broadcast_to(values[s], (CHUNK, LANES))
        column_dot(matrix, rows, blocks * LANES, upper, values, total)

    each_chunk(matrices, copies, step)
    whole = -jnp.sum(total[...], axis=1)
    if extra:
        rest[...] = whole
        place = position("y0") * (blocks // 2) + position("z")
        for row in range(extra):
            at = pl.ds(place * extra + row, 1)
            rest[at, :] = rest[at, :] + rest_in[2 + row : 3 + row, :]
        whole = rest[...]
    else:
        whole = whole + rest_in[0 : 2 * upper, :]
        rest[...] = whole
    for copy in range(send.shape[0]):
        send[copy] = whole[2 * keep :, :]


def forward(received, matrices, rest_in, blocks, upper, keep, copies, extra):
    rows = matrices[-1].shape[0]
    streamed = len(matrices) > 1
    width = upper * LANES + blocks * LANES
    return call(
        functools.partial(forward_kernel, blocks, upper, keep, extra, len(matrices)),
        (f32(PAIR, rows, LANES), f32(copies, 2 * (upper - keep), LANES), f32(2 * upper, LANES)),
        in_specs=[VMEM, VMEM] + ([VMEM, HBM] if streamed else [VMEM]),
        out_specs=(VMEM,) * 3,
        scratch_shapes=[pltpu.VMEM((2 * blocks, LANES), jnp.float32), pltpu.VMEM((2 * upper, 8, LANES), jnp.float32)]
        + stream_buffers(matrices, width),
        limit=STREAM if streamed else LIMIT,
        cost_estimate=cost(rows * width),
    )(received, rest_in, *matrices)


def lowest_kernel(blocks, upper, received, own, other, path, send, total, buffer, ready):
    rows = own.shape[0]
    copies = chunk_copies(own, buffer.at[0:rows, :], ready.at[0]) + chunk_copies(other, buffer.at[rows:, :], ready.at[1])
    for copy in copies:
        copy.start()
    for copy in copies:
        copy.wait()
    samples = range(received.shape[1])
    sums = [jnp.zeros((2 * rows, LANES), jnp.float32) for _ in samples]
    for block in range(blocks):
        tile = buffer[:, block * LANES : (block + 1) * LANES]
        for s in samples:
            sums[s] = sums[s] + tile * received[block, s : s + 1, :]
    wide = [jnp.broadcast_to(jnp.sum(value, axis=1, keepdims=True), (2 * rows, LANES)) for value in sums]
    for s in samples:
        total[s] = wide[s]

    def one(block, carry):
        at = pl.multiple_of((blocks + block) * LANES, LANES)
        tile = buffer[:, pl.ds(at, LANES)]
        parts = [jnp.sum(tile * total[s], axis=0, keepdims=True) for s in samples]
        path_block = path[block] - jnp.concatenate(parts, axis=0)
        send_block(block, path_block)
        return carry

    groups = send.shape[0] // X
    share = (upper - groups) // groups

    def send_block(block, value):
        low = block >= upper - groups
        place = jnp.where(low, block - (upper - groups), block // share)
        row = jnp.where(low, 0, 2 + 2 * lax.rem(block, share))
        depth = groups // 2
        for x in range(X):
            dest = (place // depth) * (X * depth) + x * depth + lax.rem(place, depth)
            send[dest, pl.ds(row, 2), :] = value[2 * x : 2 * x + 2, :]

    lax.fori_loop(0, upper, one, 0, unroll=4)


def lowest(received, own, other, path, blocks, upper, groups):
    rows, width = own.shape
    return call(
        functools.partial(lowest_kernel, blocks, upper),
        f32(X * groups, 8, LANES),
        in_specs=[VMEM, HBM, HBM, VMEM],
        out_specs=VMEM,
        scratch_shapes=[
            pltpu.VMEM((received.shape[1], 2 * rows, LANES), jnp.float32),
            pltpu.VMEM((2 * rows, width), jnp.float32),
            pltpu.SemaphoreType.DMA((2, rows // 8)),
        ],
        cost_estimate=cost(2 * rows * width),
    )(received, own, other, path)


def backward_kernel(blocks, known_blocks, number, received, solved, *refs):
    matrices, refs = refs[:number], refs[number:]
    known, (send, newest, total, vector, *stream) = refs[: len(known_blocks) - 1], refs[len(known_blocks) - 1 :]
    matrices, copies = begin(matrices, stream)
    newest[...] = jnp.sum(received[...], axis=0)
    total[...] = jnp.zeros_like(total)
    again = solved.shape[2] == LANES and solved.shape[0] == blocks
    if again:
        for block in range(blocks):
            vector[2 * block : 2 * block + 2, :] = solved[block, pl.ds(position("x") * 2, 2), :]

    def step(matrix, rows, place):
        if again:
            values = row_dot(matrix, rows, 0, vector, 0, blocks)
        else:
            values = [solved[s, place, 0:1] for s in range(PAIR)]
        column = blocks * LANES
        for ref, count in zip((*known, newest), known_blocks):
            part = row_dot(matrix, rows, column, ref, 0, count)
            values = [values[s] - part[s] for s in range(PAIR)]
            column += count * LANES
        column_dot(matrix, rows, 0, blocks, values, total)

    each_chunk(matrices, copies, step)
    whole = jnp.sum(total[...], axis=1)
    for copy in range(send.shape[0]):
        send[copy] = whole


def backward(received, matrices, solved, known, blocks, copies):
    rows = matrices[-1].shape[0]
    streamed = len(matrices) > 1
    counts = [array.shape[0] // PAIR for array in known] + [received.shape[1] // PAIR]
    width = (blocks + sum(counts)) * LANES
    return call(
        functools.partial(backward_kernel, blocks, counts, len(matrices)),
        (f32(copies, 2 * blocks, LANES), f32(*received.shape[1:])),
        in_specs=[VMEM, VMEM] + ([VMEM, HBM] if streamed else [VMEM]) + [VMEM] * len(known),
        out_specs=(VMEM,) * 2,
        scratch_shapes=[pltpu.VMEM((2 * blocks, 8, LANES), jnp.float32), pltpu.VMEM((2 * blocks, LANES), jnp.float32)]
        + stream_buffers(matrices, width),
        limit=STREAM if streamed else LIMIT,
        cost_estimate=cost(rows * width),
    )(received, solved, *matrices, *known)


def root_kernel(column, blocks, vector, matrix, send, total):
    total[...] = jnp.zeros_like(total)

    def step(rows):
        values = row_dot(matrix, rows, column, vector, 0, blocks)
        column_dot(matrix, rows, column, blocks, values, total)

    for chunk in range(matrix.shape[0] // CHUNK):
        step(pl.ds(chunk * CHUNK, CHUNK))
    whole = jnp.sum(total[...], axis=1)
    for copy in range(send.shape[0]):
        send[copy] = whole


def root(vector, matrix, column, copies):
    rows = matrix.shape[0]
    blocks = vector.shape[0] // PAIR
    return call(
        functools.partial(root_kernel, column, blocks),
        f32(copies, 2 * blocks, LANES),
        in_specs=[VMEM, VMEM],
        out_specs=VMEM,
        scratch_shapes=[pltpu.VMEM((2 * blocks, 8, LANES), jnp.float32)],
        cost_estimate=cost(rows * blocks * LANES),
    )(vector, matrix)


def sum_kernel(copies, received, send):
    whole = jnp.sum(received[...], axis=0)
    for copy in range(copies):
        send[copy] = whole


def sum_and_copy(received, copies):
    return call(functools.partial(sum_kernel, copies), f32(copies, *received.shape[1:]))(received)


def expand(counts, terms, index, first_block, path):
    subtree = own_subtree()

    def one(block, carry):
        at = window(counts, position("x") // 2, first_block + block, index.shape[1])
        selector = one_hot(index[pl.ds(subtree, 1), pl.ds(at, 2 * LANES)], first_block + block)
        out = lax.dot_general(terms[:, pl.ds(at, 2 * LANES)], selector, NT, preferred_element_type=jnp.float32)
        path[block] = -(out[0:8] + out[8:16] + out[16:24])
        return carry

    lax.fori_loop(0, path.shape[0], one, 0, unroll=4)


def add_own(both, depth, heights, path):
    z, core, x = position("z"), position("c"), position("x")
    half = pl.multiple_of(core * 8, 8)
    lane = lax.broadcasted_iota(jnp.int32, (8, LANES), 1)
    start = source = 0
    for height in range(4):
        width = 8 if height < 2 else 16
        for other in range(C):
            if height not in heights:
                continue
            offset = z * width
            block = start
            if height < 3:
                block = block + position(("y", "y1", "y0")[height]) * (XC * depth * width // LANES)
            if width == 8:
                offset = offset + other * 64
                block = block + x
            else:
                block = block + x * 2 + other
            small = both[other, pl.ds(half, 8), both.shape[2] - LANES :]
            moved = pltpu.roll(small, lax.rem(offset - source + LANES, LANES), 1)
            path[block] = path[block] + jnp.where((lane >= offset) & (lane < offset + width), moved, 0.0)
        start += WIDTHS[height] // LANES if height in heights else 0
        source += width


def product_kernel(values, coupling, rhs0, rhs1, rhs2, rhs3, index, out, ahead):
    columns = coupling.shape[1]
    out[:, :columns] = lax.dot_general(
        values[...], coupling[...], NN, precision=lax.Precision.HIGHEST, preferred_element_type=jnp.float32
    )
    parts = [jnp.transpose(rhs0[...]), jnp.transpose(rhs1[...]), rhs2[...], rhs3[...]]
    filled = sum(part.shape[1] for part in parts)
    parts.append(jnp.zeros((out.shape[0], LANES - filled), jnp.float32))
    out[:, columns:] = jnp.concatenate(parts, axis=1)
    edges = lax.broadcasted_iota(jnp.int32, (LANES, 2 * LANES), 0) * LANES
    for half in range(2):
        def compare(block, total):
            at = pl.multiple_of(block * 2 * LANES, LANES)
            row = index[pl.ds(position("y") * 2 + half, 1), pl.ds(at, 2 * LANES)]
            return total + jnp.where(row < edges, 1.0, 0.0)

        total = lax.fori_loop(0, columns // (2 * LANES), compare, jnp.zeros((LANES, 2 * LANES), jnp.float32), unroll=2)
        total = jnp.broadcast_to(jnp.sum(total, axis=1, keepdims=True), (LANES, LANES))
        ahead[half : half + 1, :] = jnp.transpose(total)[0:1, :].astype(jnp.int32)


def own_product(values, coupling, rhs_parts, index):
    rhs0, rhs1, rhs2, rhs3 = rhs_parts
    shapes = (f32(values.shape[0], coupling.shape[1] + LANES), jax.ShapeDtypeStruct((2, LANES), jnp.int32))
    return call(product_kernel, shapes, in_specs=[VMEM] * 7, out_specs=(VMEM, VMEM), limit=WHOLE)(
        values, coupling, rhs0.T, rhs1.T, rhs2, rhs3, index
    )


def stage_in(parts, stages, groups, ready):
    copies = []
    for stage, size in zip(stages, groups):
        column = 0
        for part in parts[:size]:
            width = part.shape[1]
            for row in range(0, part.shape[0], 8):
                rows = pl.ds(row, 8)
                copies.append(
                    pltpu.make_async_copy(part.at[rows, :], stage.at[rows, pl.ds(column, width)], ready.at[len(copies)])
                )
            column += width
        parts = parts[size:]
    for copy in copies:
        copy.start()
    return copies


def stage_out(copies, stages, packs, done):
    for copy in copies:
        copy.wait()
    copies = []
    for stage, pack in zip(stages, packs):
        for row in range(0, pack.shape[0], 8):
            rows = pl.ds(row, 8)
            copies.append(pltpu.make_async_copy(stage.at[rows, :], pack.at[rows, :], done.at[len(copies)]))
    for copy in copies:
        copy.start()
    return copies


def pack_shapes(groups):
    parts = [part for group in groups for part in group]
    packs = [f32(group[0].shape[0], sum(part.shape[1] for part in group)) for group in groups]
    scratch = [
        pltpu.SemaphoreType.DMA((sum(part.shape[0] // 8 for part in parts),)),
        pltpu.SemaphoreType.DMA((sum(pack.shape[0] // 8 for pack in packs),)),
    ]
    return parts, packs, scratch + [pltpu.VMEM(pack.shape, jnp.float32) for pack in packs]


def first_kernel(depth, groups, counts, both, index, *refs):
    count, number = sum(groups), len(groups)
    parts, (send, terms, *packs), (path, ready, done, *stages) = refs[:count], refs[count : -3 - number], refs[-3 - number :]
    copies = stage_in(parts, stages, groups, ready)
    columns = both.shape[2] - LANES
    half = pl.multiple_of(position("c") * 8, 8)
    pieces = split3(both[0, pl.ds(half, 8), :columns] + both[1, pl.ds(half, 8), :columns])
    terms[...] = jnp.concatenate([*pieces, jnp.zeros_like(pieces[0])], axis=0)
    expand(counts, terms, index, sum(WIDTHS[:3]) // LANES, path)
    copies = stage_out(copies, stages, packs, done)
    add_own(both, depth, (3,), path)
    for dest in range(X):
        for other in range(depth):
            send[dest * depth + other] = path[other]
    for copy in copies:
        copy.wait()


def first(both, index, counts, depth, groups):
    columns = both.shape[2] - LANES
    parts, packs, scratch = pack_shapes(groups)
    outs = call(
        functools.partial(first_kernel, depth, [len(group) for group in groups]),
        (f32(X * depth, 8, LANES), jax.ShapeDtypeStruct((32, columns), jnp.bfloat16), *packs),
        in_specs=[SMEM, VMEM, VMEM] + [HBM] * len(parts),
        out_specs=(VMEM, VMEM) + (HBM,) * len(packs),
        scratch_shapes=[pltpu.VMEM((WIDTHS[3] // LANES, 8, LANES), jnp.float32)] + scratch,
        limit=WHOLE,
    )(counts, both, index, *parts)
    return outs[0], outs[1], outs[2:]


def upper_kernel(depth, counts, both, terms, index, path):
    expand(counts, terms, index, 0, path)
    add_own(both, depth, (0, 1, 2), path)


def upper_path(both, terms, index, counts, depth):
    blocks = sum(WIDTHS[:3]) // LANES
    return call(
        functools.partial(upper_kernel, depth),
        f32(blocks, 8, LANES),
        in_specs=[SMEM, VMEM, VMEM, VMEM],
        out_specs=VMEM,
        cost_estimate=cost(blocks * LANES * LANES),
    )(counts, both, terms, index)


def pick(counts, index, terms, first_block, blocks, chosen):
    def one(block, carry):
        for half in range(2):
            at = window(counts, half, first_block + block, index.shape[1])
            selector = one_hot(index[pl.ds(position("y") * 2 + half, 1), pl.ds(at, 2 * LANES)], first_block + block)
            out = lax.dot_general(
                terms[block].astype(jnp.bfloat16), selector, NN, preferred_element_type=jnp.float32
            )
            chosen[half, :, pl.ds(at, 2 * LANES)] = chosen[half, :, pl.ds(at, 2 * LANES)] + out
        return carry

    lax.fori_loop(0, blocks, one, 0, unroll=4)


def store_terms(ref, terms):
    blocks = ref.shape[0] // PAIR
    pieces = split3(ref[...].reshape(blocks, PAIR, LANES))
    terms[...] = jnp.concatenate([*pieces, jnp.zeros_like(pieces[0])], axis=1).astype(jnp.float32)


def pick_kernel(first_block, counts, x, index, chosen, terms):
    store_terms(x, terms)
    chosen[...] = jnp.zeros_like(chosen)
    pick(counts, index, terms, first_block, x.shape[0] // PAIR, chosen)


def picked(x, index, counts, first_block):
    blocks = x.shape[0] // PAIR
    return call(
        functools.partial(pick_kernel, first_block),
        f32(2, 8, index.shape[1]),
        in_specs=[SMEM, VMEM, VMEM],
        out_specs=VMEM,
        scratch_shapes=[pltpu.VMEM((blocks, 8, LANES), jnp.float32)],
        cost_estimate=cost(blocks * 2 * LANES * LANES),
    )(counts, x, index)


def last_kernel(widths, counts, received, x0, x1, x2, coupling, index, chosen0, chosen1, chosen2, send, x3, terms, chosen):
    x3[...] = jnp.sum(received[...], axis=0)
    store_terms(x3, terms)
    chosen[...] = chosen0[...] + chosen1[...] + chosen2[...]
    pick(counts, index, terms, sum(widths[:3]), widths[3], chosen)
    rows, columns = coupling.shape[0] // 2, coupling.shape[1]
    lane = lax.broadcasted_iota(jnp.int32, (CHUNK, LANES), 1)
    handed = []
    for half in range(2):
        chosen[half, 0:2, :] = chosen[half, 0:2, :] + chosen[half, 2:4, :] + chosen[half, 4:6, :]
        columns_of = []
        for chunk in range(rows // CHUNK):
            at = half * rows + chunk * CHUNK
            sums = [[None, None] for _ in range(PAIR)]
            for block in range(columns // LANES):
                place = slice(block * LANES, (block + 1) * LANES)
                tile = coupling[at : at + CHUNK, place]
                for s in range(PAIR):
                    part, old = tile * chosen[half, s : s + 1, place], sums[s][block % 2]
                    sums[s][block % 2] = part if old is None else old + part
            totals = [jnp.sum(value[0] + value[1], axis=1, keepdims=True) for value in sums]
            columns_of.append(jnp.where(lane == 0, totals[0], jnp.where(lane == 1, totals[1], 0.0)))
        handed.append(jnp.transpose(jnp.concatenate(columns_of, axis=0))[0:PAIR, :])
    send[...] = jnp.zeros_like(send)
    for dest in range(XC):
        core, x = dest // X, dest % X
        for level, ref in enumerate((x0, x1, x2, x3)):
            block = x if level < 2 else x * 2 + core
            if level < 3:
                block = block + position(("y", "y1", "y0")[level]) * (widths[level] // (Y // 2**level))
            send[dest, 2 * level : 2 * level + 2, :] = ref[pl.ds(block * 2, 2), :]
        send[dest, 8:10, :] = handed[x // 2]


def last(received, known, chosen, coupling, index, counts):
    widths = [width // LANES for width in WIDTHS]
    return call(
        functools.partial(last_kernel, widths),
        f32(XC, 16, LANES),
        in_specs=[SMEM] + [VMEM] * 9,
        out_specs=VMEM,
        scratch_shapes=[
            pltpu.VMEM(received.shape[1:], jnp.float32),
            pltpu.VMEM((widths[3], 8, LANES), jnp.float32),
            pltpu.VMEM((2, 8, coupling.shape[1]), jnp.float32),
        ],
    )(counts, received, *known, coupling, index, *chosen)


def finish_kernel(received, values, out0, out1, out2, out3, handed):
    z, core = position("z"), position("c")
    offsets = (core * 64 + z * 8, core * 64 + z * 8, z * 16, z * 16, (lax.rem(position("x"), 2) * 2 + core) * values.shape[1])
    for level, ref in enumerate((out0, out1, out2, out3, handed)):
        value = jnp.concatenate([received[source, 2 * level : 2 * level + 2, :] for source in range(XC)], axis=0)
        moved = pltpu.roll(value, lax.rem(LANES - offsets[level], LANES), 1)
        if level < 2:
            ref[...] = jnp.transpose(moved)[: ref.shape[0], :]
        elif level < 4:
            ref[...] = moved[:, : ref.shape[1]]
        else:
            ref[...] = values[...] - moved[:, : ref.shape[1]]


def finish(received, values, widths):
    samples = XC * PAIR
    shapes = [f32(width, samples) for width in widths[:2]] + [f32(samples, width) for width in widths[2:]]
    outs = call(finish_kernel, (*shapes, f32(*values.shape)), in_specs=[VMEM, VMEM])(received, values)
    return outs[0].T, outs[1].T, *outs[2:]


def body(
    rhs_root,
    rhs_level1,
    rhs_level2,
    rhs_level3,
    inv_root,
    inv_level1,
    inv_level2,
    inv_level3,
    cross_level1,
    cross_level2,
    cross_level3,
    subtree_values,
    coupling,
    coupled_rows,
):
    depth = lax.axis_size("z")
    counts = [width // LANES for width in WIDTHS]

    rhs_parts = [rhs_root, rhs_level1, rhs_level2, rhs_level3]
    product, ahead = own_product(subtree_values, coupling, rhs_parts, coupled_rows)
    both = lax.all_gather(product, "c", axis=0, tiled=False)

    def gathered(whole):
        return lax.all_gather(whole, ("x", "c"), axis=0, tiled=True)

    groups = ((inv_level3, cross_level3), (inv_level2, cross_level2), (inv_level1, cross_level1, inv_root))
    send, terms, (own3, pack2, pack1) = first(both, coupled_rows, ahead, depth, groups)
    matrix2 = gathered(pack2)
    path = upper_path(both, terms, coupled_rows, ahead, depth)
    received, other3, path, pack1 = lax.optimization_barrier(
        (exchange(send, ("x", "z")), lax.ppermute(own3, "c", [(0, 1), (1, 0)]), path, pack1)
    )
    matrix1 = gathered(pack1)
    target3 = exchange(sum_and_copy(received, depth), ("z",))
    send = lowest(target3, own3, other3, path, counts[3], sum(counts[:3]), 2 * depth)
    send, own3, coupling = lax.optimization_barrier((send, own3, coupling))
    matrix3 = gathered(own3)
    all_coupling = gathered(coupling)
    received = sum_and_copy(exchange(send, ("y0", "x", "z")), 2 * depth)
    target2, half2 = lax.optimization_barrier((exchange(received, ("y0", "z")), fetched(matrix2, 0.5)))
    solved2, send, rest = forward(
        target2, (half2, matrix2), received[0], counts[2], counts[0] + counts[1], counts[0], 4 * depth, 6
    )
    received, matrix1 = lax.optimization_barrier((exchange(send, ("y1", "y0", "z")), fetched(matrix1)))
    solved1, send, rest = forward(received, (matrix1,), rest, counts[1], counts[0], 0, Y, 0)

    def sum_root(copies):
        received = exchange(copies.reshape(Y * depth, -1, LANES), ALL_Y + ("z",))
        return exchange(sum_and_copy(received, depth), ("z",))

    target = sum_root(send).reshape(-1, LANES)
    received = sum_root(root(target, matrix1, WIDTHS[1] + WIDTHS[0], Y)).reshape(1, -1, LANES)
    send, x0 = backward(received, (matrix1,), solved1, [], counts[1], 4 * depth)
    x0, matrix2 = lax.optimization_barrier((x0, matrix2))
    received, chosen0, half2 = lax.optimization_barrier(
        (exchange(send, ("y1", "y0", "z")), picked(x0, coupled_rows, ahead, 0), fetched(matrix2, 0.5))
    )
    send, x1 = backward(received, (half2, matrix2), solved2, [x0], counts[2], 2 * depth)
    received, chosen1, half3 = lax.optimization_barrier(
        (exchange(send, ("y0", "z")), picked(x1, coupled_rows, ahead, counts[0]), fetched(matrix3, 0.5))
    )
    send, x2 = backward(received, (half3, matrix3), target3, [x0, x1], counts[3], depth)
    received, chosen2, all_coupling = lax.optimization_barrier(
        (exchange(send, ("z",)), picked(x2, coupled_rows, ahead, counts[0] + counts[1]), fetched(all_coupling))
    )
    send = last(received, [x0, x1, x2], [chosen0, chosen1, chosen2], all_coupling, coupled_rows, ahead)
    received = exchange(send, ("c", "x"))
    return finish(received, subtree_values, [part.shape[1] for part in rhs_parts])


def solution(mesh):
    shape = (2, 2, 2, X, C, mesh.shape["sep"])
    fine = Mesh(mesh.devices.reshape(shape), ("y2", "y1", "y0", "x", "c", "z"))
    every = ("y2", "y1", "y0", "x", "c", "z")
    columns, rows = P(None, every), P(every, None)
    in_specs = (columns,) * 4 + (rows,) * 7 + (columns, rows, P())
    return jax.shard_map(body, mesh=fine, in_specs=in_specs, out_specs=(columns,) * 5, check_vma=False)
```

```python
import functools

import jax
import jax.numpy as jnp
from jax import lax
from jax.experimental import pallas as pl
from jax.experimental.pallas import tpu as pltpu
from jax.sharding import Mesh, PartitionSpec as P

ROOT_ROWS = 4096
LEVEL1_ROWS = 2048
LEVEL2_ROWS = 2048
LEVEL3_ROWS = 1024
WIDTHS = (ROOT_ROWS, LEVEL1_ROWS, LEVEL2_ROWS, LEVEL3_ROWS)
Y, X, C = 8, 4, 2
XC = X * C
PAIR = 2
LANES = 128
CHUNK = 32
HBM = pl.BlockSpec(memory_space=pltpu.HBM)
LIMIT = 16 * 2**20
STREAM = 50 * 2**20
WHOLE = 57 * 2**20
ALL_Y = ("y2", "y1", "y0")
INTERPRET = False
VMEM = pl.BlockSpec(memory_space=pltpu.VMEM)
SMEM = pl.BlockSpec(memory_space=pltpu.SMEM)


def call(kernel, out_shape, **options):
    limit = options.pop("limit", LIMIT)
    return pl.pallas_call(
        kernel,
        out_shape=out_shape,
        compiler_params=pltpu.CompilerParams(vmem_limit_bytes=limit),
        interpret=INTERPRET,
        **options,
    )


def cost(elements):
    return pl.CostEstimate(flops=8 * elements, bytes_accessed=4 * elements, transcendentals=0)


def position(name):
    if name == "y":
        return (lax.axis_index("y2") * 2 + lax.axis_index("y1")) * 2 + lax.axis_index("y0")
    if name == "y1":
        return lax.axis_index("y1") * 2 + lax.axis_index("y0")
    return lax.axis_index(name)


def own_subtree():
    return position("y") * 2 + position("x") // 2


def window(counts, half, block, columns):
    return pl.multiple_of(jnp.minimum(counts[half, block] // LANES, columns // LANES - 2) * LANES, LANES)


def f32(*shape):
    return jax.ShapeDtypeStruct(shape, jnp.float32)


def exchange(operand, axes):
    flat = operand.reshape(-1, LANES)
    return lax.all_to_all(flat, axes, 0, 0, tiled=True).reshape(operand.shape)


def split3(value):
    high = value.astype(jnp.bfloat16)
    rest = value - high.astype(jnp.float32)
    middle = rest.astype(jnp.bfloat16)
    low = (rest - middle.astype(jnp.float32)).astype(jnp.bfloat16)
    return high, middle, low


def one_hot(index_row, block):
    shape = (LANES, index_row.shape[1])
    rows = lax.broadcasted_iota(jnp.int32, shape, 0) + block * LANES
    return jnp.where(rows == index_row, 1.0, 0.0).astype(jnp.bfloat16)


NT = (((1,), (1,)), ((), ()))
NN = (((1,), (0,)), ((), ()))


def row_dot(matrix, rows, column, vector, first, blocks):
    sums = [[None, None] for _ in range(PAIR)]
    for block in range(blocks):
        tile = matrix[rows, column + block * LANES : column + (block + 1) * LANES]
        for s in range(PAIR):
            at = (first + block) * PAIR + s
            part, old = tile * vector[at : at + 1, :], sums[s][block % 2]
            sums[s][block % 2] = part if old is None else old + part
    return [jnp.sum(value[0] + value[1], axis=1, keepdims=True) for value in sums]


def column_dot(matrix, rows, column, blocks, factors, total):
    wide = [jnp.broadcast_to(value, (CHUNK, LANES)) for value in factors]
    for block in range(blocks):
        tile = matrix[rows, column + block * LANES : column + (block + 1) * LANES]
        for s in range(PAIR):
            part = jnp.sum((tile * wide[s]).reshape(CHUNK // 8, 8, LANES), axis=0)
            at = block * PAIR + s
            total[at] = total[at] + part


def chunk_copies(matrix, buffer, ready):
    copies = []
    for place in range(matrix.shape[0] // 8):
        rows, columns = pl.ds(place * 8, 8), pl.ds(0, buffer.shape[1])
        copies.append(pltpu.make_async_copy(matrix.at[rows, columns], buffer.at[rows, columns], ready.at[place]))
    return copies


def begin(matrices, stream):
    if not stream:
        return matrices, None
    buffer, ready = stream
    copies = chunk_copies(matrices[-1].at[pl.ds(matrices[-1].shape[0] - buffer.shape[0], buffer.shape[0]), :], buffer, ready)
    for copy in copies:
        copy.start()
    return (*matrices[:-1], buffer), copies


def each_chunk(matrices, copies, step):
    share = CHUNK // 8
    base = 0
    for matrix in matrices:
        streamed = copies and matrix is matrices[-1]
        for chunk in range(matrix.shape[0] // CHUNK):
            if streamed:
                for copy in copies[chunk * share : (chunk + 1) * share]:
                    copy.wait()
            step(matrix, pl.ds(chunk * CHUNK, CHUNK), pl.ds(base + chunk * CHUNK, CHUNK))
        base += matrix.shape[0]


def stream_buffers(matrices, width):
    if len(matrices) == 1:
        return []
    rows = matrices[1].shape[0] - matrices[0].shape[0]
    return [pltpu.VMEM((rows, width), jnp.float32), pltpu.SemaphoreType.DMA((rows // 8,))]


def fetch_kernel(matrix, out, ready):
    copies = chunk_copies(matrix.at[pl.ds(0, out.shape[0]), :], out, ready)
    for copy in copies:
        copy.start()
    for copy in copies:
        copy.wait()


def fetched(matrix, part=1.0):
    rows, width = int(matrix.shape[0] * part), matrix.shape[1]
    return call(
        fetch_kernel,
        f32(rows, width),
        in_specs=[HBM],
        out_specs=VMEM,
        scratch_shapes=[pltpu.SemaphoreType.DMA((rows // 8,))],
        cost_estimate=cost(2 * rows * width),
    )(matrix)


def forward_kernel(blocks, upper, keep, extra, count, received, rest_in, *refs):
    matrices, (solved, send, rest, vector, total, *stream) = refs[:count], refs[count:]
    matrices, copies = begin(matrices, stream)
    if extra:
        for source in range(blocks):
            vector[2 * source : 2 * source + 2, :] = received[source, 0:2, :]
    else:
        vector[...] = jnp.sum(received[...], axis=0)
    total[...] = jnp.zeros_like(total)

    def step(matrix, rows, place):
        values = row_dot(matrix, rows, 0, vector, 0, blocks)
        for s in range(PAIR):
            solved[s, place, :] = jnp.broadcast_to(values[s], (CHUNK, LANES))
        column_dot(matrix, rows, blocks * LANES, upper, values, total)

    each_chunk(matrices, copies, step)
    whole = -jnp.sum(total[...], axis=1)
    if extra:
        rest[...] = whole
        place = position("y0") * (blocks // 2) + position("z")
        for row in range(extra):
            at = pl.ds(place * extra + row, 1)
            rest[at, :] = rest[at, :] + rest_in[2 + row : 3 + row, :]
        whole = rest[...]
    else:
        whole = whole + rest_in[0 : 2 * upper, :]
        rest[...] = whole
    for copy in range(send.shape[0]):
        send[copy] = whole[2 * keep :, :]


def forward(received, matrices, rest_in, blocks, upper, keep, copies, extra):
    rows = matrices[-1].shape[0]
    streamed = len(matrices) > 1
    width = upper * LANES + blocks * LANES
    return call(
        functools.partial(forward_kernel, blocks, upper, keep, extra, len(matrices)),
        (f32(PAIR, rows, LANES), f32(copies, 2 * (upper - keep), LANES), f32(2 * upper, LANES)),
        in_specs=[VMEM, VMEM] + ([VMEM, HBM] if streamed else [VMEM]),
        out_specs=(VMEM,) * 3,
        scratch_shapes=[pltpu.VMEM((2 * blocks, LANES), jnp.float32), pltpu.VMEM((2 * upper, 8, LANES), jnp.float32)]
        + stream_buffers(matrices, width),
        limit=STREAM if streamed else LIMIT,
        cost_estimate=cost(rows * width),
    )(received, rest_in, *matrices)


def lowest_kernel(blocks, upper, received, own, other, path, send, total, buffer, ready):
    rows = own.shape[0]
    copies = chunk_copies(own, buffer.at[0:rows, :], ready.at[0]) + chunk_copies(other, buffer.at[rows:, :], ready.at[1])
    for copy in copies:
        copy.start()
    for copy in copies:
        copy.wait()
    samples = range(received.shape[1])
    sums = [jnp.zeros((2 * rows, LANES), jnp.float32) for _ in samples]
    for block in range(blocks):
        tile = buffer[:, block * LANES : (block + 1) * LANES]
        for s in samples:
            sums[s] = sums[s] + tile * received[block, s : s + 1, :]
    wide = [jnp.broadcast_to(jnp.sum(value, axis=1, keepdims=True), (2 * rows, LANES)) for value in sums]
    for s in samples:
        total[s] = wide[s]

    def one(block, carry):
        at = pl.multiple_of((blocks + block) * LANES, LANES)
        tile = buffer[:, pl.ds(at, LANES)]
        parts = [jnp.sum(tile * total[s], axis=0, keepdims=True) for s in samples]
        path_block = path[block] - jnp.concatenate(parts, axis=0)
        send_block(block, path_block)
        return carry

    groups = send.shape[0] // X
    share = (upper - groups) // groups

    def send_block(block, value):
        low = block >= upper - groups
        place = jnp.where(low, block - (upper - groups), block // share)
        row = jnp.where(low, 0, 2 + 2 * lax.rem(block, share))
        depth = groups // 2
        for x in range(X):
            dest = (place // depth) * (X * depth) + x * depth + lax.rem(place, depth)
            send[dest, pl.ds(row, 2), :] = value[2 * x : 2 * x + 2, :]

    lax.fori_loop(0, upper, one, 0, unroll=4)


def lowest(received, own, other, path, blocks, upper, groups):
    rows, width = own.shape
    return call(
        functools.partial(lowest_kernel, blocks, upper),
        f32(X * groups, 8, LANES),
        in_specs=[VMEM, HBM, HBM, VMEM],
        out_specs=VMEM,
        scratch_shapes=[
            pltpu.VMEM((received.shape[1], 2 * rows, LANES), jnp.float32),
            pltpu.VMEM((2 * rows, width), jnp.float32),
            pltpu.SemaphoreType.DMA((2, rows // 8)),
        ],
        cost_estimate=cost(2 * rows * width),
    )(received, own, other, path)


def backward_kernel(blocks, known_blocks, number, received, solved, *refs):
    matrices, refs = refs[:number], refs[number:]
    known, (send, newest, total, vector, *stream) = refs[: len(known_blocks) - 1], refs[len(known_blocks) - 1 :]
    matrices, copies = begin(matrices, stream)
    newest[...] = jnp.sum(received[...], axis=0)
    total[...] = jnp.zeros_like(total)
    again = solved.shape[2] == LANES and solved.shape[0] == blocks
    if again:
        for block in range(blocks):
            vector[2 * block : 2 * block + 2, :] = solved[block, pl.ds(position("x") * 2, 2), :]

    def step(matrix, rows, place):
        if again:
            values = row_dot(matrix, rows, 0, vector, 0, blocks)
        else:
            values = [solved[s, place, 0:1] for s in range(PAIR)]
        column = blocks * LANES
        for ref, count in zip((*known, newest), known_blocks):
            part = row_dot(matrix, rows, column, ref, 0, count)
            values = [values[s] - part[s] for s in range(PAIR)]
            column += count * LANES
        column_dot(matrix, rows, 0, blocks, values, total)

    each_chunk(matrices, copies, step)
    whole = jnp.sum(total[...], axis=1)
    for copy in range(send.shape[0]):
        send[copy] = whole


def backward(received, matrices, solved, known, blocks, copies):
    rows = matrices[-1].shape[0]
    streamed = len(matrices) > 1
    counts = [array.shape[0] // PAIR for array in known] + [received.shape[1] // PAIR]
    width = (blocks + sum(counts)) * LANES
    return call(
        functools.partial(backward_kernel, blocks, counts, len(matrices)),
        (f32(copies, 2 * blocks, LANES), f32(*received.shape[1:])),
        in_specs=[VMEM, VMEM] + ([VMEM, HBM] if streamed else [VMEM]) + [VMEM] * len(known),
        out_specs=(VMEM,) * 2,
        scratch_shapes=[pltpu.VMEM((2 * blocks, 8, LANES), jnp.float32), pltpu.VMEM((2 * blocks, LANES), jnp.float32)]
        + stream_buffers(matrices, width),
        limit=STREAM if streamed else LIMIT,
        cost_estimate=cost(rows * width),
    )(received, solved, *matrices, *known)


def root_kernel(column, blocks, vector, matrix, send, total):
    total[...] = jnp.zeros_like(total)

    def step(rows):
        values = row_dot(matrix, rows, column, vector, 0, blocks)
        column_dot(matrix, rows, column, blocks, values, total)

    for chunk in range(matrix.shape[0] // CHUNK):
        step(pl.ds(chunk * CHUNK, CHUNK))
    whole = jnp.sum(total[...], axis=1)
    for copy in range(send.shape[0]):
        send[copy] = whole


def root(vector, matrix, column, copies):
    rows = matrix.shape[0]
    blocks = vector.shape[0] // PAIR
    return call(
        functools.partial(root_kernel, column, blocks),
        f32(copies, 2 * blocks, LANES),
        in_specs=[VMEM, VMEM],
        out_specs=VMEM,
        scratch_shapes=[pltpu.VMEM((2 * blocks, 8, LANES), jnp.float32)],
        cost_estimate=cost(rows * blocks * LANES),
    )(vector, matrix)


def sum_kernel(copies, received, send):
    whole = jnp.sum(received[...], axis=0)
    for copy in range(copies):
        send[copy] = whole


def sum_and_copy(received, copies):
    return call(functools.partial(sum_kernel, copies), f32(copies, *received.shape[1:]))(received)


def expand(counts, terms, index, first_block, path):
    subtree = own_subtree()

    def one(block, carry):
        at = window(counts, position("x") // 2, first_block + block, index.shape[1])
        selector = one_hot(index[pl.ds(subtree, 1), pl.ds(at, 2 * LANES)], first_block + block)
        out = lax.dot_general(terms[:, pl.ds(at, 2 * LANES)], selector, NT, preferred_element_type=jnp.float32)
        path[block] = -(out[0:8] + out[8:16] + out[16:24])
        return carry

    lax.fori_loop(0, path.shape[0], one, 0, unroll=4)


def add_own(both, depth, heights, path):
    z, core, x = position("z"), position("c"), position("x")
    half = pl.multiple_of(core * 8, 8)
    lane = lax.broadcasted_iota(jnp.int32, (8, LANES), 1)
    start = source = 0
    for height in range(4):
        width = 8 if height < 2 else 16
        for other in range(C):
            if height not in heights:
                continue
            offset = z * width
            block = start
            if height < 3:
                block = block + position(("y", "y1", "y0")[height]) * (XC * depth * width // LANES)
            if width == 8:
                offset = offset + other * 64
                block = block + x
            else:
                block = block + x * 2 + other
            small = both[other, pl.ds(half, 8), both.shape[2] - LANES :]
            moved = pltpu.roll(small, lax.rem(offset - source + LANES, LANES), 1)
            path[block] = path[block] + jnp.where((lane >= offset) & (lane < offset + width), moved, 0.0)
        start += WIDTHS[height] // LANES if height in heights else 0
        source += width


def stage_in(parts, stages, groups, ready):
    copies = []
    for stage, size in zip(stages, groups):
        column = 0
        for part in parts[:size]:
            width = part.shape[1]
            for row in range(0, part.shape[0], 8):
                rows = pl.ds(row, 8)
                copies.append(
                    pltpu.make_async_copy(part.at[rows, :], stage.at[rows, pl.ds(column, width)], ready.at[len(copies)])
                )
            column += width
        parts = parts[size:]
    for copy in copies:
        copy.start()
    return copies


def stage_out(copies, stages, packs, done):
    for copy in copies:
        copy.wait()
    copies = []
    for stage, pack in zip(stages, packs):
        for row in range(0, pack.shape[0], 8):
            rows = pl.ds(row, 8)
            copies.append(pltpu.make_async_copy(stage.at[rows, :], pack.at[rows, :], done.at[len(copies)]))
    for copy in copies:
        copy.start()
    return copies


def pack_shapes(groups):
    parts = [part for group in groups for part in group]
    packs = [f32(group[0].shape[0], sum(part.shape[1] for part in group)) for group in groups]
    scratch = [
        pltpu.SemaphoreType.DMA((sum(part.shape[0] // 8 for part in parts),)),
        pltpu.SemaphoreType.DMA((sum(pack.shape[0] // 8 for pack in packs),)),
    ]
    return parts, packs, scratch + [pltpu.VMEM(pack.shape, jnp.float32) for pack in packs]


def product_kernel(groups, values, coupling, rhs0, rhs1, rhs2, rhs3, index, *refs):
    count, number = sum(groups), len(groups)
    parts, (out, ahead, *packs), (ready, done, *stages) = refs[:count], refs[count : -2 - number], refs[-2 - number :]
    copies = stage_in(parts, stages, groups, ready)
    columns = coupling.shape[1]
    out[:, :columns] = lax.dot_general(
        values[...], coupling[...], NN, precision=lax.Precision.HIGHEST, preferred_element_type=jnp.float32
    )
    copies = stage_out(copies, stages, packs, done)
    sides = [jnp.transpose(rhs0[...]), jnp.transpose(rhs1[...]), rhs2[...], rhs3[...]]
    filled = sum(side.shape[1] for side in sides)
    sides.append(jnp.zeros((out.shape[0], LANES - filled), jnp.float32))
    out[:, columns:] = jnp.concatenate(sides, axis=1)
    edges = lax.broadcasted_iota(jnp.int32, (LANES, 2 * LANES), 0) * LANES
    for half in range(2):
        def compare(block, total):
            at = pl.multiple_of(block * 2 * LANES, LANES)
            row = index[pl.ds(position("y") * 2 + half, 1), pl.ds(at, 2 * LANES)]
            return total + jnp.where(row < edges, 1.0, 0.0)

        total = lax.fori_loop(0, columns // (2 * LANES), compare, jnp.zeros((LANES, 2 * LANES), jnp.float32), unroll=2)
        total = jnp.broadcast_to(jnp.sum(total, axis=1, keepdims=True), (LANES, LANES))
        ahead[half : half + 1, :] = jnp.transpose(total)[0:1, :].astype(jnp.int32)
    for copy in copies:
        copy.wait()


def own_product(values, coupling, rhs_parts, index, groups):
    rhs0, rhs1, rhs2, rhs3 = rhs_parts
    parts, packs, scratch = pack_shapes(groups)
    shapes = (f32(values.shape[0], coupling.shape[1] + LANES), jax.ShapeDtypeStruct((2, LANES), jnp.int32))
    outs = call(
        functools.partial(product_kernel, [len(group) for group in groups]),
        (*shapes, *packs),
        in_specs=[VMEM] * 7 + [HBM] * len(parts),
        out_specs=(VMEM, VMEM) + (HBM,) * len(packs),
        scratch_shapes=scratch,
        limit=WHOLE,
    )(values, coupling, rhs0.T, rhs1.T, rhs2, rhs3, index, *parts)
    return outs[0], outs[1], outs[2:]


def first_kernel(depth, counts, both, index, send, terms, path):
    columns = both.shape[2] - LANES
    half = pl.multiple_of(position("c") * 8, 8)
    pieces = split3(both[0, pl.ds(half, 8), :columns] + both[1, pl.ds(half, 8), :columns])
    terms[...] = jnp.concatenate([*pieces, jnp.zeros_like(pieces[0])], axis=0)
    expand(counts, terms, index, sum(WIDTHS[:3]) // LANES, path)
    add_own(both, depth, (3,), path)
    for dest in range(X):
        for other in range(depth):
            send[dest * depth + other] = path[other]


def first(both, index, counts, depth):
    columns = both.shape[2] - LANES
    return call(
        functools.partial(first_kernel, depth),
        (f32(X * depth, 8, LANES), jax.ShapeDtypeStruct((32, columns), jnp.bfloat16)),
        in_specs=[SMEM, VMEM, VMEM],
        out_specs=(VMEM, VMEM),
        scratch_shapes=[pltpu.VMEM((WIDTHS[3] // LANES, 8, LANES), jnp.float32)],
    )(counts, both, index)


def upper_kernel(depth, counts, both, terms, index, path):
    expand(counts, terms, index, 0, path)
    add_own(both, depth, (0, 1, 2), path)


def upper_path(both, terms, index, counts, depth):
    blocks = sum(WIDTHS[:3]) // LANES
    return call(
        functools.partial(upper_kernel, depth),
        f32(blocks, 8, LANES),
        in_specs=[SMEM, VMEM, VMEM, VMEM],
        out_specs=VMEM,
        cost_estimate=cost(blocks * LANES * LANES),
    )(counts, both, terms, index)


def pick(counts, index, terms, first_block, blocks, chosen):
    def one(block, carry):
        for half in range(2):
            at = window(counts, half, first_block + block, index.shape[1])
            selector = one_hot(index[pl.ds(position("y") * 2 + half, 1), pl.ds(at, 2 * LANES)], first_block + block)
            out = lax.dot_general(
                terms[block].astype(jnp.bfloat16), selector, NN, preferred_element_type=jnp.float32
            )
            chosen[half, :, pl.ds(at, 2 * LANES)] = chosen[half, :, pl.ds(at, 2 * LANES)] + out
        return carry

    lax.fori_loop(0, blocks, one, 0, unroll=4)


def store_terms(ref, terms):
    blocks = ref.shape[0] // PAIR
    pieces = split3(ref[...].reshape(blocks, PAIR, LANES))
    terms[...] = jnp.concatenate([*pieces, jnp.zeros_like(pieces[0])], axis=1).astype(jnp.float32)


def pick_kernel(first_block, counts, x, index, chosen, terms):
    store_terms(x, terms)
    chosen[...] = jnp.zeros_like(chosen)
    pick(counts, index, terms, first_block, x.shape[0] // PAIR, chosen)


def picked(x, index, counts, first_block):
    blocks = x.shape[0] // PAIR
    return call(
        functools.partial(pick_kernel, first_block),
        f32(2, 8, index.shape[1]),
        in_specs=[SMEM, VMEM, VMEM],
        out_specs=VMEM,
        scratch_shapes=[pltpu.VMEM((blocks, 8, LANES), jnp.float32)],
        cost_estimate=cost(blocks * 2 * LANES * LANES),
    )(counts, x, index)


def last_kernel(widths, counts, received, x0, x1, x2, coupling, index, chosen0, chosen1, chosen2, send, x3, terms, chosen):
    x3[...] = jnp.sum(received[...], axis=0)
    store_terms(x3, terms)
    chosen[...] = chosen0[...] + chosen1[...] + chosen2[...]
    pick(counts, index, terms, sum(widths[:3]), widths[3], chosen)
    rows, columns = coupling.shape[0] // 2, coupling.shape[1]
    lane = lax.broadcasted_iota(jnp.int32, (CHUNK, LANES), 1)
    handed = []
    for half in range(2):
        chosen[half, 0:2, :] = chosen[half, 0:2, :] + chosen[half, 2:4, :] + chosen[half, 4:6, :]
        columns_of = []
        for chunk in range(rows // CHUNK):
            at = half * rows + chunk * CHUNK
            sums = [[None, None] for _ in range(PAIR)]
            for block in range(columns // LANES):
                place = slice(block * LANES, (block + 1) * LANES)
                tile = coupling[at : at + CHUNK, place]
                for s in range(PAIR):
                    part, old = tile * chosen[half, s : s + 1, place], sums[s][block % 2]
                    sums[s][block % 2] = part if old is None else old + part
            totals = [jnp.sum(value[0] + value[1], axis=1, keepdims=True) for value in sums]
            columns_of.append(jnp.where(lane == 0, totals[0], jnp.where(lane == 1, totals[1], 0.0)))
        handed.append(jnp.transpose(jnp.concatenate(columns_of, axis=0))[0:PAIR, :])
    send[...] = jnp.zeros_like(send)
    for dest in range(XC):
        core, x = dest // X, dest % X
        for level, ref in enumerate((x0, x1, x2, x3)):
            block = x if level < 2 else x * 2 + core
            if level < 3:
                block = block + position(("y", "y1", "y0")[level]) * (widths[level] // (Y // 2**level))
            send[dest, 2 * level : 2 * level + 2, :] = ref[pl.ds(block * 2, 2), :]
        send[dest, 8:10, :] = handed[x // 2]


def last(received, known, chosen, coupling, index, counts):
    widths = [width // LANES for width in WIDTHS]
    return call(
        functools.partial(last_kernel, widths),
        f32(XC, 16, LANES),
        in_specs=[SMEM] + [VMEM] * 9,
        out_specs=VMEM,
        scratch_shapes=[
            pltpu.VMEM(received.shape[1:], jnp.float32),
            pltpu.VMEM((widths[3], 8, LANES), jnp.float32),
            pltpu.VMEM((2, 8, coupling.shape[1]), jnp.float32),
        ],
    )(counts, received, *known, coupling, index, *chosen)


def finish_kernel(received, values, out0, out1, out2, out3, handed):
    z, core = position("z"), position("c")
    offsets = (core * 64 + z * 8, core * 64 + z * 8, z * 16, z * 16, (lax.rem(position("x"), 2) * 2 + core) * values.shape[1])
    for level, ref in enumerate((out0, out1, out2, out3, handed)):
        value = jnp.concatenate([received[source, 2 * level : 2 * level + 2, :] for source in range(XC)], axis=0)
        moved = pltpu.roll(value, lax.rem(LANES - offsets[level], LANES), 1)
        if level < 2:
            ref[...] = jnp.transpose(moved)[: ref.shape[0], :]
        elif level < 4:
            ref[...] = moved[:, : ref.shape[1]]
        else:
            ref[...] = values[...] - moved[:, : ref.shape[1]]


def finish(received, values, widths):
    samples = XC * PAIR
    shapes = [f32(width, samples) for width in widths[:2]] + [f32(samples, width) for width in widths[2:]]
    outs = call(finish_kernel, (*shapes, f32(*values.shape)), in_specs=[VMEM, VMEM])(received, values)
    return outs[0].T, outs[1].T, *outs[2:]


def body(
    rhs_root,
    rhs_level1,
    rhs_level2,
    rhs_level3,
    inv_root,
    inv_level1,
    inv_level2,
    inv_level3,
    cross_level1,
    cross_level2,
    cross_level3,
    subtree_values,
    coupling,
    coupled_rows,
):
    depth = lax.axis_size("z")
    counts = [width // LANES for width in WIDTHS]

    rhs_parts = [rhs_root, rhs_level1, rhs_level2, rhs_level3]
    groups = ((inv_level3, cross_level3), (inv_level2, cross_level2), (inv_level1, cross_level1, inv_root))
    product, ahead, (own3, pack2, pack1) = own_product(subtree_values, coupling, rhs_parts, coupled_rows, groups)
    both = lax.all_gather(product, "c", axis=0, tiled=False)

    def gathered(whole):
        return lax.all_gather(whole, ("x", "c"), axis=0, tiled=True)

    send, terms = first(both, coupled_rows, ahead, depth)
    matrix2 = gathered(pack2)
    path = upper_path(both, terms, coupled_rows, ahead, depth)
    received, other3, path, pack1 = lax.optimization_barrier(
        (exchange(send, ("x", "z")), lax.ppermute(own3, "c", [(0, 1), (1, 0)]), path, pack1)
    )
    matrix1 = gathered(pack1)
    target3 = exchange(sum_and_copy(received, depth), ("z",))
    send = lowest(target3, own3, other3, path, counts[3], sum(counts[:3]), 2 * depth)
    send, own3, coupling = lax.optimization_barrier((send, own3, coupling))
    matrix3 = gathered(own3)
    all_coupling = gathered(coupling)
    received = sum_and_copy(exchange(send, ("y0", "x", "z")), 2 * depth)
    target2, half2 = lax.optimization_barrier((exchange(received, ("y0", "z")), fetched(matrix2, 0.5)))
    solved2, send, rest = forward(
        target2, (half2, matrix2), received[0], counts[2], counts[0] + counts[1], counts[0], 4 * depth, 6
    )
    received, matrix1 = lax.optimization_barrier((exchange(send, ("y1", "y0", "z")), fetched(matrix1)))
    solved1, send, rest = forward(received, (matrix1,), rest, counts[1], counts[0], 0, Y, 0)

    def sum_root(copies):
        received = exchange(copies.reshape(Y * depth, -1, LANES), ALL_Y + ("z",))
        return exchange(sum_and_copy(received, depth), ("z",))

    target = sum_root(send).reshape(-1, LANES)
    received = sum_root(root(target, matrix1, WIDTHS[1] + WIDTHS[0], Y)).reshape(1, -1, LANES)
    send, x0 = backward(received, (matrix1,), solved1, [], counts[1], 4 * depth)
    x0, matrix2 = lax.optimization_barrier((x0, matrix2))
    received, chosen0, half2 = lax.optimization_barrier(
        (exchange(send, ("y1", "y0", "z")), picked(x0, coupled_rows, ahead, 0), fetched(matrix2, 0.5))
    )
    send, x1 = backward(received, (half2, matrix2), solved2, [x0], counts[2], 2 * depth)
    received, chosen1, half3 = lax.optimization_barrier(
        (exchange(send, ("y0", "z")), picked(x1, coupled_rows, ahead, counts[0]), fetched(matrix3, 0.5))
    )
    send, x2 = backward(received, (half3, matrix3), target3, [x0, x1], counts[3], depth)
    received, chosen2, all_coupling = lax.optimization_barrier(
        (exchange(send, ("z",)), picked(x2, coupled_rows, ahead, counts[0] + counts[1]), fetched(all_coupling))
    )
    send = last(received, [x0, x1, x2], [chosen0, chosen1, chosen2], all_coupling, coupled_rows, ahead)
    received = exchange(send, ("c", "x"))
    return finish(received, subtree_values, [part.shape[1] for part in rhs_parts])


def solution(mesh):
    shape = (2, 2, 2, X, C, mesh.shape["sep"])
    fine = Mesh(mesh.devices.reshape(shape), ("y2", "y1", "y0", "x", "c", "z"))
    every = ("y2", "y1", "y0", "x", "c", "z")
    columns, rows = P(None, every), P(every, None)
    in_specs = (columns,) * 4 + (rows,) * 7 + (columns, rows, P())
    return jax.shard_map(body, mesh=fine, in_specs=in_specs, out_specs=(columns,) * 5, check_vma=False)
```
